32 devices in a mesh: blk: 32 (over z, y, x, core).
Axes of the slice: x: 2, y: 2, z: 4, core: 2. Of those that a mesh axis runs over, the one named last changes fastest.
Arguments:
- text_tokens: bfloat16 [8192, 768], P('blk'), may hold values from -6 to 6
- segment_ids: int32 [128, 64], P('blk'), may hold values from 0 to 3, never falling along the last dimension, each value on 1 to 28 neighbouring positions
- pair_index: int32 [512], P('blk'), may hold values from 0 to 511, each once
- image_tokens: bfloat16 [25600, 768], P('blk'), may hold values from -6 to 6
- logit_scale: float32 [1], replicated, may hold values from 30 to 90
- img_gains: bfloat16 [1536], P('blk'), may hold values from 0.5 to 1.5
- img_shifts: bfloat16 [1536], P('blk'), may hold values from -2 to 2
- img_qkv: bfloat16 [768, 2304], P('blk'), may hold values from -0.21875 to 0.21875
- img_out: bfloat16 [768, 768], P('blk'), may hold values from -1.25 to 1.25
- img_in: bfloat16 [768, 3072], P('blk'), may hold values from -0.21875 to 0.21875
- img_down: bfloat16 [3072, 768], P('blk'), may hold values from -0.15625 to 0.15625
- img_biases: bfloat16 [3840], P('blk'), may hold values from -2 to 2
- img_proj: bfloat16 [768, 768], P('blk'), may hold values from -0.21875 to 0.21875
- txt_gains: bfloat16 [1536], P('blk'), may hold values from 0.5 to 1.5
- txt_shifts: bfloat16 [1536], P('blk'), may hold values from -2 to 2
- txt_qkv: bfloat16 [768, 2304], P('blk'), may hold values from -0.21875 to 0.21875
- txt_out: bfloat16 [768, 768], P('blk'), may hold values from -0.875 to 0.875
- txt_in: bfloat16 [768, 3072], P('blk'), may hold values from -0.21875 to 0.21875
- txt_down: bfloat16 [3072, 768], P('blk'), may hold values from -0.15625 to 0.15625
- txt_biases: bfloat16 [3840], P('blk'), may hold values from -2 to 2
- txt_proj: bfloat16 [768, 768], P('blk'), may hold values from -0.21875 to 0.21875
Outputs:
- pair_loss: float32 [512], P('blk')
- text_out: bfloat16 [8192, 768], P('blk')
- text_grad: float32 [8192, 768], P('blk')
- grad_gains: float32 [1536], P('blk')
- grad_shifts: float32 [1536], P('blk')
- grad_qkv: float32 [768, 2304], P('blk')
- grad_out: float32 [768, 768], P('blk')
- grad_in: float32 [768, 3072], P('blk')
- grad_down: float32 [3072, 768], P('blk')
- grad_biases: float32 [3840], P('blk')
- grad_proj: float32 [768, 768], P('blk')
The draws below stay inside these ranges and needn't reach their ends.
Inputs may be any that keep to these rules, and one draw needn't show every extreme that they name: `segment_ids`: each row holds 4 captions in order, ids never falling, each caption 1 to 28 tokens. `pair_index`: each image belongs to exactly one caption.
All inputs are finite; a program needn't handle non-finite values.
Results may differ from the reference program's by a relative error of at most 0.018.
The reference program's roundings to bfloat16 on the way count: a program that leaves them out, or rounds other values in their place, can miss the bound.
Values may be sent and summed in bfloat16 or wider, within the bound.
No kernel may reach another device: no remote copies, remote signals or barrier semaphores. Data moves between devices by JAX's collectives and lax.ppermute only.
A program may use at most 192 MiB of HBM per device.

```python
import math
import jax
import jax.numpy as jnp
import numpy as np
from jax import lax

D = 768
FF = 3072
HEAD = 64
PATCHES = 50
SEQ = 64
CAPS = 4
PAIRS = 512
TEXT_ROWS = 128
TEXT_TOK = 8192
IMG_TOK = 25600


def block_levels(rng, dims, cuts, low, top_value):
    def one(dim, parts):
        draws = jax.random.uniform(jax.random.fold_in(jax.random.fold_in(rng, 6), dim), (parts,), jnp.float32, low / len(cuts), top_value / len(cuts))
        return jnp.repeat(jnp.exp(draws), dims[dim] // parts).reshape((-1,) + (1,) * (len(dims) - dim - 1))

    level = one(*cuts[0])
    for cut in cuts[1:]:
        level = level * one(*cut)
    return level


def length_profile(count, total, reach, lean):
    portions = [(1 << 20) // math.isqrt(standing ** lean) + 1 for standing in range(2, count + 1)]
    spare, counts = total - reach - (count - 1), [1] * (count - 1)
    while spare > 0:
        free = [i for i in range(count - 1) if counts[i] < reach]
        mass, remaining = sum([portions[i] for i in free]), spare
        for i in free:
            addition = min(reach - counts[i], max(1, remaining * portions[i] // mass), spare)
            counts[i] = counts[i] + addition
            spare = spare - addition
    return np.array([reach] + counts)


def uneven_parts(own_key, count, total, most, lean):
    if count == 2:
        one = jax.random.randint(own_key, (), max(1, total - most), min(most, total - 1) + 1)
        return jnp.stack([one, total - one])
    sizes = jnp.asarray(length_profile(count, total, most, lean), jnp.int32)
    couples = (count - 1) // 2
    donor, taker = sizes[1:1 + 2 * couples:2], sizes[2:2 + 2 * couples:2]
    room = jnp.minimum(donor - 1, most - taker)
    passed = jax.random.randint(jax.random.fold_in(own_key, 1), (couples,), 0, 1 << 20) % (room + 1)
    sizes = sizes.at[1:1 + 2 * couples:2].set(donor - passed).at[2:2 + 2 * couples:2].set(taker + passed)
    return sizes[jax.random.permutation(jax.random.fold_in(own_key, 2), count)]


def centred(own_key, extent, spread, most, split=(), held_as=jnp.bfloat16):
    gain = block_levels(own_key, extent, split, -0.22, 0.18) if split else 1.0
    drawn = jax.random.normal(own_key, extent, jnp.float32) * spread * gain
    return jnp.minimum(jnp.maximum(drawn, -most), most).astype(held_as)


def setup_inputs(seed: int = 0) -> dict:
    seeds = jax.random.split(jax.random.key(seed), 22)
    text_tokens = centred(seeds[0], (TEXT_TOK, D), 1.0, 6.0, ((0, 32),))
    segment_ids = jax.vmap(lambda own: jnp.searchsorted(jnp.cumsum(uneven_parts(own, CAPS, SEQ, min(28, SEQ - SEQ // 4), 2)), jnp.arange(SEQ), side="right"))(jax.random.split(seeds[1], TEXT_ROWS)).reshape((TEXT_ROWS, SEQ)).astype(jnp.int32)
    pair_index = jax.random.permutation(seeds[2], PAIRS).astype(jnp.int32)
    image_tokens = centred(seeds[3], (IMG_TOK, D), 1.0, 6.0, ((0, 32),))
    logit_scale = jnp.clip(jnp.exp(jax.random.uniform(seeds[4], (1,), jnp.float32, math.log(30.0), math.log(90.0))), 30.0, 90.0)
    img_gains = jnp.clip(1.0 + 0.1 * jax.random.normal(seeds[5], (2 * D,), jnp.float32), 0.5, 1.5).astype(jnp.bfloat16)
    img_shifts = centred(seeds[6], (2 * D,), 0.3, 2.0, ((0, 32),))
    img_qkv = centred(seeds[7], (D, 3 * D), D ** -0.5, 0.21875, ((0, 32),))
    img_out = centred(seeds[8], (D, D), (D // 32) ** -0.5, 1.25, ((0, 32),))
    img_in = centred(seeds[9], (D, FF), D ** -0.5, 0.21875, ((0, 32),))
    img_down = centred(seeds[10], (FF, D), (FF // 2) ** -0.5, 0.15625, ((0, 32),))
    img_biases = centred(seeds[11], (FF + D,), 0.3, 2.0, ((0, 32),))
    img_proj = centred(seeds[12], (D, D), D ** -0.5, 0.21875, ((0, 32),))
    txt_gains = jnp.clip(1.0 + 0.1 * jax.random.normal(seeds[13], (2 * D,), jnp.float32), 0.5, 1.5).astype(jnp.bfloat16)
    txt_shifts = centred(seeds[14], (2 * D,), 0.3, 2.0, ((0, 32),))
    txt_qkv = centred(seeds[15], (D, 3 * D), D ** -0.5, 0.21875, ((0, 32),))
    txt_out = centred(seeds[16], (D, D), (D // 16) ** -0.5, 0.875, ((0, 32),))
    txt_in = centred(seeds[17], (D, FF), D ** -0.5, 0.21875, ((0, 32),))
    txt_down = centred(seeds[18], (FF, D), (FF // 2) ** -0.5, 0.15625, ((0, 32),))
    txt_biases = centred(seeds[19], (FF + D,), 0.3, 2.0, ((0, 32),))
    txt_proj = centred(seeds[20], (D, D), D ** -0.5, 0.21875, ((0, 32),))
    return {"text_tokens": text_tokens, "segment_ids": segment_ids, "pair_index": pair_index, "image_tokens": image_tokens, "logit_scale": logit_scale, "img_gains": img_gains, "img_shifts": img_shifts, "img_qkv": img_qkv, "img_out": img_out, "img_in": img_in, "img_down": img_down, "img_biases": img_biases, "img_proj": img_proj, "txt_gains": txt_gains, "txt_shifts": txt_shifts, "txt_qkv": txt_qkv, "txt_out": txt_out, "txt_in": txt_in, "txt_down": txt_down, "txt_biases": txt_biases, "txt_proj": txt_proj}


HIGH = lax.Precision.HIGHEST

@jax.custom_vjp
def low(v):
    return lax.optimization_barrier(v.astype(jnp.bfloat16)).astype(jnp.float32)

@jax.custom_vjp
def low_back(v):
    return v

def low_keep(v):
    return (low(v), None)

def low_pass(kept, grad):
    return (grad,)

def back_keep(v):
    return (v, None)

def back_low(kept, grad):
    return (low(grad),)
low.defvjp(low_keep, low_pass)
low_back.defvjp(back_keep, back_low)

def gelu(z):
    return 0.5 * z * (1.0 + jnp.tanh(0.7978845608028654 * (z + 0.044715 * z * z * z)))

def layer_stats(x):
    mean = lax.optimization_barrier(jnp.mean(x, axis=-1, keepdims=True))
    cent = x - mean
    return cent * lax.rsqrt(lax.optimization_barrier(jnp.mean(cent * cent, axis=-1, keepdims=True)) + 1e-06)

def project(a, w):
    return jnp.einsum('gld,de->gle', a, w, precision=HIGH, preferred_element_type=jnp.float32)

def block(x, same, gains, shifts, w_qkv, w_out, w_in, w_down, biases):
    groups, length, width = x.shape
    units = w_in.shape[1]
    heads = width // HEAD
    act1 = low(layer_stats(x) * gains[:width] + shifts[:width])
    qkv = low(low_back(project(act1, w_qkv)))
    query = qkv[..., :width].reshape(groups, length, heads, HEAD)
    keys = qkv[..., width:2 * width].reshape(groups, length, heads, HEAD)
    values = qkv[..., 2 * width:].reshape(groups, length, heads, HEAD)
    scores = low_back(0.125 * jnp.einsum('gthd,gshd->ghts', query, keys, precision=HIGH))
    scores = jnp.where(same[:, None], scores, -1000000000.0)
    top = lax.optimization_barrier(jnp.max(scores, axis=-1, keepdims=True))
    expo = jnp.exp(scores - top)
    probs = low(expo / lax.optimization_barrier(jnp.sum(expo, axis=-1, keepdims=True)))
    mixed = jnp.einsum('ghts,gshd->gthd', probs, values, precision=HIGH)
    mixed = low(low_back(mixed)).reshape(groups, length, width)
    second = x + low_back(project(mixed, w_out))
    act2 = low(layer_stats(second) * gains[width:] + shifts[width:])
    inner = low_back(project(act2, w_in) + biases[:units])
    hidden = low(gelu(inner))
    return second + low_back(project(hidden, w_down)) + biases[units:]

def embed(pooled, w_proj):
    proj = low_back(jnp.dot(low(pooled), w_proj, precision=HIGH, preferred_element_type=jnp.float32))
    return low(proj * lax.rsqrt(lax.optimization_barrier(jnp.sum(proj * proj, axis=-1, keepdims=True)) + 1e-06))

def contrast(caption_emb, image_emb, pairs, scale):
    rows = math.gcd(PAIRS, 512)
    columns = jnp.arange(PAIRS, dtype=jnp.int32)

    def step(carry, item):
        col_max, col_sum = carry
        block_emb, block_pairs = item
        sim = low_back(scale * jnp.dot(block_emb, image_emb.T, precision=HIGH, preferred_element_type=jnp.float32))
        top = lax.optimization_barrier(jnp.max(sim, axis=1, keepdims=True))
        row_lse = top[:, 0] + jnp.log(lax.optimization_barrier(jnp.sum(jnp.exp(sim - top), axis=1)))
        pos = lax.optimization_barrier(jnp.sum(jnp.where(block_pairs[:, None] == columns[None, :], sim, 0.0), axis=1))
        new_max = jnp.maximum(col_max, lax.optimization_barrier(jnp.max(sim, axis=0)))
        col_sum = col_sum * jnp.exp(col_max - new_max) + lax.optimization_barrier(jnp.sum(jnp.exp(sim - new_max[None, :]), axis=0))
        return ((new_max, col_sum), (row_lse, pos))
    init = (jnp.full((PAIRS,), -1e+30, jnp.float32), jnp.zeros((PAIRS,), jnp.float32))
    items = (caption_emb.reshape(PAIRS // rows, rows, D), pairs.reshape(PAIRS // rows, rows))
    (col_max, col_sum), (row_lse, pos) = lax.scan(jax.checkpoint(step), init, items)
    col_lse = col_max + jnp.log(col_sum)
    row_lse = row_lse.reshape(PAIRS)
    pos = pos.reshape(PAIRS)
    return 0.5 * (row_lse - pos) + 0.5 * (col_lse[pairs] - pos)

def reference(text_tokens, segment_ids, pair_index, image_tokens, logit_scale, img_gains, img_shifts, img_qkv, img_out, img_in, img_down, img_biases, img_proj, txt_gains, txt_shifts, txt_qkv, txt_out, txt_in, txt_down, txt_biases, txt_proj):
    image_weights = [w.astype(jnp.float32) for w in (img_gains, img_shifts, img_qkv, img_out, img_in, img_down, img_biases, img_proj)]
    group = math.gcd(PAIRS, 64)
    images = image_tokens.astype(jnp.float32).reshape(PAIRS // group, group, PATCHES, D)
    every = jnp.ones((group, PATCHES, PATCHES), jnp.bool_)

    def image_group(x):
        y = block(x, every, *image_weights[:7])
        return embed(lax.optimization_barrier(jnp.mean(y, axis=1)), image_weights[7])
    image_emb = lax.map(image_group, images).reshape(PAIRS, D)
    scale = logit_scale[0].astype(jnp.float32)
    row_group = math.gcd(TEXT_ROWS, 64)
    segments = segment_ids.reshape(TEXT_ROWS // row_group, row_group, SEQ)
    caption_ids = jnp.arange(CAPS, dtype=jnp.int32)

    def forward(x, gains, shifts, w_qkv, w_out, w_in, w_down, biases, w_proj):
        rows = x.reshape(TEXT_ROWS // row_group, row_group, SEQ, D)

        def text_group(item):
            xg, sg = item
            same = sg[:, :, None] == sg[:, None, :]
            y = block(xg, same, gains, shifts, w_qkv, w_out, w_in, w_down, biases)
            member = (sg[:, None, :] == caption_ids[None, :, None]).astype(jnp.float32)
            member = member / lax.optimization_barrier(jnp.sum(member, axis=2, keepdims=True))
            pooled = jnp.einsum('gcl,gld->gcd', member, y, precision=HIGH)
            return (y, pooled)
        y, pooled = lax.map(jax.checkpoint(text_group), (rows, segments))
        caption_emb = embed(pooled.reshape(PAIRS, D), w_proj)
        losses = contrast(caption_emb, image_emb, pair_index, scale)
        return (jnp.sum(losses), (losses, y.reshape(TEXT_TOK, D)))
    inputs = [w.astype(jnp.float32) for w in (text_tokens, txt_gains, txt_shifts, txt_qkv, txt_out, txt_in, txt_down, txt_biases, txt_proj)]
    total, pullback, extra = jax.vjp(forward, *inputs, has_aux=True)
    grads = pullback(jnp.ones_like(total))
    losses, y = extra
    return (losses, y.astype(jnp.bfloat16), grads[0], grads[1], grads[2], grads[3], grads[4], grads[5], grads[6], grads[7], grads[8])
```

```python
import jax
import jax.numpy as jnp
from jax import lax
from jax.sharding import PartitionSpec as P

HEAD = 64
PATCHES = 50
CAPS = 4
TILE = 512

HIGH = lax.Precision.HIGHEST
F32 = jnp.float32
BF16 = jnp.bfloat16


def gelu(z):
    return 0.5 * z * (1.0 + jnp.tanh(0.7978845608028654 * (z + 0.044715 * z * z * z)))


def normalize(x):
    mean = jnp.mean(x, axis=-1, keepdims=True)
    cent = x - mean
    rstd = lax.rsqrt(jnp.mean(cent * cent, axis=-1, keepdims=True) + 1e-06)
    return (cent * rstd, rstd)


def norm_back(grad, normed, rstd):
    return rstd * (
        grad
        - jnp.mean(grad, axis=-1, keepdims=True)
        - normed * jnp.mean(grad * normed, axis=-1, keepdims=True)
    )


def matmul(left, right):
    return jnp.dot(left, right, preferred_element_type=F32)


def left_product(left, right):
    return lax.dot_general(left, right, (((0,), (0,)), ((), ())), preferred_element_type=F32)


def right_product(left, right):
    return lax.dot_general(left, right, (((1,), (1,)), ((), ())), preferred_element_type=F32)


def attention(qkv, same):
    groups, length, triple = qkv.shape
    width = triple // 3
    heads = width // HEAD
    query = qkv[..., :width].reshape(groups, length, heads, HEAD)
    keys = qkv[..., width : 2 * width].reshape(groups, length, heads, HEAD)
    values = qkv[..., 2 * width :].reshape(groups, length, heads, HEAD)
    scores = jnp.einsum("gthd,gshd->ghts", query, keys, preferred_element_type=F32) * 0.125
    scores = jnp.where(same[:, None], scores, -1000000000.0)
    top = jnp.max(scores, axis=-1, keepdims=True)
    expo = jnp.exp(scores - top)
    probs = expo / jnp.sum(expo, axis=-1, keepdims=True)
    mixed = jnp.einsum("ghts,gshd->gthd", probs.astype(BF16), values, preferred_element_type=F32)
    return (mixed.reshape(groups * length, width).astype(BF16), probs, query, keys, values)


def forward_block(x, same, groups, gains, shifts, w_qkv, w_out, w_in, biases):
    width = x.shape[1]
    units = w_in.shape[1]
    normed1, rstd1 = normalize(x)
    act1 = (normed1 * gains[:width] + shifts[:width]).astype(BF16)
    qkv = matmul(act1, w_qkv).astype(BF16).reshape(groups, -1, 3 * width)
    mixed, probs, query, keys, values = attention(qkv, same)
    second = x + matmul(mixed, w_out)
    normed2, rstd2 = normalize(second)
    act2 = (normed2 * gains[width:] + shifts[width:]).astype(BF16)
    inner = matmul(act2, w_in) + biases[:units]
    hidden = gelu(inner).astype(BF16)
    return (second, hidden, (normed1, rstd1, act1, probs, query, keys, values, mixed, normed2, rstd2, act2, inner))


def pack(w_qkv, w_out, w_in, w_down, w_proj, vectors):
    rows = w_qkv.shape[0]
    down = w_down.reshape(-1, rows, w_down.shape[1])
    block = jnp.pad(vectors, (0, rows * 128 - vectors.shape[0])).reshape(rows, 128)
    return jnp.concatenate([w_qkv, w_out, w_in, w_proj, *down, block], axis=1)


def unpack(whole, devices, width, units):
    rows = width // devices
    cuts = [3 * width, 4 * width, 4 * width + units, 5 * width + units]
    down = whole[:, cuts[3] : cuts[3] + units]
    down = down.reshape(devices, rows, units // width, width).transpose(0, 2, 1, 3).reshape(units, width)
    vectors = whole[:, cuts[3] + units :].reshape(devices, rows * 128)
    return (
        whole[:, : cuts[0]],
        whole[:, cuts[0] : cuts[1]],
        whole[:, cuts[1] : cuts[2]],
        down,
        whole[:, cuts[2] : cuts[3]],
        vectors,
    )


def gather(part):
    return lax.all_gather(part, "blk", axis=0, tiled=True)


def split_vectors(vectors, sizes):
    parts = []
    start = 0
    for size in sizes:
        parts.append(vectors[:, start : start + size].reshape(-1))
        start += size
    return parts


def head_tile(proj, factor, image_emb, scale, row_lse, col_lse, pairs, sim):
    hit = pairs[:, None] == jnp.arange(image_emb.shape[0], dtype=jnp.int32)[None, :]
    weights_sim = (
        0.5 * jnp.exp(sim - row_lse[:, None]) + 0.5 * jnp.exp(sim - col_lse[None, :]) - hit.astype(F32)
    )
    d_emb = scale * matmul(weights_sim.astype(BF16), image_emb)
    d_proj = factor * d_emb - proj * (factor * factor * factor) * jnp.sum(d_emb * proj, axis=-1, keepdims=True)
    pos = jnp.sum(jnp.where(hit, sim, 0.0), axis=1)
    pair_col = jnp.sum(jnp.where(hit, col_lse[None, :], 0.0), axis=1)
    return (d_proj.astype(BF16), 0.5 * (row_lse - pos) + 0.5 * (pair_col - pos))


def unit_rows(proj):
    factor = lax.rsqrt(jnp.sum(proj * proj, axis=-1, keepdims=True) + 1e-06)
    return (proj * factor, factor)


def on_device(devices, *args):
    (
        text_tokens,
        segment_ids,
        pair_index,
        image_tokens,
        logit_scale,
        img_gains,
        img_shifts,
        img_qkv,
        img_out,
        img_in,
        img_down,
        img_biases,
        img_proj,
        txt_gains,
        txt_shifts,
        txt_qkv,
        txt_out,
        txt_in,
        txt_down,
        txt_biases,
        txt_proj,
    ) = args
    width = text_tokens.shape[1]
    units = img_in.shape[1]
    scale = logit_scale[0]
    rows, length = segment_ids.shape
    tokens = rows * length
    captions = pair_index.shape[0]
    images = image_tokens.shape[0] // PATCHES
    device = lax.axis_index("blk")

    caption_of = (jnp.arange(rows, dtype=jnp.int32)[:, None] * CAPS + segment_ids).reshape(tokens)
    member = (jnp.arange(captions, dtype=jnp.int32)[:, None] == caption_of[None, :]).astype(F32)
    counts = jnp.sum(member, axis=1)

    vec = (width * 2 // devices, width * 2 // devices, (units + width) // devices)
    image_whole = gather(
        pack(img_qkv, img_out, img_in, img_down, img_proj, jnp.concatenate([img_gains, img_shifts, img_biases]))
    )
    text_vectors = jnp.concatenate(
        [
            txt_gains,
            txt_shifts,
            txt_biases,
            (pair_index // 64).astype(BF16),
            (pair_index % 64).astype(BF16),
            counts.astype(BF16),
        ]
    )
    text_whole = gather(pack(txt_qkv, txt_out, txt_in, txt_down, txt_proj, text_vectors))

    w_qkv, w_out, w_in, w_down, w_proj, vectors = unpack(image_whole, devices, width, units)
    gains, shifts, biases = split_vectors(vectors, vec)
    every = jnp.ones((images, PATCHES, PATCHES), jnp.bool_)
    second, hidden, unused = forward_block(
        image_tokens.astype(F32), every, images, gains, shifts, w_qkv, w_out, w_in, biases
    )
    image_y = second + matmul(hidden, w_down) + biases[units:]
    image_pool = jnp.mean(image_y.reshape(images, PATCHES, width), axis=1).astype(BF16)
    image_proj = w_proj

    w_qkv, w_out, w_in, w_down, w_proj, vectors = unpack(text_whole, devices, width, units)
    gains, shifts, biases, pair_hi, pair_lo, every_count = split_vectors(vectors, vec + (captions,) * 3)
    every_pair = pair_hi.astype(jnp.int32) * 64 + pair_lo.astype(jnp.int32)
    same = segment_ids[:, :, None] == segment_ids[:, None, :]
    x = text_tokens.astype(F32)
    second, hidden, kept = forward_block(x, same, rows, gains, shifts, w_qkv, w_out, w_in, biases)
    y = second + matmul(hidden, w_down) + biases[units:]
    normed1, rstd1, act1, probs, query, keys, values, mixed, normed2, rstd2, act2, inner = kept
    text_out = y.astype(BF16)
    share = member / counts[:, None]
    pool_low = jnp.dot(share, y, precision=HIGH, preferred_element_type=F32).astype(BF16)
    hidden_sum = jnp.dot(member, hidden.astype(F32), precision=HIGH, preferred_element_type=F32).astype(BF16)
    hidden_sum = lax.all_to_all(hidden_sum, "blk", split_axis=1, concat_axis=0, tiled=True)

    pools = gather(jnp.concatenate([image_pool, pool_low])).reshape(devices, 2, captions, width)
    image_emb = unit_rows(matmul(pools[:, 0].reshape(-1, width), image_proj))[0].astype(BF16)
    pool_all = pools[:, 1].reshape(-1, width)
    total = pool_all.shape[0]
    col_max = jnp.full((total,), -1e30, F32)
    col_sum = jnp.zeros((total,), F32)
    held = []
    for start in range(0, total, TILE):
        proj = matmul(pool_all[start : start + TILE], w_proj)
        unit, factor = unit_rows(proj)
        sim = scale * right_product(unit.astype(BF16), image_emb)
        top = jnp.max(sim, axis=1)
        row_lse = top + jnp.log(jnp.sum(jnp.exp(sim - top[:, None]), axis=1))
        new_max = jnp.maximum(col_max, jnp.max(sim, axis=0))
        col_sum = col_sum * jnp.exp(col_max - new_max) + jnp.sum(jnp.exp(sim - new_max[None, :]), axis=0)
        col_max = new_max
        held.append((proj, factor, row_lse, sim))
    col_lse = col_max + jnp.log(col_sum)
    d_proj = []
    losses = []
    for start, (proj, factor, row_lse, sim) in zip(range(0, total, TILE), held):
        grad, loss = head_tile(
            proj, factor, image_emb, scale, row_lse, col_lse, every_pair[start : start + TILE], sim
        )
        d_proj.append(grad)
        losses.append(loss)
    d_proj = jnp.concatenate(d_proj)
    pair_loss = lax.dynamic_slice_in_dim(jnp.concatenate(losses), device * captions, captions)
    own = width // devices
    grad_proj = left_product(lax.dynamic_slice_in_dim(pool_all, device * own, own, axis=1), d_proj)
    d_each = right_product(d_proj, w_proj) / every_count.astype(F32)[:, None]
    grad_down = left_product(hidden_sum, d_each.astype(BF16))
    d_mine = lax.dynamic_slice_in_dim(d_each, device * captions, captions)

    d_y = lax.dot_general(member, d_mine, (((0,), (0,)), ((), ())), precision=HIGH, preferred_element_type=F32)
    grad_outer = jnp.sum(d_y, axis=0)
    d_hidden = right_product(d_mine.astype(BF16), w_down)
    d_hidden = lax.dot_general(member, d_hidden, (((0,), (0,)), ((), ())), precision=HIGH, preferred_element_type=F32)
    unused_value, gelu_pull = jax.vjp(gelu, inner)
    d_inner = gelu_pull(d_hidden)[0].astype(BF16)
    grad_in = left_product(act2, d_inner)
    grad_inner = jnp.sum(d_inner.astype(F32), axis=0)
    grad_biases = jnp.concatenate([grad_inner, grad_outer])
    d_act2 = right_product(d_inner, w_in)
    gain2 = jnp.sum(d_act2 * normed2, axis=0)
    shift2 = jnp.sum(d_act2, axis=0)
    d_second = d_y + norm_back(d_act2 * gains[width:], normed2, rstd2)
    d_second_low = d_second.astype(BF16)
    grad_out = left_product(mixed, d_second_low)
    d_mixed = right_product(d_second_low, w_out).astype(BF16).reshape(rows, length, width // HEAD, HEAD)
    probs_low = probs.astype(BF16)
    d_values = jnp.einsum("ghts,gthd->gshd", probs_low, d_mixed, preferred_element_type=F32)
    d_probs = jnp.einsum("gthd,gshd->ghts", d_mixed, values, preferred_element_type=F32)
    d_scores = (probs * (d_probs - jnp.sum(probs * d_probs, axis=-1, keepdims=True))).astype(BF16)
    d_query = 0.125 * jnp.einsum("ghts,gshd->gthd", d_scores, keys, preferred_element_type=F32)
    d_keys = 0.125 * jnp.einsum("ghts,gthd->gshd", d_scores, query, preferred_element_type=F32)
    d_qkv = jnp.concatenate(
        [d_query.reshape(tokens, width), d_keys.reshape(tokens, width), d_values.reshape(tokens, width)], axis=1
    ).astype(BF16)
    grad_qkv = left_product(act1, d_qkv)
    d_act1 = right_product(d_qkv, w_qkv)
    gain1 = jnp.sum(d_act1 * normed1, axis=0)
    shift1 = jnp.sum(d_act1, axis=0)
    text_grad = d_second + norm_back(d_act1 * gains[:width], normed1, rstd1)
    sums = jnp.concatenate(
        [
            jnp.concatenate([gain1, gain2]).reshape(devices, -1),
            jnp.concatenate([shift1, shift2]).reshape(devices, -1),
            grad_biases.reshape(devices, -1),
        ],
        axis=1,
    )
    used = sums.shape[1]
    sums = jnp.pad(sums, ((0, 0), (0, own * 128 - used))).reshape(width, 128)
    mine = lax.psum_scatter(
        jnp.concatenate([grad_qkv, grad_out, grad_in, sums], axis=1).astype(BF16),
        "blk",
        scatter_dimension=0,
        tiled=True,
    ).astype(F32)
    sums = mine[:, 4 * width + units :].reshape(-1)
    return (
        pair_loss,
        text_out,
        text_grad,
        sums[: vec[0]],
        sums[vec[0] : vec[0] + vec[1]],
        mine[:, : 3 * width],
        mine[:, 3 * width : 4 * width],
        mine[:, 4 * width : 4 * width + units],
        grad_down,
        sums[vec[0] + vec[1] : used],
        grad_proj,
    )


def solution(mesh):
    devices = mesh.shape["blk"]
    row = P("blk", None)
    flat = P("blk")
    tower = (flat, flat, row, row, row, row, flat, row)

    def body(*args):
        return on_device(devices, *args)

    return jax.shard_map(
        body,
        mesh=mesh,
        in_specs=(row, row, flat, row, P()) + tower + tower,
        out_specs=(flat, row, row, flat, flat, row, row, row, row, flat, row),
        check_vma=False,
    )
```

```python
import functools

import jax
import jax.numpy as jnp
from jax import lax
from jax.experimental import pallas as pl
from jax.experimental.pallas import tpu as pltpu
from jax.sharding import PartitionSpec as P

HEAD = 64
PATCHES = 50
CAPS = 4
TILE = 512
GROUP_PAD = 112

F32 = jnp.float32
BF16 = jnp.bfloat16


def gelu(z):
    return 0.5 * z * (1.0 + jnp.tanh(0.7978845608028654 * (z + 0.044715 * z * z * z)))


def normalize(x):
    mean = jnp.mean(x, axis=-1, keepdims=True)
    cent = x - mean
    rstd = lax.rsqrt(jnp.mean(cent * cent, axis=-1, keepdims=True) + 1e-06)
    return (cent * rstd, rstd)


def norm_back(grad, normed, rstd):
    return rstd * (
        grad
        - jnp.mean(grad, axis=-1, keepdims=True)
        - normed * jnp.mean(grad * normed, axis=-1, keepdims=True)
    )


def unit_rows(proj):
    factor = lax.rsqrt(jnp.sum(proj * proj, axis=-1, keepdims=True) + 1e-06)
    return (proj * factor, factor)


def matmul(left, right):
    return jnp.dot(left, right, preferred_element_type=F32)


def dot_nt(left, right):
    return lax.dot_general(left, right, (((1,), (1,)), ((), ())), preferred_element_type=F32)


def dot_tn(left, right):
    return lax.dot_general(left, right, (((0,), (0,)), ((), ())), preferred_element_type=F32)


def chunks(total, size):
    def wrap(body):
        @pl.loop(0, total // size)
        def step(j):
            body(pl.ds(pl.multiple_of(j * size, size), size))

    return wrap


def thirds(value):
    high = value.astype(BF16)
    rest = value - high.astype(F32)
    mid = rest.astype(BF16)
    return high, mid, (rest - mid.astype(F32)).astype(BF16)


def norm_rows(x, gain, shift):
    normed, rstd = normalize(x)
    return (normed * gain + shift).astype(BF16)


def head_masks(dtype, value):
    lane = lax.broadcasted_iota(jnp.int32, (1, 2 * HEAD), 1)
    first = jnp.where(lane < HEAD, value, 0.0).astype(dtype)
    second = jnp.where(lane < HEAD, 0.0, value).astype(dtype)
    return first, second


def both_heads(block, masks):
    return jnp.concatenate([block * masks[0], block * masks[1]], axis=0)


def merge_heads(stacked):
    half = stacked.shape[0] // 2
    lane = lax.broadcasted_iota(jnp.int32, (1, 2 * HEAD), 1)
    return jnp.where(lane < HEAD, stacked[:half], stacked[half:])


def softmax_unit(query, keys, mask, masks):
    scores = dot_nt(both_heads(query, masks), keys)
    scores = jnp.where(mask, scores, -1000000000.0)
    top = jnp.max(scores, axis=-1, keepdims=True)
    expo = jnp.exp(scores - top)
    return expo * (1.0 / jnp.sum(expo, axis=-1, keepdims=True))


def image_attention(x, gains, shifts, w_qkv, w_out, second, act, qkv, mixed):
    rows, width = x.shape
    group = GROUP_PAD

    @chunks(rows, group)
    def _(at):
        act[at, :] = norm_rows(x[at, :].astype(F32), gains[0:1, :], shifts[0:1, :])

    w_qkv = w_qkv()

    @chunks(3 * width, 256)
    def _(at):
        qkv[:, at] = matmul(act[...], w_qkv[:, at]).astype(BF16)

    masks = head_masks(BF16, 0.125)
    own = lax.broadcasted_iota(jnp.int32, (2 * group, group), 0)
    own = jnp.where(own >= group, own - group, own)
    other = lax.broadcasted_iota(jnp.int32, (2 * group, group), 1)
    mask = picture(own) == picture(other)

    @chunks(rows, group)
    def _(at):
        for start in range(0, width, 2 * HEAD):
            cols = slice(start, start + 2 * HEAD)
            keys = qkv[at, width + start : width + start + 2 * HEAD]
            values = qkv[at, 2 * width + start : 2 * width + start + 2 * HEAD]
            probs = softmax_unit(qkv[at, cols], keys, mask, masks)
            mixed[at, cols] = merge_heads(matmul(probs.astype(BF16), values)).astype(BF16)

    w_out = w_out()

    @chunks(width, 256)
    def _(at):
        second[:, at] = x[:, at].astype(F32) + matmul(mixed[...], w_out[:, at])


def picture(place):
    return jnp.where(place >= PATCHES, 1, 0) + jnp.where(place >= 2 * PATCHES, 1, 0)


def image_pool(value):
    value = value.reshape(-1, GROUP_PAD, value.shape[1])
    which = picture(lax.broadcasted_iota(jnp.int32, (1, GROUP_PAD, 1), 1))
    parts = [jnp.sum(jnp.where(which == kind, value, 0.0), axis=1) for kind in range(2)]
    return jnp.concatenate(parts, axis=0) * (1.0 / PATCHES)


def image_inner(second, gains, shifts, biases, w_in, pooled, pooled_second, act):
    rows, width = second.shape
    units = pooled.shape[1]

    @chunks(rows, GROUP_PAD)
    def _(at):
        act[at, :] = norm_rows(second[at, :], gains[1:2, :], shifts[1:2, :])

    for start in range(0, width, 256):
        pooled_second[:, start : start + 256] = image_pool(second[:, start : start + 256])
    w_in = w_in()

    @chunks(units, 256)
    def _(at):
        hidden = gelu(matmul(act[...], w_in[:, at]) + biases[:, at]).astype(BF16).astype(F32)
        pooled[:, at] = image_pool(hidden)


def image_embed(pooled, pooled_second, biases, w_down, w_proj, emb):
    images, units = pooled.shape
    high, mid, unused = thirds(pooled[...])
    w_down = w_down()
    y = matmul(jnp.concatenate([high, mid], axis=0), w_down[...])
    y = y[:images] + y[images:] + pooled_second[...] + biases[:, units:]
    emb[...] = unit_rows(matmul(y.astype(BF16), w_proj()[...]))[0].astype(BF16)


def text_attention(x, caption_col, caption_row, gains, shifts, w_qkv, w_out, qkv, probs, mixed, second, act):
    rows, width = x.shape
    group = 2 * HEAD
    act[...] = norm_rows(x[...].astype(F32), gains[0:1, :], shifts[0:1, :])
    w_qkv = w_qkv()

    @chunks(3 * width, 256)
    def _(at):
        qkv[:, at] = matmul(act[...], w_qkv[:, at]).astype(BF16)

    masks = head_masks(BF16, 0.125)
    unit = 0
    for top in range(0, rows, group):
        at = slice(top, top + group)
        same = caption_col[at, :] == caption_row[:, at]
        mask = jnp.concatenate([same, same], axis=0)
        for start in range(0, width, 2 * HEAD):
            cols = slice(start, start + 2 * HEAD)
            keys = qkv[at, width + start : width + start + 2 * HEAD]
            values = qkv[at, 2 * width + start : 2 * width + start + 2 * HEAD]
            prob = softmax_unit(qkv[at, cols], keys, mask, masks)
            probs[unit] = prob
            unit += 1
            mixed[at, cols] = merge_heads(matmul(prob.astype(BF16), values)).astype(BF16)

    w_out = w_out()

    @chunks(width, 256)
    def _(at):
        second[:, at] = x[:, at].astype(F32) + matmul(mixed[...], w_out[:, at])


def caption_member(caption_row, captions):
    index = lax.broadcasted_iota(jnp.int32, (captions, caption_row.shape[1]), 0)
    return (index == caption_row[...]).astype(F32)


def text_inner(second, caption_row, gains, shifts, biases, w_in, hidden, slope, hidden_sum, act):
    units = hidden.shape[1]
    act[...] = norm_rows(second[...], gains[1:2, :], shifts[1:2, :])
    low = caption_member(caption_row, hidden_sum.shape[0]).astype(BF16)
    w_in = w_in()

    @chunks(units, 256)
    def _(at):
        z = matmul(act[...], w_in[:, at]) + biases[:, at]
        inside = jnp.tanh(0.7978845608028654 * (z + 0.044715 * z * z * z))
        value = (0.5 * z * (1.0 + inside)).astype(BF16)
        hidden[:, at] = value
        slope[:, at] = 0.5 * (1.0 + inside) + 0.5 * z * (1.0 - inside * inside) * (
            0.7978845608028654 * (1.0 + 3.0 * 0.044715 * z * z)
        )
        hidden_sum[:, at] = matmul(low, value).astype(BF16)


def text_outer(second, hidden, caption_row, biases, w_down, out, pool_low):
    width = second.shape[1]
    units = hidden.shape[1]
    member = caption_member(caption_row, pool_low.shape[0])
    low = member.astype(BF16)
    count = jnp.sum(member, axis=1, keepdims=True)
    w_down = w_down()

    @chunks(width, 256)
    def _(at):
        outer = biases[:, pl.ds(pl.multiple_of(units + at.start, 256), 256)]
        y = second[:, at] + matmul(hidden[...], w_down[:, at]) + outer
        out[:, at] = y.astype(BF16)
        total = sum(matmul(low, part) for part in thirds(y))
        pool_low[:, at] = (total / count).astype(BF16)


def core_split(table, value, devices, mine, theirs):
    own = value.shape[0] // devices
    value = value.reshape(devices // 2, 2, own, value.shape[1])
    first = table[CORE] == 0
    even = value[:, 0].reshape(-1, value.shape[3])
    odd = value[:, 1].reshape(-1, value.shape[3])
    mine[...] = jnp.where(first, even, odd).astype(BF16)
    theirs[...] = jnp.where(first, odd, even).astype(BF16)


def back_inner(
    devices, table, each, caption_col, second, slope, gains, shifts, w_down, w_in, w_out,
    mine, theirs, d_second, d_mixed, sums_in, sums_out, act_t, act_u, both, d_act,
):
    rows, width = second.shape
    units = slope.shape[1]
    captions = each.shape[0]
    index = lax.broadcasted_iota(jnp.int32, (rows, 3 * captions), 1)
    index = jnp.where(index >= captions, index - captions, index)
    index = jnp.where(index >= captions, index - captions, index)
    member = (caption_col[...] == index).astype(BF16)
    normed, rstd = normalize(second[...])
    act = normed * gains[1:2, :] + shifts[1:2, :]
    core_split(table, act.T, devices, act_t, act_u)
    each_low = each[...].astype(BF16)
    w_down = w_down()

    @chunks(units, 256)
    def _(at):
        both[:, at] = jnp.concatenate(thirds(dot_nt(each_low, w_down[at, :])), axis=0)

    d_act[...] = jnp.zeros_like(d_act)
    w_in = w_in()

    @chunks(units, 256)
    def _(at):
        d_inner = matmul(member, both[:, at]) * slope[:, at]
        low = d_inner.astype(BF16)
        sums_in[:, at] = jnp.sum(low.astype(F32), axis=0, keepdims=True)
        theirs[:, at] = matmul(act_u[...], low).astype(BF16)
        mine[:, at] = matmul(act_t[...], low).astype(BF16)
        d_act[...] += dot_nt(low, w_in[:, at])

    d_y = matmul(member, jnp.concatenate(thirds(each[...]), axis=0))
    grad = d_act[...]
    sums_out[0:1, :] = jnp.sum(d_y, axis=0, keepdims=True)
    sums_out[1:2, :] = jnp.sum(grad * normed, axis=0, keepdims=True)
    sums_out[2:3, :] = jnp.sum(grad, axis=0, keepdims=True)
    d_two = d_y + norm_back(grad * gains[1:2, :], normed, rstd)
    d_second[...] = d_two
    low_two = d_two.astype(BF16)
    d_mixed[...] = dot_nt(low_two, w_out()[...]).astype(BF16)


def back_attention(
    devices, table, x, d_second, d_mixed, qkv, probs, mixed, gains, shifts, w_qkv,
    mine, theirs, text_grad, sums, d_qkv, act_t, act_u, mixed_t, mixed_u, d_act,
):
    rows, width = x.shape
    group = 2 * HEAD
    normed, rstd = normalize(x[...].astype(F32))
    act = normed * gains[0:1, :] + shifts[0:1, :]
    core_split(table, act.T, devices, act_t, act_u)
    core_split(table, mixed[...].astype(F32).T, devices, mixed_t, mixed_u)
    ones = head_masks(BF16, 1.0)
    masks = head_masks(BF16, 0.125)
    unit = 0
    for top in range(0, rows, group):
        at = slice(top, top + group)
        for start in range(0, width, 2 * HEAD):
            cols = slice(start, start + 2 * HEAD)
            key_cols = slice(width + start, width + start + 2 * HEAD)
            value_cols = slice(2 * width + start, 2 * width + start + 2 * HEAD)
            prob = probs[unit]
            unit += 1
            d_out = both_heads(d_mixed[at, cols], ones)
            query = both_heads(qkv[at, cols], masks)
            d_qkv[at, value_cols] = dot_tn(prob.astype(BF16), d_out).astype(BF16)
            d_prob = dot_nt(d_out, qkv[at, value_cols])
            d_score = (prob * (d_prob - jnp.sum(prob * d_prob, axis=-1, keepdims=True))).astype(BF16)
            d_qkv[at, cols] = (0.125 * merge_heads(matmul(d_score, qkv[at, key_cols]))).astype(BF16)
            d_qkv[at, key_cols] = dot_tn(d_score, query).astype(BF16)

    d_low = d_second[...].astype(BF16)
    for start in range(0, width, 256):
        at = slice(start, start + 256)
        to = slice(3 * width + start, 3 * width + start + 256)
        theirs[:, to] = matmul(mixed_u[...], d_low[:, at]).astype(BF16)
        mine[:, to] = matmul(mixed_t[...], d_low[:, at]).astype(BF16)
    d_act[...] = jnp.zeros_like(d_act)
    w_qkv = w_qkv()

    @chunks(3 * width, 256)
    def _(at):
        theirs[:, at] = matmul(act_u[...], d_qkv[:, at]).astype(BF16)
        mine[:, at] = matmul(act_t[...], d_qkv[:, at]).astype(BF16)
        d_act[...] += dot_nt(d_qkv[:, at], w_qkv[:, at])

    grad = d_act[...]
    sums[0:1, :] = jnp.sum(grad * normed, axis=0, keepdims=True)
    sums[1:2, :] = jnp.sum(grad, axis=0, keepdims=True)
    text_grad[...] = d_second[...] + norm_back(grad * gains[0:1, :], normed, rstd)


class Weight:
    def __init__(self, rows, cols):
        self.dims = (rows, cols)
        self.parts = []

    def add(self, array, lead, start, width, row, row_unit, col=None):
        self.parts.append((array, lead, start, width, row, row_unit, col))


def run(kernel, outs, scratch, table, operands, weights, us=5, passes_table=False):
    arrays = []
    for weight in weights:
        for part in weight.parts:
            if not any(part[0] is a for a in arrays):
                arrays.append(part[0])
    places = {id(a): i for i, a in enumerate(arrays)}
    n_op, n_arr, n_out, n_w = len(operands), len(arrays), len(outs), len(weights)

    def body(*refs):
        table_ref, refs = refs[0], refs[1:]
        ops, refs = refs[:n_op], refs[n_op:]
        arrs, refs = refs[:n_arr], refs[n_arr:]
        out, refs = refs[:n_out], refs[n_out:]
        held, refs = refs[:n_w], refs[n_w:]
        if n_w:
            sems, refs = refs[0], refs[1:]
        waits = []
        for i, weight in enumerate(weights):
            for array, lead, start, width, row, row_unit, col in weight.parts:
                at = 0 if row is None else pl.multiple_of(table_ref[row] * row_unit, 16)
                to = 0 if col is None else pl.multiple_of(table_ref[col] * width, 128)
                pltpu.make_async_copy(
                    arrs[places[id(array)]].at[lead, :, pl.ds(start, width)],
                    held[i].at[pl.ds(at, array.shape[1]), pl.ds(to, width)],
                    sems.at[i],
                ).start()

            def wait(i=i):
                pltpu.make_async_copy(held[i], held[i], sems.at[i]).wait()
                return held[i]

            waits.append(wait)
        if passes_table:
            ops = (table_ref, *ops)
        kernel(*ops, *waits, *out, *refs)

    vmem = pl.BlockSpec(memory_space=pltpu.VMEM)
    moved = sum(a.size * a.dtype.itemsize for a in (*operands, *outs))
    moved += sum(w.dims[0] * w.dims[1] * 2 for w in weights)
    held = sum(a.size * a.dtype.itemsize for a in (*operands, *outs))
    return pl.pallas_call(
        body,
        out_shape=outs,
        in_specs=[pl.BlockSpec(memory_space=pltpu.SMEM)] + [vmem] * n_op + [pl.BlockSpec(memory_space=pl.ANY)] * n_arr,
        out_specs=[vmem] * n_out,
        scratch_shapes=[pltpu.VMEM(w.dims, BF16) for w in weights]
        + ([pltpu.SemaphoreType.DMA((n_w,))] if n_w else [])
        + [pltpu.VMEM(*s) for s in scratch],
        compiler_params=pltpu.CompilerParams(vmem_limit_bytes=56 << 20),
        cost_estimate=pl.CostEstimate(flops=us * 1100000000, bytes_accessed=moved, transcendentals=0),
    )(table, *operands, *arrays)


def shape(dims, dtype):
    return jax.ShapeDtypeStruct(dims, dtype)


class Grid:
    def __init__(self, devices, sizes):
        self.devices = devices
        self.sizes = sizes
        strides = []
        step = devices
        for size in sizes:
            step //= size
            strides.append(step)
        self.strides = strides
        self.regular = len(sizes) == 4 and sizes[1:] == [2, 2, 2]

    def place(self):
        index = lax.axis_index("blk")
        return [(index // st) % size for size, st in zip(self.sizes, self.strides)]

    def shift(self, value, axis, step):
        size, stride = self.sizes[axis], self.strides[axis]
        pairs = []
        for i in range(self.devices):
            at = (i // stride) % size
            pairs.append((i, i + ((at + step) % size - at) * stride))
        return lax.ppermute(value, "blk", pairs)

    def table(self):
        place = self.place()
        chips = []
        for dz, dy, dx in self.offsets():
            origin = [(p - d) % s for p, d, s in zip(place, (dz, dy, dx), self.sizes)]
            chips.append(sum(o * st for o, st in zip(origin, self.strides)) // 2)
        chips = jnp.stack(chips)
        core = place[3]
        return jnp.concatenate([jnp.stack([core, 1 - core]), chips, 2 * chips + core, 2 * chips + 1 - core]).astype(
            jnp.int32
        )

    def offsets(self):
        z, y, x, unused = self.sizes
        return [(dz, dy, dx) for dz in range(z) for dy in range(y) for dx in range(x)]

    def row_of(self, offset, kind):
        chips = self.devices // 2
        return 2 + self.offsets().index(offset) + {"chip": 0, "own": chips, "other": 2 * chips}[kind]

    def line(self, value):
        return jnp.stack([value] + [self.shift(value, 0, k) for k in range(1, self.sizes[0])])

    def square(self, line):
        return self.shift(line, 2, 1), self.shift(line, 1, 1)

    def corner(self, by_x, by_y):
        half = self.sizes[0] // 2
        return self.shift(by_x[:half], 1, 1), self.shift(by_y[half:], 2, 1)

    def pieces(self, line, by_x, by_y, via_x, via_y):
        zs = range(self.sizes[0])
        half = self.sizes[0] // 2
        return [
            (line, [(z, 0, 0) for z in zs]),
            (by_x, [(z, 0, 1) for z in zs]),
            (by_y, [(z, 1, 0) for z in zs]),
            (via_x, [(z, 1, 1) for z in zs[:half]]),
            (via_y, [(z, 1, 1) for z in zs[half:]]),
        ]

    def pieces_z_last(self, squares):
        flat = [(0, 0), (0, 1), (1, 0), (1, 1)]
        return [(square, [(z, *f) for f in flat]) for z, square in enumerate(squares)]

    def across(self, pieces):
        return [(self.shift(array, 3, 1), offsets) for array, offsets in pieces]

    def reduce(self, mine, theirs):
        z, y, x, unused = self.place()
        depth = self.sizes[0]
        cols = mine.shape[1]

        def take(value, at, axis):
            return lax.dynamic_index_in_dim(value, at, axis, keepdims=False)

        def low(value):
            return value.astype(BF16)

        got = self.shift(theirs, 3, 1)
        total = (mine.astype(F32) + got.astype(F32)).reshape(depth, 2, 2, -1, cols)
        left, right = total[..., : cols // 2], total[..., cols // 2 :]
        left_got = self.shift(low(take(left, 1 - x, 2)), 2, 1)
        right_got = self.shift(low(take(right, 1 - y, 1)), 1, 1)
        left = take(left, x, 2) + left_got.astype(F32)
        right = take(right, y, 1) + right_got.astype(F32)
        left_got = self.shift(low(take(left, 1 - y, 1)), 1, 1)
        right_got = self.shift(low(take(right, 1 - x, 1)), 2, 1)
        left = take(left, y, 1) + left_got.astype(F32)
        right = take(right, x, 1) + right_got.astype(F32)
        line = jnp.concatenate([left, right], axis=-1)
        total = take(line, z, 0)
        for k in range(1, depth):
            total = total + self.shift(low(take(line, (z + k) % depth, 0)), 0, k).astype(F32)
        return total


def after(value, *earlier):
    return lax.optimization_barrier((value, *earlier))[0]


CORE = 0
OTHER = 1


def to_all(value, devices):
    return lax.all_to_all(jnp.broadcast_to(value[None], (devices, *value.shape)), "blk", 0, 0)


def pair_up(grid, weights):
    first = lax.axis_index("blk") % 2 == 0
    left = jnp.concatenate([w[:, : w.shape[1] // 2] for w in weights], axis=1)
    right = jnp.concatenate([w[:, w.shape[1] // 2 :] for w in weights], axis=1)
    keep = jnp.where(first, left, right)
    got = grid.shift(jnp.where(first, right, left), 3, 1)
    return jnp.concatenate([jnp.where(first, keep, got), jnp.where(first, got, keep)], axis=0)


def halves(grid, weight, pieces, others, start):
    for group, col in ((pieces, CORE), (others, OTHER)):
        for array, offsets in group:
            for lead, offset in enumerate(offsets):
                row = grid.row_of(offset, "chip")
                weight.add(array, lead, start, weight.dims[1] // 2, row, array.shape[1], col)
    return weight


def rows_of(grid, weight, pieces, others):
    for group, kind in ((pieces, "own"), (others, "other")):
        for array, offsets in group:
            for lead, offset in enumerate(offsets):
                weight.add(array, lead, 0, weight.dims[1], grid.row_of(offset, kind), array.shape[1])
    return weight


def gathered(part):
    full = lax.all_gather(part, "blk", axis=0, tiled=True)
    weight = Weight(*full.shape)
    weight.add(full[None], 0, 0, full.shape[1], None, 0)
    return weight


def reduce_grads(grid, mine, theirs, width):
    own = width // grid.devices
    if grid.regular and own % 8 == 0:
        return grid.reduce(mine, theirs)
    both = jnp.where(lax.axis_index("blk") % 2 == 0, jnp.stack([mine, theirs], 0), jnp.stack([theirs, mine], 0))
    both = both.reshape(2, grid.devices // 2, own, -1).transpose(1, 0, 2, 3).reshape(width, -1)
    return lax.psum_scatter(both, "blk", scatter_dimension=0, tiled=True).astype(F32)


def head_tile(proj, factor, image_emb, scale, row_lse, col_lse, pairs, sim):
    hit = pairs[:, None] == jnp.arange(image_emb.shape[0], dtype=jnp.int32)[None, :]
    weights_sim = (
        0.5 * jnp.exp(sim - row_lse[:, None]) + 0.5 * jnp.exp(sim - col_lse[None, :]) - hit.astype(F32)
    )
    d_emb = scale * matmul(weights_sim.astype(BF16), image_emb)
    d_proj = factor * d_emb - proj * (factor * factor * factor) * jnp.sum(d_emb * proj, axis=-1, keepdims=True)
    pos = jnp.sum(jnp.where(hit, sim, 0.0), axis=1)
    pair_col = jnp.sum(jnp.where(hit, col_lse[None, :], 0.0), axis=1)
    return (d_proj.astype(BF16), 0.5 * (row_lse - pos) + 0.5 * (pair_col - pos))


def on_device(grid, *args):
    (
        text_tokens,
        segment_ids,
        pair_index,
        image_tokens,
        logit_scale,
        img_gains,
        img_shifts,
        img_qkv,
        img_out,
        img_in,
        img_down,
        img_biases,
        img_proj,
        txt_gains,
        txt_shifts,
        txt_qkv,
        txt_out,
        txt_in,
        txt_down,
        txt_biases,
        txt_proj,
    ) = args
    devices = grid.devices
    width = text_tokens.shape[1]
    units = img_in.shape[1]
    scale = logit_scale[0]
    rows, length = segment_ids.shape
    tokens = rows * length
    captions = pair_index.shape[0]
    images = image_tokens.shape[0] // PATCHES
    device = lax.axis_index("blk")
    own = width // devices
    table = grid.table()

    caption_of = (jnp.arange(rows, dtype=jnp.int32)[:, None] * CAPS + segment_ids).reshape(tokens)
    caption_col, caption_row = caption_of[:, None], caption_of[None, :]
    member = (jnp.arange(captions, dtype=jnp.int32)[:, None] == caption_row).astype(F32)
    counts = jnp.sum(member, axis=1)

    vec = (img_gains.shape[0], img_shifts.shape[0], img_biases.shape[0])
    vectors = jnp.concatenate(
        [
            img_gains,
            img_shifts,
            img_biases,
            txt_gains,
            txt_shifts,
            txt_biases,
            (pair_index // 64).astype(BF16),
            (pair_index % 64).astype(BF16),
            counts.astype(BF16),
        ]
    )
    vectors = to_all(vectors, devices).reshape(devices, -1).astype(F32)
    parts = []
    start = 0
    for size in vec + vec + (captions,) * 3:
        parts.append(vectors[:, start : start + size].reshape(-1))
        start += size
    img_g, img_s = parts[0].reshape(2, width), parts[1].reshape(2, width)
    gains, shifts = parts[3].reshape(2, width), parts[4].reshape(2, width)
    img_b, biases = parts[2].reshape(1, -1), parts[5].reshape(1, -1)
    every_pair = parts[6].astype(jnp.int32) * 64 + parts[7].astype(jnp.int32)
    every_count = parts[8]

    regular = grid.regular and own % 8 == 0
    if regular:
        tdx, tdy = grid.square(txt_down)
        idl = grid.line(img_down)
        idl = after(idl, tdx, tdy)
        td_square = jnp.stack([txt_down, tdx, tdy, grid.shift(tdx, 1, 1)])
        pair = pair_up(grid, [txt_qkv, txt_out, img_qkv, img_out, img_in, img_proj, txt_in, txt_proj])
        cuts = [0, 4 * width, 4 * width + (units + width) // 2, 4 * width + units + width]
        idx, idy = grid.square(idl)
        idv = grid.corner(idx, idy)
        line1 = grid.line(pair[:, : cuts[1]])
        line1 = after(line1, idx, idy, td_square)
        x1, y1 = grid.square(line1)
        line2 = after(grid.line(after(pair[:, cuts[1] : cuts[2]], idx, idy)), x1, y1, *idv)
        line3 = grid.line(after(pair[:, cuts[2] :], line1))
        ring1 = grid.shift(after(td_square, line1), 0, 1)
        v1 = grid.corner(x1, y1)
        x2, y2 = grid.square(line2)
        one = grid.pieces(line1, x1, y1, *v1)
        one_x = grid.across(one)
        text_w = [
            halves(grid, Weight(width, 3 * width), one, one_x, 0),
            halves(grid, Weight(width, width), one, one_x, 3 * width // 2),
        ]
        image_w = [
            halves(grid, Weight(width, 3 * width), one, one_x, 2 * width),
            halves(grid, Weight(width, width), one, one_x, 2 * width + 3 * width // 2),
        ]
        table1 = after(table, line2, line3)
    else:
        image_w = [gathered(w) for w in (img_qkv, img_out, img_in, img_proj, img_down)]
        text_w = [gathered(w) for w in (txt_qkv, txt_out, txt_in, txt_proj, txt_down)]
        table1 = table

    heads = tokens // (2 * HEAD) * (width // (2 * HEAD))
    qkv, probs, mixed, second = run(
        text_attention,
        [
            shape((tokens, 3 * width), BF16),
            shape((heads, 4 * HEAD, 2 * HEAD), F32),
            shape((tokens, width), BF16),
            shape((tokens, width), F32),
        ],
        [((tokens, width), BF16)],
        table1,
        [text_tokens, caption_col, caption_row, gains, shifts],
        text_w[:2],
        us=10,
    )
    table2 = table
    if regular:
        x2k, y2k, unused = lax.optimization_barrier((x2, y2, second))
        v2 = grid.corner(x2k, y2k)
        x3, y3 = grid.square(after(line3, x2k))
        ring2 = grid.shift(ring1, 0, 1)
        table2 = after(table, x2k, y2k, ring1)
    pairs = images // 2
    padded = pairs * GROUP_PAD
    x_image = jnp.pad(
        image_tokens.reshape(pairs, 2 * PATCHES, width), ((0, 0), (0, GROUP_PAD - 2 * PATCHES), (0, 0))
    ).reshape(padded, width)
    image_second = run(
        image_attention,
        [shape((padded, width), F32)],
        [((padded, width), BF16), ((padded, 3 * width), BF16), ((padded, width), BF16)],
        table2,
        [x_image, img_g, img_s],
        image_w[:2],
        us=19,
    )[0]
    table3 = table
    if regular:
        x3, y3, unused = lax.optimization_barrier((x3, y3, image_second))
        v3 = grid.corner(x3, y3)
        ring3 = grid.shift(ring2, 0, 1)
        table3 = after(table, x3, y3, ring2)
        two = grid.pieces(line2, x2, y2, *v2)
        two_x = grid.across(two)
        three = grid.pieces(line3, x3, y3, *v3)
        three_x = grid.across(three)
        img_d = grid.pieces(idl, idx, idy, *idv)
        txt_d = grid.pieces_z_last([td_square, ring1, ring2, ring3])
        image_w += [
            halves(grid, Weight(width, units), two, two_x, 0),
            halves(grid, Weight(width, width), two, two_x, units // 2),
            rows_of(grid, Weight(units, width), img_d, grid.across(img_d)),
        ]
        text_w += [
            halves(grid, Weight(width, units), three, three_x, 0),
            halves(grid, Weight(width, width), three, three_x, units // 2),
            rows_of(grid, Weight(units, width), txt_d, grid.across(txt_d)),
        ]
    pooled, pooled_second = run(
        image_inner,
        [shape((images, units), F32), shape((images, width), F32)],
        [((padded, width), BF16)],
        table3,
        [image_second, img_g, img_s, img_b],
        image_w[2:3],
        us=13,
    )
    hidden, slope, hidden_sum = run(
        text_inner,
        [shape((tokens, units), BF16), shape((tokens, units), F32), shape((captions, units), BF16)],
        [((tokens, width), BF16)],
        table,
        [second, caption_row, gains, shifts, biases],
        text_w[2:3],
        us=7,
    )
    image_emb = run(
        image_embed,
        [shape((images, width), BF16)],
        [],
        table,
        [pooled, pooled_second, img_b],
        [image_w[4], image_w[3]],
        us=5,
    )[0]
    image_emb = image_emb.reshape(2, pairs, width).transpose(1, 0, 2).reshape(images, width)
    image_emb = to_all(image_emb, devices).reshape(-1, width)
    hidden_sum = lax.all_to_all(hidden_sum, "blk", split_axis=1, concat_axis=0, tiled=True)
    text_out, pool_low = run(
        text_outer,
        [shape((tokens, width), BF16), shape((captions, width), BF16)],
        [],
        table,
        [second, hidden, caption_row, biases],
        text_w[4:5],
        us=5,
    )
    w_proj = run(copy_weight, [shape((width, width), BF16)], [], table, [], text_w[3:4])[0]

    pool_all = to_all(pool_low, devices).reshape(-1, width)
    total = pool_all.shape[0]
    col_max = jnp.full((total,), -1e30, F32)
    col_sum = jnp.zeros((total,), F32)
    held = []
    for start in range(0, total, TILE):
        proj = matmul(pool_all[start : start + TILE], w_proj)
        unit, factor = unit_rows(proj)
        sim = scale * dot_nt(unit.astype(BF16), image_emb)
        top = jnp.max(sim, axis=1)
        row_lse = top + jnp.log(jnp.sum(jnp.exp(sim - top[:, None]), axis=1))
        new_max = jnp.maximum(col_max, jnp.max(sim, axis=0))
        col_sum = col_sum * jnp.exp(col_max - new_max) + jnp.sum(jnp.exp(sim - new_max[None, :]), axis=0)
        col_max = new_max
        held.append((proj, factor, row_lse, sim))
    col_lse = col_max + jnp.log(col_sum)
    d_proj = []
    losses = []
    for start, (proj, factor, row_lse, sim) in zip(range(0, total, TILE), held):
        grad, loss = head_tile(
            proj, factor, image_emb, scale, row_lse, col_lse, every_pair[start : start + TILE], sim
        )
        d_proj.append(grad)
        losses.append(loss)
    d_proj = jnp.concatenate(d_proj)
    pair_loss = lax.dynamic_slice_in_dim(jnp.concatenate(losses), device * captions, captions)
    grad_proj = dot_tn(lax.dynamic_slice_in_dim(pool_all, device * own, own, axis=1), d_proj)
    d_each = dot_nt(d_proj, w_proj) / every_count[:, None]
    grad_down = dot_tn(hidden_sum, d_each.astype(BF16))
    d_mine = lax.dynamic_slice_in_dim(d_each, device * captions, captions)

    half = width // 2
    mine_in, theirs_in, d_second, d_mixed, sums_in, sums_out = run(
        functools.partial(back_inner, devices),
        [
            shape((half, units), BF16),
            shape((half, units), BF16),
            shape((tokens, width), F32),
            shape((tokens, width), BF16),
            shape((1, units), F32),
            shape((8, width), F32),
        ],
        [
            ((half, tokens), BF16),
            ((half, tokens), BF16),
            ((3 * captions, units), BF16),
            ((tokens, width), F32),
        ],
        table,
        [d_mine, caption_col, second, slope, gains, shifts],
        [text_w[4], text_w[2], text_w[1]],
        us=18,
        passes_table=True,
    )
    mine_qkv, theirs_qkv, text_grad, sums_qkv = run(
        functools.partial(back_attention, devices),
        [
            shape((half, 4 * width), BF16),
            shape((half, 4 * width), BF16),
            shape((tokens, width), F32),
            shape((8, width), F32),
        ],
        [((tokens, 3 * width), BF16)] + [((half, tokens), BF16)] * 4 + [((tokens, width), F32)],
        table,
        [text_tokens, d_second, d_mixed, qkv, probs, mixed, gains, shifts],
        text_w[:1],
        us=14,
        passes_table=True,
    )
    grad_in = reduce_grads(grid, mine_in, theirs_in, width)
    grad_qkv = reduce_grads(grid, mine_qkv, theirs_qkv, width)
    sums = jnp.concatenate(
        [
            jnp.concatenate([sums_qkv[0], sums_out[1]]).reshape(devices, -1),
            jnp.concatenate([sums_qkv[1], sums_out[2]]).reshape(devices, -1),
            jnp.concatenate([sums_in[0], sums_out[0]]).reshape(devices, -1),
        ],
        axis=1,
    )
    sums = jnp.sum(lax.all_to_all(sums, "blk", 0, 0, tiled=True), axis=0)
    return (
        pair_loss,
        text_out,
        text_grad,
        sums[: vec[0]],
        sums[vec[0] : vec[0] + vec[1]],
        grad_qkv[:, : 3 * width],
        grad_qkv[:, 3 * width :],
        grad_in,
        grad_down,
        sums[vec[0] + vec[1] :],
        grad_proj,
    )


def copy_weight(weight, out):
    out[...] = weight()[...]


def axis_sizes(mesh):
    devices = list(mesh.devices.flat)
    places = [(*d.coords, d.core_on_chip) for d in devices]
    sizes = []
    stride = len(devices)
    left = [0, 1, 2, 3]
    while stride > 1 and left:
        for axis in left:
            size = 1 + max(p[axis] for p in places) - min(p[axis] for p in places)
            step = stride // size
            if size > 1 and all(
                p[axis] - places[0][axis] == (i // step) % size for i, p in enumerate(places)
            ):
                sizes.append(size)
                left.remove(axis)
                stride = step
                break
        else:
            return [len(devices)]
    return sizes


def solution(mesh):
    grid = Grid(mesh.shape["blk"], axis_sizes(mesh))
    row = P("blk", None)
    flat = P("blk")
    tower = (flat, flat, row, row, row, row, flat, row)

    def body(*args):
        return on_device(grid, *args)

    return jax.shard_map(
        body,
        mesh=mesh,
        in_specs=(row, row, flat, row, P()) + tower + tower,
        out_specs=(flat, row, row, flat, flat, row, row, row, row, flat, row),
        check_vma=False,
    )
```

```python
import functools

import jax
import jax.numpy as jnp
from jax import lax
from jax.experimental import pallas as pl
from jax.experimental.pallas import tpu as pltpu
from jax.sharding import PartitionSpec as P

HEAD = 64
PATCHES = 50
CAPS = 4
TILE = 512
GROUP_PAD = 112

F32 = jnp.float32
BF16 = jnp.bfloat16


def gelu(z):
    return 0.5 * z * (1.0 + jnp.tanh(0.7978845608028654 * (z + 0.044715 * z * z * z)))


def normalize(x):
    mean = jnp.mean(x, axis=-1, keepdims=True)
    cent = x - mean
    rstd = lax.rsqrt(jnp.mean(cent * cent, axis=-1, keepdims=True) + 1e-06)
    return (cent * rstd, rstd)


def norm_back(grad, normed, rstd):
    return rstd * (
        grad
        - jnp.mean(grad, axis=-1, keepdims=True)
        - normed * jnp.mean(grad * normed, axis=-1, keepdims=True)
    )


def unit_rows(proj):
    factor = lax.rsqrt(jnp.sum(proj * proj, axis=-1, keepdims=True) + 1e-06)
    return (proj * factor, factor)


def matmul(left, right):
    return jnp.dot(left, right, preferred_element_type=F32)


def dot_nt(left, right):
    return lax.dot_general(left, right, (((1,), (1,)), ((), ())), preferred_element_type=F32)


def dot_tn(left, right):
    return lax.dot_general(left, right, (((0,), (0,)), ((), ())), preferred_element_type=F32)


def chunks(total, size, unroll=True):
    def wrap(body):
        @pl.loop(0, total // size, unroll=unroll)
        def step(j):
            body(pl.ds(pl.multiple_of(j * size, size), size))

    return wrap


def thirds(value):
    high = value.astype(BF16)
    rest = value - high.astype(F32)
    mid = rest.astype(BF16)
    return high, mid, (rest - mid.astype(F32)).astype(BF16)


def norm_rows(x, gain, shift):
    normed, rstd = normalize(x)
    return (normed * gain + shift).astype(BF16)


def head_masks(dtype, value):
    lane = lax.broadcasted_iota(jnp.int32, (1, 2 * HEAD), 1)
    first = jnp.where(lane < HEAD, value, 0.0).astype(dtype)
    second = jnp.where(lane < HEAD, 0.0, value).astype(dtype)
    return first, second


def both_heads(block, masks):
    return jnp.concatenate([block * masks[0], block * masks[1]], axis=0)


def merge_heads(stacked):
    half = stacked.shape[0] // 2
    lane = lax.broadcasted_iota(jnp.int32, (1, 2 * HEAD), 1)
    return jnp.where(lane < HEAD, stacked[:half], stacked[half:])


def softmax_unit(query, keys, mask, masks):
    scores = dot_nt(both_heads(query, masks), keys)
    scores = jnp.where(mask, scores, -1000000000.0)
    top = jnp.max(scores, axis=-1, keepdims=True)
    expo = jnp.exp(scores - top)
    return expo * (1.0 / jnp.sum(expo, axis=-1, keepdims=True))


def image_attention(x, gains, shifts, w_qkv, w_out, second, act, qkv, mixed):
    rows, width = x.shape
    group = GROUP_PAD

    @chunks(rows, group)
    def _(at):
        act[at, :] = norm_rows(x[at, :].astype(F32), gains[0:1, :], shifts[0:1, :])

    w_qkv = w_qkv()

    @chunks(3 * width, 256)
    def _(at):
        qkv[:, at] = matmul(act[...], w_qkv[:, at]).astype(BF16)

    masks = head_masks(BF16, 0.125)
    own = lax.broadcasted_iota(jnp.int32, (2 * group, group), 0)
    own = jnp.where(own >= group, own - group, own)
    other = lax.broadcasted_iota(jnp.int32, (2 * group, group), 1)
    mask = picture(own) == picture(other)

    @chunks(rows, group, 2)
    def _(at):
        for start in range(0, width, 2 * HEAD):
            cols = slice(start, start + 2 * HEAD)
            keys = qkv[at, width + start : width + start + 2 * HEAD]
            values = qkv[at, 2 * width + start : 2 * width + start + 2 * HEAD]
            probs = softmax_unit(qkv[at, cols], keys, mask, masks)
            mixed[at, cols] = merge_heads(matmul(probs.astype(BF16), values)).astype(BF16)

    w_out = w_out()

    @chunks(width, 256)
    def _(at):
        second[:, at] = x[:, at].astype(F32) + matmul(mixed[...], w_out[:, at])


def picture(place):
    return jnp.where(place >= PATCHES, 1, 0) + jnp.where(place >= 2 * PATCHES, 1, 0)


def image_pool(value):
    value = value.reshape(-1, GROUP_PAD, value.shape[1])
    which = picture(lax.broadcasted_iota(jnp.int32, (1, GROUP_PAD, 1), 1))
    parts = [jnp.sum(jnp.where(which == kind, value, 0.0), axis=1) for kind in range(2)]
    return jnp.concatenate(parts, axis=0) * (1.0 / PATCHES)


def image_inner(second, gains, shifts, biases, w_in, pooled, pooled_second, act):
    rows, width = second.shape
    units = pooled.shape[1]

    @chunks(rows, GROUP_PAD)
    def _(at):
        act[at, :] = norm_rows(second[at, :], gains[1:2, :], shifts[1:2, :])

    for start in range(0, width, 256):
        pooled_second[:, start : start + 256] = image_pool(second[:, start : start + 256])
    w_in = w_in()

    @chunks(units, 256)
    def _(at):
        hidden = gelu(matmul(act[...], w_in[:, at]) + biases[:, at]).astype(BF16).astype(F32)
        pooled[:, at] = image_pool(hidden)


def image_embed(pooled, pooled_second, biases, w_down, w_proj, emb):
    images, units = pooled.shape
    high, mid, unused = thirds(pooled[...])
    w_down = w_down()
    y = matmul(jnp.concatenate([high, mid], axis=0), w_down[...])
    y = y[:images] + y[images:] + pooled_second[...] + biases[:, units:]
    unit = unit_rows(matmul(y.astype(BF16), w_proj()[...]))[0].astype(BF16)
    to = lax.broadcasted_iota(jnp.int32, (images, images), 0)
    source = lax.broadcasted_iota(jnp.int32, (images, images), 1)
    half = images // 2
    order = (jnp.where(source >= half, 2 * (source - half) + 1, 2 * source) == to).astype(BF16)
    emb[...] = matmul(order, unit).astype(BF16)


def text_attention(x, caption_col, caption_row, gains, shifts, w_qkv, w_out, qkv, probs, mixed, second, act):
    rows, width = x.shape
    group = 2 * HEAD
    act[...] = norm_rows(x[...].astype(F32), gains[0:1, :], shifts[0:1, :])
    w_qkv = w_qkv()

    @chunks(3 * width, 256)
    def _(at):
        qkv[:, at] = matmul(act[...], w_qkv[:, at]).astype(BF16)

    masks = head_masks(BF16, 0.125)
    unit = 0
    for top in range(0, rows, group):
        at = slice(top, top + group)
        same = caption_col[at, :] == caption_row[:, at]
        mask = jnp.concatenate([same, same], axis=0)
        for start in range(0, width, 2 * HEAD):
            cols = slice(start, start + 2 * HEAD)
            keys = qkv[at, width + start : width + start + 2 * HEAD]
            values = qkv[at, 2 * width + start : 2 * width + start + 2 * HEAD]
            prob = softmax_unit(qkv[at, cols], keys, mask, masks)
            probs[unit] = prob
            unit += 1
            mixed[at, cols] = merge_heads(matmul(prob.astype(BF16), values)).astype(BF16)

    w_out = w_out()

    @chunks(width, 256)
    def _(at):
        second[:, at] = x[:, at].astype(F32) + matmul(mixed[...], w_out[:, at])


def caption_member(caption_row, captions):
    index = lax.broadcasted_iota(jnp.int32, (captions, caption_row.shape[1]), 0)
    return (index == caption_row[...]).astype(F32)


def text_inner(second, caption_row, gains, shifts, biases, w_in, hidden, slope, hidden_sum, act):
    units = hidden.shape[1]
    act[...] = norm_rows(second[...], gains[1:2, :], shifts[1:2, :])
    low = caption_member(caption_row, hidden_sum.shape[0]).astype(BF16)
    w_in = w_in()

    @chunks(units, 256)
    def _(at):
        z = matmul(act[...], w_in[:, at]) + biases[:, at]
        inside = jnp.tanh(0.7978845608028654 * (z + 0.044715 * z * z * z))
        value = (0.5 * z * (1.0 + inside)).astype(BF16)
        hidden[:, at] = value
        slope[:, at] = 0.5 * (1.0 + inside) + 0.5 * z * (1.0 - inside * inside) * (
            0.7978845608028654 * (1.0 + 3.0 * 0.044715 * z * z)
        )
        hidden_sum[:, at] = matmul(low, value).astype(BF16)


def text_outer(second, hidden, caption_row, biases, w_down, out, pool_low):
    width = second.shape[1]
    units = hidden.shape[1]
    member = caption_member(caption_row, pool_low.shape[0])
    low = member.astype(BF16)
    count = jnp.sum(member, axis=1, keepdims=True)
    w_down = w_down()

    @chunks(width, 256)
    def _(at):
        outer = biases[:, pl.ds(pl.multiple_of(units + at.start, 256), 256)]
        y = second[:, at] + matmul(hidden[...], w_down[:, at]) + outer
        out[:, at] = y.astype(BF16)
        total = sum(matmul(low, part) for part in thirds(y))
        pool_low[:, at] = (total / count).astype(BF16)


def head_kernel(
    table, scale_ref, pool_all, image_emb, pair_col, count, hidden_sum, pool_cols, w_proj,
    loss, d_mine, grad_proj, grad_down,
):
    scale = scale_ref[0]
    captions = d_mine.shape[0]
    w_proj = w_proj()
    proj = matmul(pool_all[...], w_proj[...])
    unit, factor = unit_rows(proj)
    sim = scale * dot_nt(unit.astype(BF16), image_emb[...])
    row_max = jnp.max(sim, axis=1, keepdims=True)
    row_lse = row_max + jnp.log(jnp.sum(jnp.exp(sim - row_max), axis=1, keepdims=True))
    col_max = jnp.max(sim, axis=0, keepdims=True)
    col_lse = col_max + jnp.log(jnp.sum(jnp.exp(sim - col_max), axis=0, keepdims=True))
    hit = pair_col[...] == lax.broadcasted_iota(jnp.int32, sim.shape, 1)
    both = 0.5 * jnp.exp(sim - row_lse) + 0.5 * jnp.exp(sim - col_lse)
    weights_sim = jnp.where(hit, both - 1.0, both).astype(BF16)
    pos = jnp.sum(jnp.where(hit, sim, 0.0), axis=1, keepdims=True)
    pair_lse = jnp.sum(jnp.where(hit, col_lse, 0.0), axis=1, keepdims=True)
    loss[...] = 0.5 * (row_lse - pos) + 0.5 * (pair_lse - pos)
    d_emb = scale * matmul(weights_sim, image_emb[...])
    inside = jnp.sum(d_emb * proj, axis=-1, keepdims=True)
    d_proj = (factor * d_emb - proj * (factor * factor * factor * inside)).astype(BF16)
    grad_proj[...] = dot_tn(pool_cols[...], d_proj)
    d_each = dot_nt(d_proj, w_proj[...]) / count[...]
    d_low = d_each.astype(BF16)
    grad_down[...] = dot_tn(hidden_sum[...], d_low)
    first = table[PLACE] * captions
    index = lax.broadcasted_iota(jnp.int32, (captions, d_each.shape[0]), 1)
    pick = (index == first + lax.broadcasted_iota(jnp.int32, (captions, d_each.shape[0]), 0)).astype(BF16)
    d_mine[...] = sum(matmul(pick, part) for part in thirds(d_each))


def pack_sums(sums_qkv, sums_out, sums_in, out):
    devices, width = out.shape[0], sums_out.shape[1]
    first, second = sums_qkv[...], sums_out[...]
    vectors = [
        jnp.concatenate([first[0:1], second[1:2]], axis=1),
        jnp.concatenate([first[1:2], second[2:3]], axis=1),
        jnp.concatenate([sums_in[...], second[0:1]], axis=1),
    ]
    for i, vector in enumerate(vectors):
        total = vector.shape[1]
        share = total // devices
        row = lax.broadcasted_iota(jnp.int32, (devices, total), 0)
        place = lax.broadcasted_iota(jnp.int32, (devices, total), 1) - row * share
        mine = jnp.where(place >= 0, jnp.where(place < share, vector, 0.0), 0.0)
        to = lax.broadcasted_iota(jnp.int32, (total, 128), 1)
        source = lax.broadcasted_iota(jnp.int32, (total, 128), 0)
        pick = (lax.rem(source, share) == to).astype(BF16)
        out[:, i * 128 : (i + 1) * 128] = sum(matmul(part, pick) for part in thirds(mine))


def core_split(table, value, devices, mine, theirs):
    own = value.shape[0] // devices
    value = value.reshape(devices // 2, 2, own, value.shape[1])
    first = table[CORE] == 0
    even = value[:, 0].reshape(-1, value.shape[3])
    odd = value[:, 1].reshape(-1, value.shape[3])
    mine[...] = jnp.where(first, even, odd).astype(BF16)
    theirs[...] = jnp.where(first, odd, even).astype(BF16)


def token_member(caption_col, captions):
    index = lax.broadcasted_iota(jnp.int32, (caption_col.shape[0], 3 * captions), 1)
    index = jnp.where(index >= captions, index - captions, index)
    index = jnp.where(index >= captions, index - captions, index)
    return (caption_col[...] == index).astype(BF16)


def back_inner(
    devices, table, each, caption_col, second, slope, gains, shifts, w_down,
    mine, theirs, d_inner, sums, act_t, act_u, both,
):
    rows, width = second.shape
    units = slope.shape[1]
    captions = each.shape[0]
    member = token_member(caption_col, captions)
    normed, rstd = normalize(second[...])
    act = normed * gains[1:2, :] + shifts[1:2, :]
    core_split(table, act.T, devices, act_t, act_u)
    each_low = each[...].astype(BF16)
    w_down = w_down()

    @chunks(units, 256)
    def _(at):
        both[:, at] = jnp.concatenate(thirds(dot_nt(each_low, w_down[at, :])), axis=0)

    @chunks(units, 256)
    def _(at):
        low = (matmul(member, both[:, at]) * slope[:, at]).astype(BF16)
        d_inner[:, at] = low
        sums[:, at] = jnp.sum(low.astype(F32), axis=0, keepdims=True)
        theirs[:, at] = matmul(act_u[...], low).astype(BF16)
        mine[:, at] = matmul(act_t[...], low).astype(BF16)


def back_second(each, d_inner, caption_col, second, gains, w_in, w_out, d_second, d_mixed, sums, d_act):
    width = second.shape[1]
    normed, rstd = normalize(second[...])
    d_y = matmul(token_member(caption_col, each.shape[0]), jnp.concatenate(thirds(each[...]), axis=0))
    sums[0:1, :] = jnp.sum(d_y, axis=0, keepdims=True)
    w_in = w_in()

    @chunks(width, 256)
    def _(at):
        d_act[:, at] = dot_nt(d_inner[...], w_in[at, :])

    grad = d_act[...]
    sums[1:2, :] = jnp.sum(grad * normed, axis=0, keepdims=True)
    sums[2:3, :] = jnp.sum(grad, axis=0, keepdims=True)
    d_two = d_y + norm_back(grad * gains[1:2, :], normed, rstd)
    d_second[...] = d_two
    d_mixed[...] = dot_nt(d_two.astype(BF16), w_out()[...]).astype(BF16)


def back_attention(d_mixed, qkv, probs, d_qkv):
    rows, width = d_mixed.shape
    group = 2 * HEAD
    ones = head_masks(BF16, 1.0)
    masks = head_masks(BF16, 0.125)
    unit = 0
    for top in range(0, rows, group):
        at = slice(top, top + group)
        for start in range(0, width, 2 * HEAD):
            cols = slice(start, start + 2 * HEAD)
            key_cols = slice(width + start, width + start + 2 * HEAD)
            value_cols = slice(2 * width + start, 2 * width + start + 2 * HEAD)
            prob = probs[unit]
            unit += 1
            d_out = both_heads(d_mixed[at, cols], ones)
            query = both_heads(qkv[at, cols], masks)
            d_qkv[at, value_cols] = dot_tn(prob.astype(BF16), d_out).astype(BF16)
            d_prob = dot_nt(d_out, qkv[at, value_cols])
            d_score = (prob * (d_prob - jnp.sum(prob * d_prob, axis=-1, keepdims=True))).astype(BF16)
            d_qkv[at, cols] = (0.125 * merge_heads(matmul(d_score, qkv[at, key_cols]))).astype(BF16)
            d_qkv[at, key_cols] = dot_tn(d_score, query).astype(BF16)


def back_weights(
    devices, table, x, d_second, d_qkv, mixed, gains, shifts,
    mine, theirs, act_t, act_u, mixed_t, mixed_u,
):
    width = x.shape[1]
    core_split(table, norm_rows(x[...].astype(F32), gains[0:1, :], shifts[0:1, :]).astype(F32).T, devices, act_t, act_u)
    core_split(table, mixed[...].astype(F32).T, devices, mixed_t, mixed_u)
    d_low = d_second[...].astype(BF16)
    for start in range(0, width, 256):
        at = slice(start, start + 256)
        to = slice(3 * width + start, 3 * width + start + 256)
        theirs[:, to] = matmul(mixed_u[...], d_low[:, at]).astype(BF16)
        mine[:, to] = matmul(mixed_t[...], d_low[:, at]).astype(BF16)

    @chunks(3 * width, 256)
    def _(at):
        theirs[:, at] = matmul(act_u[...], d_qkv[:, at]).astype(BF16)
        mine[:, at] = matmul(act_t[...], d_qkv[:, at]).astype(BF16)


def back_outer(x, d_second, d_qkv, gains, w_qkv, text_grad, sums, d_act):
    width = x.shape[1]
    normed, rstd = normalize(x[...].astype(F32))
    w_qkv = w_qkv()

    @chunks(width, 256)
    def _(at):
        d_act[:, at] = dot_nt(d_qkv[...], w_qkv[at, :])

    grad = d_act[...]
    sums[0:1, :] = jnp.sum(grad * normed, axis=0, keepdims=True)
    sums[1:2, :] = jnp.sum(grad, axis=0, keepdims=True)
    text_grad[...] = d_second[...] + norm_back(grad * gains[0:1, :], normed, rstd)


class Weight:
    def __init__(self, rows, cols):
        self.dims = (rows, cols)
        self.parts = []

    def add(self, array, lead, start, width, row=None, unit=0, below=0, col=None, beside=0):
        self.parts.append((array, lead, start, width, row, unit, below, col, beside))


def run(kernel, outs, scratch, table, operands, weights, us=5, passes_table=False, scalars=()):
    arrays = []
    for weight in weights:
        for part in weight.parts:
            if not any(part[0] is a for a in arrays):
                arrays.append(part[0])
    places = {id(a): i for i, a in enumerate(arrays)}
    n_s, n_op, n_arr, n_out, n_w = len(scalars), len(operands), len(arrays), len(outs), len(weights)

    def body(*refs):
        table_ref, refs = refs[0], refs[1:]
        ops, refs = refs[: n_s + n_op], refs[n_s + n_op :]
        arrs, refs = refs[:n_arr], refs[n_arr:]
        out, refs = refs[:n_out], refs[n_out:]
        held, refs = refs[:n_w], refs[n_w:]
        if n_w:
            sems, refs = refs[0], refs[1:]
        waits = []
        for i, weight in enumerate(weights):
            for array, lead, start, width, row, unit, below, col, beside in weight.parts:
                at = 0 if row is None else pl.multiple_of(table_ref[row] * unit + below, 16)
                to = beside
                if col is not None:
                    to = pl.multiple_of(table_ref[col] * (weight.dims[1] // 2) + beside, 128)
                pltpu.make_async_copy(
                    arrs[places[id(array)]].at[lead, :, pl.ds(start, width)],
                    held[i].at[pl.ds(at, array.shape[1]), pl.ds(to, width)],
                    sems.at[i],
                ).start()

            def wait(i=i):
                pltpu.make_async_copy(held[i], held[i], sems.at[i]).wait()
                return held[i]

            waits.append(wait)
        if passes_table:
            ops = (table_ref, *ops)
        kernel(*ops, *waits, *out, *refs)

    vmem = pl.BlockSpec(memory_space=pltpu.VMEM)
    return pl.pallas_call(
        body,
        out_shape=outs,
        in_specs=[pl.BlockSpec(memory_space=pltpu.SMEM)] * (1 + n_s) + [vmem] * n_op + [pl.BlockSpec(memory_space=pltpu.HBM)] * n_arr,
        out_specs=[vmem] * n_out,
        scratch_shapes=[pltpu.VMEM(w.dims, BF16) for w in weights]
        + ([pltpu.SemaphoreType.DMA((n_w,))] if n_w else [])
        + [pltpu.VMEM(*s) for s in scratch],
        compiler_params=pltpu.CompilerParams(vmem_limit_bytes=60 << 20),
        cost_estimate=pl.CostEstimate(flops=us * 2000000000, bytes_accessed=1000, transcendentals=0),
    )(table, *scalars, *operands, *arrays)


def shape(dims, dtype):
    return jax.ShapeDtypeStruct(dims, dtype)


class Grid:
    def __init__(self, devices, sizes):
        self.devices = devices
        self.sizes = sizes
        strides = []
        step = devices
        for size in sizes:
            step //= size
            strides.append(step)
        self.strides = strides
        self.regular = len(sizes) == 4 and sizes[1:] == [2, 2, 2]

    def place(self):
        index = lax.axis_index("blk")
        return [(index // st) % size for size, st in zip(self.sizes, self.strides)]

    def shift(self, value, axis, step):
        size, stride = self.sizes[axis], self.strides[axis]
        pairs = []
        for i in range(self.devices):
            at = (i // stride) % size
            pairs.append((i, i + ((at + step) % size - at) * stride))
        return lax.ppermute(value, "blk", pairs)

    def table(self):
        if len(self.sizes) != 4:
            index = lax.axis_index("blk")
            return jnp.stack([index % 2, 1 - index % 2, index]).astype(jnp.int32)
        place = self.place()
        chips = []
        for offset in self.offsets():
            origin = [
                d[1] if isinstance(d, tuple) else (p - d) % s for p, d, s in zip(place, offset, self.sizes)
            ]
            chips.append(sum(o * st for o, st in zip(origin, self.strides)) // 2)
        chips = jnp.stack(chips)
        core = place[3]
        return jnp.concatenate(
            [jnp.stack([core, 1 - core, lax.axis_index("blk"), *place[:3]]), chips, 2 * chips + core, 2 * chips + 1 - core]
        ).astype(jnp.int32)

    def offsets(self):
        z, y, x, unused = self.sizes
        zs = list(range(z)) + [("z", i) for i in range(z)]
        return [(dz, dy, dx) for dz in zs for dy in range(y) for dx in range(x)]

    def row_of(self, offset, kind):
        count = len(self.offsets())
        return FIRST_ROW + self.offsets().index(offset) + {"chip": 0, "own": count, "other": 2 * count}[kind]

    def line(self, value):
        return [value] + [self.shift(value, 0, k) for k in range(1, self.sizes[0])]

    def square(self, line):
        return self.shift(line, 2, 1), self.shift(line, 1, 1)

    def along_z(self, value):
        depth = self.sizes[0]
        groups = [[i + k * self.strides[0] for k in range(depth)] for i in range(self.strides[0])]
        return lax.all_to_all(
            jnp.broadcast_to(value[None], (depth, *value.shape)), "blk", 0, 0, axis_index_groups=groups
        )

    def across(self, *arrays):
        return [self.shift(a, 3, 1) for a in arrays]

    def parts(self, value):
        return value.reshape(*self.sizes[:3], -1, value.shape[1])

    def reduce_start(self, table, mine, got):
        mine, got = self.parts(mine), self.parts(got)
        depth, unused, unused, rows, cols = mine.shape
        sent = shape((depth, 2, rows, cols // 2), BF16)
        held = [((depth, 2, rows, cols // 2), BF16)] * 4
        to_x, to_y = fetching(sum_cores, [sent, sent], held, table, [mine, got])
        return (mine, got), (self.shift(to_x, 2, 1), self.shift(to_y, 1, 1)), (to_x, to_y)

    def reduce_next(self, table, held, came):
        depth, unused, unused, rows, cols = held[0].shape
        sent = shape((depth, rows, cols // 2), BF16)
        scratch = [((depth, rows, cols // 2), BF16)] * 6
        to_y, to_x = fetching(sum_sides, [sent, sent], scratch, table, [*held, *came])
        return (*held, *came), (self.shift(to_y, 1, 1), self.shift(to_x, 2, 1)), (to_y, to_x)

    def reduce_line(self, table, held, came):
        depth, unused, unused, rows, cols = held[0].shape
        sent = shape((rows, cols), BF16)
        scratch = [((depth, rows, cols // 2), BF16)] * 8
        outs = [shape((rows, cols), F32)] + [sent] * (depth - 1)
        kept, *to = fetching(sum_corner, outs, scratch, table, [*held, *came])
        return kept, [self.shift(value, 0, k) for k, value in enumerate(to, 1)]

    def reduce_end(self, table, kept, came, widths):
        kernel = functools.partial(sum_line, len(came))
        return run(kernel, [shape((kept.shape[0], w), F32) for w in widths], [], table, [kept, *came], [], us=1)


def wide(*values):
    return sum(v.astype(F32) for v in values)


def fetching(kernel, outs, scratch, table, arrays):
    count, n_out = len(arrays), len(outs)

    def body(*refs):
        table_ref, refs = refs[0], refs[1:]
        arrs, out, held, sems = refs[:count], refs[count : count + n_out], refs[count + n_out : -1], refs[-1]
        steps = kernel(table_ref, *arrs, *out)
        copies = [pltpu.make_async_copy(s, h, sems.at[i]) for i, (s, h) in enumerate(zip(next(steps), held))]
        for copy in copies:
            copy.start()
        for copy in copies:
            copy.wait()
        steps.send(held)

    vmem = pl.BlockSpec(memory_space=pltpu.VMEM)
    return pl.pallas_call(
        body,
        out_shape=outs,
        in_specs=[pl.BlockSpec(memory_space=pltpu.SMEM)] + [pl.BlockSpec(memory_space=pltpu.HBM)] * count,
        out_specs=[vmem] * n_out,
        scratch_shapes=[pltpu.VMEM(*s) for s in scratch] + [pltpu.SemaphoreType.DMA((len(scratch),))],
        compiler_params=pltpu.CompilerParams(vmem_limit_bytes=60 << 20),
        cost_estimate=pl.CostEstimate(flops=1000, bytes_accessed=1000, transcendentals=0),
    )(table, *arrays)


def sum_cores(table, mine, got, to_x, to_y):
    half = to_x.shape[3]
    other_y, other_x = 1 - table[AT_Y], 1 - table[AT_X]
    left, right = pl.ds(0, half), pl.ds(half, half)
    held = yield [
        mine.at[:, :, other_x, :, left],
        got.at[:, :, other_x, :, left],
        mine.at[:, other_y, :, :, right],
        got.at[:, other_y, :, :, right],
    ]
    for z in range(mine.shape[0]):
        for i in range(2):
            to_x[z, i] = wide(held[0][z, i], held[1][z, i]).astype(BF16)
            to_y[z, i] = wide(held[2][z, i], held[3][z, i]).astype(BF16)
    yield


def sum_sides(table, mine, got, by_x, by_y, to_y, to_x):
    half = to_x.shape[2]
    y, x = table[AT_Y], table[AT_X]
    left, right = pl.ds(0, half), pl.ds(half, half)
    held = yield [
        mine.at[:, 1 - y, x, :, left],
        got.at[:, 1 - y, x, :, left],
        by_x.at[:, 1 - y],
        mine.at[:, y, 1 - x, :, right],
        got.at[:, y, 1 - x, :, right],
        by_y.at[:, 1 - x],
    ]
    for z in range(mine.shape[0]):
        to_y[z] = wide(*[h[z] for h in held[:3]]).astype(BF16)
        to_x[z] = wide(*[h[z] for h in held[3:]]).astype(BF16)
    yield


def sum_corner(table, mine, got, by_x, by_y, left_by_y, right_by_x, kept, *to):
    depth = mine.shape[0]
    half = by_x.shape[3]
    y, x = table[AT_Y], table[AT_X]
    left, right = pl.ds(0, half), pl.ds(half, half)
    held = yield [
        mine.at[:, y, x, :, left],
        got.at[:, y, x, :, left],
        by_x.at[:, y],
        left_by_y,
        mine.at[:, y, x, :, right],
        got.at[:, y, x, :, right],
        by_y.at[:, x],
        right_by_x,
    ]
    for k in range(depth):
        z = lax.rem(table[AT_Z] + k, depth)
        out = to[k - 1] if k else kept
        out[:, :half] = wide(*[h[z] for h in held[:4]]).astype(out.dtype)
        out[:, half:] = wide(*[h[z] for h in held[4:]]).astype(out.dtype)
    yield


def sum_line(spans, kept, *refs):
    came = refs[:spans]
    start = 0
    for out in refs[spans:]:
        cols = slice(start, start + out.shape[1])
        start += out.shape[1]
        out[...] = kept[:, cols] + wide(*[c[:, cols] for c in came])


class Chunk:
    def __init__(self, grid, line, cut, ordered):
        self.grid, self.line, self.cut = grid, line, cut
        self.cols = line.shape[2]
        self.zs = [("z", z) if ordered else z for z in range(grid.sizes[0])]
        self.own, self.other = [], []

    def hold(self, mine, theirs, dy, dx, start, low, high):
        offsets = [(z, dy, dx) for z in self.zs]
        for pieces, array in ((self.own, mine), (self.other, theirs)):
            pieces.append((array, offsets, start, low, high))

    def halves(self, rows, cols, start):
        weight = Weight(rows, cols)
        for pieces, col in ((self.own, CORE), (self.other, OTHER)):
            for array, offsets, begin, low, high in pieces:
                left, right = max(low, start), min(high, start + cols // 2)
                if left < right:
                    for lead, offset in enumerate(offsets):
                        row = self.grid.row_of(offset, "chip")
                        at = begin + left - low
                        weight.add(array, lead, at, right - left, row, array.shape[1], 0, col, left - start)
        return weight

    def deep(self, rows, cols):
        weight = Weight(rows, cols)
        parts = self.cols // cols
        for pieces, kind in ((self.own, "own"), (self.other, "other")):
            for array, offsets, begin, low, high in pieces:
                for part in range(parts):
                    left, right = max(low, part * cols), min(high, part * cols + cols)
                    if left < right:
                        for lead, offset in enumerate(offsets):
                            row = self.grid.row_of(offset, kind)
                            high_rows = array.shape[1]
                            at = begin + left - low
                            weight.add(
                                array, lead, at, right - left, row, parts * high_rows, part * high_rows,
                                None, left - part * cols,
                            )
        return weight


def tie(*values):
    return lax.optimization_barrier(values)


def after_all(values, *earlier):
    return lax.optimization_barrier((*values, *earlier))[: len(values)]


def after(value, *earlier):
    return lax.optimization_barrier((value, *earlier))[0]


CORE = 0
OTHER = 1
PLACE = 2
AT_Z, AT_Y, AT_X = 3, 4, 5
FIRST_ROW = 6


def to_all(value, devices):
    return lax.all_to_all(jnp.broadcast_to(value[None], (devices, *value.shape)), "blk", 0, 0)


def pack_kernel(table, *refs):
    first = table[CORE] == 0
    keep, send = refs[-2:]
    start = 0
    for weight in refs[:-2]:
        half = weight.shape[1] // 2
        left, right = weight[:, :half], weight[:, half:]
        keep[:, start : start + half] = jnp.where(first, left, right)
        send[:, start : start + half] = jnp.where(first, right, left)
        start += half


def vector_pack_kernel(caption_row, pair_index, *refs):
    block, refs = refs[-1], refs[:-1]
    captions = pair_index.shape[1]
    pairs = pair_index[...].astype(F32)
    high = jnp.floor(pairs * (1.0 / 64.0))
    member = caption_member(caption_row, captions).astype(BF16)
    count = dot_nt(jnp.ones((8, caption_row.shape[1]), BF16), member)[0:1]
    rows = [r[...].astype(F32) for r in refs] + [high, pairs - 64.0 * high, count]
    rows = [jnp.concatenate([r, jnp.zeros((1, 128 - r.shape[1]), F32)], axis=1) for r in rows]
    rows.append(jnp.zeros((block.shape[0] - len(rows), 128), F32))
    block[...] = jnp.concatenate(rows, axis=0).astype(BF16)


def pair_kernel(table, keep, got, *outs):
    first = table[CORE] == 0
    start = 0
    for out in outs:
        cols = slice(start, start + out.shape[1])
        start += out.shape[1]
        one, two = keep[:, cols].astype(F32), got[:, cols].astype(F32)
        out[...] = jnp.concatenate([jnp.where(first, one, two), jnp.where(first, two, one)], axis=0).astype(BF16)


def pair_up(grid, table, groups):
    rows = groups[0][0].shape[0]
    widths = [sum(w.shape[1] for w in group) // 2 for group in groups]
    packed = shape((rows, sum(widths)), BF16)
    keep, send = run(
        pack_kernel, [packed, packed], [], table, [w for group in groups for w in group], [], us=1, passes_table=True
    )
    return run(
        pair_kernel,
        [shape((2 * rows, w), BF16) for w in widths],
        [],
        table,
        [keep, grid.shift(send, 3, 1)],
        [],
        us=1,
        passes_table=True,
    )


def copied(arrays, outs, moves):
    count = len(arrays)

    def kernel(*refs):
        sems = refs[-1]
        copies = [
            pltpu.make_async_copy(refs[a].at[source], refs[count + o].at[to], sems.at[i])
            for i, (a, source, o, to) in enumerate(moves)
        ]
        for copy in copies:
            copy.start()
        for copy in copies:
            copy.wait()

    anywhere = pl.BlockSpec(memory_space=pltpu.HBM)
    return pl.pallas_call(
        kernel,
        out_shape=outs,
        in_specs=[anywhere] * count,
        out_specs=[pl.BlockSpec(memory_space=pltpu.VMEM)] * len(outs),
        scratch_shapes=[pltpu.SemaphoreType.DMA((len(moves),))],
        cost_estimate=pl.CostEstimate(flops=1000, bytes_accessed=1000, transcendentals=0),
    )(*arrays)


def columns(start, stop):
    return (slice(None), slice(None), pl.ds(start, stop - start))


def side_operands(last, parts):
    chunk, by_x, by_y = last
    cut, end = chunk.cut, chunk.cols
    if parts is None:
        depth, rows = by_x.shape[:2]
        outs = [shape((depth, rows, end - cut), BF16), shape((depth, rows, cut), BF16)]
        moves = [(0, columns(cut, end), 0, columns(0, end - cut)), (1, columns(0, cut), 1, columns(0, cut))]
        return copied([by_y, by_x], outs, moves)
    line = None
    if len(parts) == 1:
        line = parts[0]
        depth, rows, cols = line.shape
        parts = [(0, columns(0, cols), columns(0, cols))]
        arrays = [line]
        outs = []
    else:
        arrays = list(parts)
        depth, (rows, cols) = len(parts), parts[0].shape
        outs = [shape((depth, rows, cols), BF16)]
        parts = [(i, (slice(None), slice(None)), (i, slice(None), pl.ds(0, cols))) for i in range(depth)]
    outs += [shape((depth, rows, cols + end - cut), BF16), shape((depth, rows, cols + cut), BF16)]
    count = len(arrays)
    moves = []
    for o in range(len(outs)):
        moves += [(a, source, o, to) for a, source, to in parts]
    moves.append((count, columns(cut, end), len(outs) - 2, columns(cols, cols + end - cut)))
    moves.append((count + 1, columns(0, cut), len(outs) - 1, columns(cols, cols + cut)))
    out = copied([*arrays, by_y, by_x], outs, moves)
    return out if line is None else [line, *out]


def beside(value):
    half = value.shape[0] // 2
    return jnp.concatenate([value[:half], value[half:]], axis=1)


def settle(chunk, last, mine, theirs):
    by_x, by_y = mine
    start = 0
    if chunk is not None:
        start = chunk.cols
        chunk.hold(by_x, theirs[0], 0, 1, 0, 0, chunk.cols)
        chunk.hold(by_y, theirs[1], 1, 0, 0, 0, chunk.cols)
    if last is not None:
        last.hold(by_x, theirs[0], 1, 1, start, last.cut, last.cols)
        last.hold(by_y, theirs[1], 1, 1, start, 0, last.cut)


def columns_of(whole, widths):
    weights = []
    start = 0
    array = whole[None]
    for width in widths:
        weight = Weight(whole.shape[0], width)
        weight.add(array, 0, start, width)
        weights.append(weight)
        start += width
    return weights


def gathered(part):
    full = lax.all_gather(part, "blk", axis=0, tiled=True)
    weight = Weight(*full.shape)
    weight.add(full[None], 0, 0, full.shape[1])
    return weight


def reduce_grads(grid, mine, theirs, width):
    own = width // grid.devices
    both = jnp.where(lax.axis_index("blk") % 2 == 0, jnp.stack([mine, theirs], 0), jnp.stack([theirs, mine], 0))
    both = both.reshape(2, grid.devices // 2, own, -1).transpose(1, 0, 2, 3).reshape(width, -1)
    return lax.psum_scatter(both, "blk", scatter_dimension=0, tiled=True).astype(F32)


def head_tile(proj, factor, image_emb, scale, row_lse, col_lse, pairs, sim):
    hit = pairs[:, None] == jnp.arange(image_emb.shape[0], dtype=jnp.int32)[None, :]
    weights_sim = (
        0.5 * jnp.exp(sim - row_lse[:, None]) + 0.5 * jnp.exp(sim - col_lse[None, :]) - hit.astype(F32)
    )
    d_emb = scale * matmul(weights_sim.astype(BF16), image_emb)
    d_proj = factor * d_emb - proj * (factor * factor * factor) * jnp.sum(d_emb * proj, axis=-1, keepdims=True)
    pos = jnp.sum(jnp.where(hit, sim, 0.0), axis=1)
    pair_col = jnp.sum(jnp.where(hit, col_lse[None, :], 0.0), axis=1)
    return (d_proj.astype(BF16), 0.5 * (row_lse - pos) + 0.5 * (pair_col - pos))


def head_tiled(total, captions, own, scale, pool_all, image_emb, every_pair, every_count, hidden_sum, w_proj):
    device = lax.axis_index("blk")
    col_max = jnp.full((total,), -1e30, F32)
    col_sum = jnp.zeros((total,), F32)
    held = []
    for start in range(0, total, TILE):
        proj = matmul(pool_all[start : start + TILE], w_proj)
        unit, factor = unit_rows(proj)
        sim = scale * dot_nt(unit.astype(BF16), image_emb)
        top = jnp.max(sim, axis=1)
        row_lse = top + jnp.log(jnp.sum(jnp.exp(sim - top[:, None]), axis=1))
        new_max = jnp.maximum(col_max, jnp.max(sim, axis=0))
        col_sum = col_sum * jnp.exp(col_max - new_max) + jnp.sum(jnp.exp(sim - new_max[None, :]), axis=0)
        col_max = new_max
        held.append((proj, factor, row_lse, sim))
    col_lse = col_max + jnp.log(col_sum)
    d_proj = []
    losses = []
    for start, (proj, factor, row_lse, sim) in zip(range(0, total, TILE), held):
        grad, loss = head_tile(
            proj, factor, image_emb, scale, row_lse, col_lse, every_pair[start : start + TILE], sim
        )
        d_proj.append(grad)
        losses.append(loss)
    d_proj = jnp.concatenate(d_proj)
    pair_loss = lax.dynamic_slice_in_dim(jnp.concatenate(losses), device * captions, captions)
    grad_proj = dot_tn(lax.dynamic_slice_in_dim(pool_all, device * own, own, axis=1), d_proj)
    d_each = dot_nt(d_proj, w_proj) / every_count[:, None]
    grad_down = dot_tn(hidden_sum, d_each.astype(BF16))
    d_mine = lax.dynamic_slice_in_dim(d_each, device * captions, captions)

    return pair_loss, d_mine, grad_proj, grad_down


def on_device(grid, *args):
    (
        text_tokens,
        segment_ids,
        pair_index,
        image_tokens,
        logit_scale,
        img_gains,
        img_shifts,
        img_qkv,
        img_out,
        img_in,
        img_down,
        img_biases,
        img_proj,
        txt_gains,
        txt_shifts,
        txt_qkv,
        txt_out,
        txt_in,
        txt_down,
        txt_biases,
        txt_proj,
    ) = args
    devices = grid.devices
    width = text_tokens.shape[1]
    units = img_in.shape[1]
    scale = logit_scale[0]
    rows, length = segment_ids.shape
    tokens = rows * length
    captions = pair_index.shape[0]
    images = image_tokens.shape[0] // PATCHES
    device = lax.axis_index("blk")
    own = width // devices
    table = grid.table()

    caption_of = (jnp.arange(rows, dtype=jnp.int32)[:, None] * CAPS + segment_ids).reshape(tokens)
    caption_col, caption_row = caption_of[:, None], caption_of[None, :]
    member = (jnp.arange(captions, dtype=jnp.int32)[:, None] == caption_row).astype(F32)

    vec = (img_gains.shape[0], img_shifts.shape[0], img_biases.shape[0])
    vectors = [img_gains, img_shifts, img_biases, txt_gains, txt_shifts, txt_biases]
    (block,) = run(
        vector_pack_kernel,
        [shape((16, 128), BF16)],
        [],
        table,
        [caption_row, pair_index[None], *[v[None] for v in vectors]],
        [],
        us=1,
    )
    block = to_all(block, devices)
    pairs = images // 2
    padded = pairs * GROUP_PAD
    x_image = jnp.pad(
        image_tokens.reshape(pairs, 2 * PATCHES, width), ((0, 0), (0, GROUP_PAD - 2 * PATCHES), (0, 0))
    ).reshape(padded, width)
    regular = grid.regular and own % 8 == 0
    text_parts = [txt_qkv, txt_out, txt_in, txt_proj]
    if regular:
        line0 = grid.line(beside(img_down))
        pair1, pair2 = pair_up(grid, table, [[img_qkv, img_out], [img_in, img_proj]])
        *line0, pair1, pair2 = tie(*line0, pair1, pair2)

        chunk0 = Chunk(grid, jnp.stack(line0), width, False)
        side0 = grid.square(chunk0.line)
        line1 = grid.line(pair1)
        *side0, line1[1], line1[2], line1[3], block = tie(*side0, *line1[1:], block)
        text_all = lax.all_gather(
            after(jnp.concatenate(text_parts, axis=1), line1[1]), "blk", axis=0, tiled=True
        )
        text_w = columns_of(text_all, [w.shape[1] for w in text_parts])

        line1, *to = side_operands((chunk0, *side0), line1)
        chunk1 = Chunk(grid, line1, width, False)
        side1 = grid.shift(to[0], 2, 1), grid.shift(to[1], 1, 1)
        line2 = grid.line(pair2)
        *side1, line2[1], line2[2], line2[3], x_image = tie(*side1, *line2[1:], x_image)

        line2, *to = side_operands((chunk1, *side1), line2)
        chunk2 = Chunk(grid, line2, 1024, False)
        side2 = grid.shift(to[0], 2, 1), grid.shift(to[1], 1, 1)
        other1 = grid.across(chunk1.line, *side1)
        tied = tie(*side2, *other1)
        side2, other1 = tied[:2], tied[2:]

        to = side_operands((chunk2, *side2), None)
        side3 = grid.shift(to[0], 2, 1), grid.shift(to[1], 1, 1)
        line3 = grid.line(beside(txt_down))
        other2 = grid.across(*after_all(side2, *to), chunk2.line)
        chunk1.hold(chunk1.line, other1[0], 0, 0, 0, 0, chunk1.cols)
        settle(chunk1, chunk0, side1, other1[1:])
        settle(chunk2, chunk1, side2, other2[:2])
        chunk2.hold(chunk2.line, other2[2], 0, 0, 0, 0, chunk2.cols)
        image_w = [chunk1.halves(width, 3 * width, 0), chunk1.halves(width, width, 3 * width // 2)]
        where = after(table, *to)
    else:
        image_w = [gathered(w) for w in (img_qkv, img_out, img_in, img_proj, img_down)]
        text_w = [gathered(w) for w in (*text_parts, txt_down)]
        where = table
    sizes = vec + vec + (captions,) * 3
    block = block.astype(F32)
    parts = [block[:, i, :size].reshape(-1) for i, size in enumerate(sizes)]
    img_g, img_s = parts[0].reshape(2, width), parts[1].reshape(2, width)
    gains, shifts = parts[3].reshape(2, width), parts[4].reshape(2, width)
    img_b, biases = parts[2].reshape(1, -1), parts[5].reshape(1, -1)
    every_pair = parts[6].astype(jnp.int32) * 64 + parts[7].astype(jnp.int32)
    every_count = parts[8]

    image_second = run(
        image_attention,
        [shape((padded, width), F32)],
        [((padded, width), BF16), ((padded, 3 * width), BF16), ((padded, width), BF16)],
        where,
        [x_image, img_g, img_s],
        image_w[:2],
        us=19,
    )[0]
    where = table
    if regular:
        tied = tie(*side3, image_second, *line3[1:])
        side3, image_second, line3 = tied[:2], tied[2], [line3[0], *tied[3:]]
        chunk3 = Chunk(grid, jnp.stack(line3), width, False)
        side4 = grid.square(chunk3.line)
        settle(None, chunk2, side3, grid.across(*after_all(side3, chunk3.line)))
        other0 = grid.across(chunk0.line, *after_all(side0, chunk3.line))
        chunk0.hold(chunk0.line, other0[0], 0, 0, 0, 0, chunk0.cols)
        settle(chunk0, None, side0, other0[1:])
        image_w += [
            chunk2.halves(width, units, 0),
            chunk2.halves(width, width, units // 2),
            chunk0.deep(units, width),
        ]
        where = after(table, chunk3.line)
    pooled, pooled_second = run(
        image_inner,
        [shape((images, units), F32), shape((images, width), F32)],
        [((padded, width), BF16)],
        where,
        [image_second, img_g, img_s, img_b],
        image_w[2:3],
        us=13,
    )
    image_emb = run(
        image_embed,
        [shape((images, width), BF16)],
        [],
        table,
        [pooled, pooled_second, img_b],
        [image_w[4], image_w[3]],
        us=5,
    )[0]
    if regular:
        *side4, image_emb = tie(*side4, image_emb)
        to = side_operands((chunk3, *side4), None)
        side5 = grid.shift(to[0], 2, 1), grid.shift(to[1], 1, 1)
        other4 = grid.across(*after_all(side4, *to), chunk3.line)
        settle(chunk3, None, side4, other4[:2])
        chunk3.hold(chunk3.line, other4[2], 0, 0, 0, 0, chunk3.cols)
    image_all = to_all(image_emb, devices)
    where = after(table, image_emb)

    heads = tokens // (2 * HEAD) * (width // (2 * HEAD))
    qkv, probs, mixed, second = run(
        text_attention,
        [
            shape((tokens, 3 * width), BF16),
            shape((heads, 4 * HEAD, 2 * HEAD), F32),
            shape((tokens, width), BF16),
            shape((tokens, width), F32),
        ],
        [((tokens, width), BF16)],
        where,
        [text_tokens, caption_col, caption_row, gains, shifts],
        text_w[:2],
        us=10,
    )
    if regular:
        *side5, second = tie(*side5, second)
        settle(None, chunk3, side5, grid.across(*side5))
        text_w.append(chunk3.deep(units, width))
    hidden, slope, hidden_sum = run(
        text_inner,
        [shape((tokens, units), BF16), shape((tokens, units), F32), shape((captions, units), BF16)],
        [((tokens, width), BF16)],
        table,
        [second, caption_row, gains, shifts, biases],
        text_w[2:3],
        us=7,
    )
    text_out, pool_low = run(
        text_outer,
        [shape((tokens, width), BF16), shape((captions, width), BF16)],
        [],
        table,
        [second, hidden, caption_row, biases],
        text_w[4:5],
        us=5,
    )
    pool_low, image_emb = tie(pool_low, image_all)
    image_emb = image_emb.reshape(-1, width)
    wide_part = units // devices
    sent = jnp.concatenate(
        [
            jnp.broadcast_to(pool_low[None], (devices, captions, width)),
            hidden_sum.reshape(captions, devices, wide_part).transpose(1, 0, 2),
        ],
        axis=2,
    )
    sent = lax.all_to_all(sent, "blk", 0, 0).reshape(-1, width + wide_part)
    pool_all, hidden_sum = sent[:, :width], sent[:, width:]
    total = pool_all.shape[0]
    if total <= TILE:
        pool_cols = lax.dynamic_slice_in_dim(pool_all, device * own, own, axis=1)
        losses, d_mine, grad_proj, grad_down = run(
            head_kernel,
            [
                shape((total, 1), F32),
                shape((captions, width), F32),
                shape((own, width), F32),
                shape((units // devices, width), F32),
            ],
            [],
            table,
            [pool_all, image_emb, every_pair[:, None], every_count[:, None], hidden_sum, pool_cols],
            text_w[3:4],
            us=12,
            passes_table=True,
            scalars=[logit_scale],
        )
        pair_loss = lax.dynamic_slice_in_dim(losses[:, 0], device * captions, captions)
    else:
        w_proj = run(copy_weight, [shape((width, width), BF16)], [], table, [], text_w[3:4])[0]
        pair_loss, d_mine, grad_proj, grad_down = head_tiled(
            total, captions, own, scale, pool_all, image_emb, every_pair, every_count, hidden_sum, w_proj
        )

    half = width // 2
    mine_in, theirs_in, d_inner, sums_in = run(
        functools.partial(back_inner, devices),
        [
            shape((half, units), BF16),
            shape((half, units), BF16),
            shape((tokens, units), BF16),
            shape((1, units), F32),
        ],
        [((half, tokens), BF16), ((half, tokens), BF16), ((3 * captions, units), BF16)],
        table,
        [d_mine, caption_col, second, slope, gains, shifts],
        text_w[4:5],
        us=15,
        passes_table=True,
    )
    d_second, d_mixed, sums_out = run(
        back_second,
        [shape((tokens, width), F32), shape((tokens, width), BF16), shape((8, width), F32)],
        [((tokens, width), F32)],
        table,
        [d_mine, d_inner, caption_col, second, gains],
        [text_w[2], text_w[1]],
    )
    if regular:
        got_in, d_mixed = tie(grid.shift(theirs_in, 3, 1), d_mixed)
        held_in, got_in, sent = grid.reduce_start(table, mine_in, got_in)
    (d_qkv,) = run(back_attention, [shape((tokens, 3 * width), BF16)], [], table, [d_mixed, qkv, probs], [])
    where = table
    mine_qkv, theirs_qkv = run(
        functools.partial(back_weights, devices),
        [shape((half, 4 * width), BF16), shape((half, 4 * width), BF16)],
        [((half, tokens), BF16)] * 4,
        where,
        [text_tokens, d_second, d_qkv, mixed, gains, shifts],
        [],
        us=5,
        passes_table=True,
    )
    where = after(table, mine_qkv)
    if regular:
        *got_in, mine_qkv, theirs_qkv = tie(*got_in, mine_qkv, theirs_qkv)
        got_qkv = grid.shift(theirs_qkv, 3, 1)
        held_in, got_in, sent = grid.reduce_next(table, held_in, got_in)
    if regular:
        held_qkv, got_qkv, sent = grid.reduce_start(table, mine_qkv, got_qkv)
        where = after(table, *sent)
    text_grad, sums_qkv = run(
        back_outer,
        [shape((tokens, width), F32), shape((8, width), F32)],
        [((tokens, width), F32)],
        where,
        [text_tokens, d_second, d_qkv, gains],
        text_w[:1],
        us=5,
    )
    (sums,) = run(
        pack_sums, [shape((devices, 384), F32)], [], table, [sums_qkv, sums_out, sums_in], [], us=2
    )
    if not regular:
        sums = lax.all_to_all(sums, "blk", 0, 0, tiled=True)
    if regular:
        text_grad, sums, *got_in = tie(text_grad, sums, *got_in)
        kept_in, got_in = grid.reduce_line(table, held_in, got_in)
        kept_in, *got_qkv = tie(kept_in, *got_qkv)
        held_qkv, got_qkv, sent = grid.reduce_next(table, held_qkv, got_qkv)
        sums = lax.all_to_all(sums, "blk", 0, 0, tiled=True)
        sums, *tied = tie(sums, *got_in, *got_qkv)
        got_in, got_qkv = tied[: len(got_in)], tied[len(got_in) :]
        kept_qkv, got_qkv = grid.reduce_line(table, held_qkv, got_qkv)
        (grad_in,) = grid.reduce_end(table, kept_in, got_in, [units])
        grad_qkv, grad_out = grid.reduce_end(table, kept_qkv, got_qkv, [3 * width, width])
    else:
        grad_in = reduce_grads(grid, mine_in, theirs_in, width)
        grad_qkv = reduce_grads(grid, mine_qkv, theirs_qkv, width)
        grad_qkv, grad_out = grad_qkv[:, : 3 * width], grad_qkv[:, 3 * width :]
    sums = jnp.sum(sums, axis=0)
    return (
        pair_loss,
        text_out,
        text_grad,
        sums[: vec[0]],
        sums[128 : 128 + vec[1]],
        grad_qkv,
        grad_out,
        grad_in,
        grad_down,
        sums[256 : 256 + vec[2]],
        grad_proj,
    )


def copy_weight(weight, out):
    out[...] = weight()[...]


def axis_sizes(mesh):
    devices = list(mesh.devices.flat)
    places = [(*d.coords, d.core_on_chip) for d in devices]
    sizes = []
    stride = len(devices)
    left = [0, 1, 2, 3]
    while stride > 1 and left:
        for axis in left:
            size = 1 + max(p[axis] for p in places) - min(p[axis] for p in places)
            step = stride // size
            if size > 1 and all(
                p[axis] - places[0][axis] == (i // step) % size for i, p in enumerate(places)
            ):
                sizes.append(size)
                left.remove(axis)
                stride = step
                break
        else:
            return [len(devices)]
    return sizes


def solution(mesh):
    grid = Grid(mesh.shape["blk"], axis_sizes(mesh))
    row = P("blk", None)
    flat = P("blk")
    tower = (flat, flat, row, row, row, row, flat, row)

    def body(*args):
        return on_device(grid, *args)

    return jax.shard_map(
        body,
        mesh=mesh,
        in_specs=(row, row, flat, row, P()) + tower + tower,
        out_specs=(flat, row, row, flat, flat, row, row, row, row, flat, row),
        check_vma=False,
    )
```

```python
import functools

import jax
import jax.numpy as jnp
from jax import lax
from jax.experimental import pallas as pl
from jax.experimental.pallas import tpu as pltpu
from jax.sharding import PartitionSpec as P

HEAD = 64
PATCHES = 50
CAPS = 4
TILE = 512
GROUP_PAD = 112

F32 = jnp.float32
BF16 = jnp.bfloat16


def gelu(z):
    return 0.5 * z * (1.0 + jnp.tanh(0.7978845608028654 * (z + 0.044715 * z * z * z)))


def normalize(x):
    mean = jnp.mean(x, axis=-1, keepdims=True)
    cent = x - mean
    rstd = lax.rsqrt(jnp.mean(cent * cent, axis=-1, keepdims=True) + 1e-06)
    return (cent * rstd, rstd)


def norm_back(grad, normed, rstd):
    return rstd * (
        grad
        - jnp.mean(grad, axis=-1, keepdims=True)
        - normed * jnp.mean(grad * normed, axis=-1, keepdims=True)
    )


def unit_rows(proj):
    factor = lax.rsqrt(jnp.sum(proj * proj, axis=-1, keepdims=True) + 1e-06)
    return (proj * factor, factor)


def matmul(left, right):
    return jnp.dot(left, right, preferred_element_type=F32)


def dot_nt(left, right):
    return lax.dot_general(left, right, (((1,), (1,)), ((), ())), preferred_element_type=F32)


def dot_tn(left, right):
    return lax.dot_general(left, right, (((0,), (0,)), ((), ())), preferred_element_type=F32)


def chunks(total, size, unroll=True):
    def wrap(body):
        @pl.loop(0, total // size, unroll=unroll)
        def step(j):
            body(pl.ds(pl.multiple_of(j * size, size), size))

    return wrap


def thirds(value):
    high = value.astype(BF16)
    rest = value - high.astype(F32)
    mid = rest.astype(BF16)
    return high, mid, (rest - mid.astype(F32)).astype(BF16)


def norm_rows(x, gain, shift):
    normed, rstd = normalize(x)
    return (normed * gain + shift).astype(BF16)


def head_masks(dtype, value):
    lane = lax.broadcasted_iota(jnp.int32, (1, 2 * HEAD), 1)
    first = jnp.where(lane < HEAD, value, 0.0).astype(dtype)
    second = jnp.where(lane < HEAD, 0.0, value).astype(dtype)
    return first, second


def both_heads(block, masks):
    return jnp.concatenate([block * masks[0], block * masks[1]], axis=0)


def merge_heads(stacked):
    half = stacked.shape[0] // 2
    lane = lax.broadcasted_iota(jnp.int32, (1, 2 * HEAD), 1)
    return jnp.where(lane < HEAD, stacked[:half], stacked[half:])


def softmax_unit(query, keys, mask, masks):
    scores = dot_nt(both_heads(query, masks), keys)
    scores = jnp.where(mask, scores, -1000000000.0)
    top = jnp.max(scores, axis=-1, keepdims=True)
    expo = jnp.exp(scores - top)
    return expo * (1.0 / jnp.sum(expo, axis=-1, keepdims=True))


def image_attention(x, gains, shifts, w_qkv, w_out, second, act, qkv, mixed):
    rows, width = x.shape
    group = GROUP_PAD

    @chunks(rows, group)
    def _(at):
        act[at, :] = norm_rows(x[at, :].astype(F32), gains[0:1, :], shifts[0:1, :])

    w_qkv = w_qkv()

    @chunks(3 * width, 256)
    def _(at):
        qkv[:, at] = matmul(act[...], w_qkv[:, at]).astype(BF16)

    masks = head_masks(BF16, 0.125)
    own = lax.broadcasted_iota(jnp.int32, (2 * group, group), 0)
    own = jnp.where(own >= group, own - group, own)
    other = lax.broadcasted_iota(jnp.int32, (2 * group, group), 1)
    mask = picture(own) == picture(other)

    @chunks(rows, group, 2)
    def _(at):
        for start in range(0, width, 2 * HEAD):
            cols = slice(start, start + 2 * HEAD)
            keys = qkv[at, width + start : width + start + 2 * HEAD]
            values = qkv[at, 2 * width + start : 2 * width + start + 2 * HEAD]
            probs = softmax_unit(qkv[at, cols], keys, mask, masks)
            mixed[at, cols] = merge_heads(matmul(probs.astype(BF16), values)).astype(BF16)

    w_out = w_out()

    @chunks(width, 256)
    def _(at):
        second[:, at] = x[:, at].astype(F32) + matmul(mixed[...], w_out[:, at])


def picture(place):
    return jnp.where(place >= PATCHES, 1, 0) + jnp.where(place >= 2 * PATCHES, 1, 0)


def image_pool(value):
    value = value.reshape(-1, GROUP_PAD, value.shape[1])
    which = picture(lax.broadcasted_iota(jnp.int32, (1, GROUP_PAD, 1), 1))
    parts = [jnp.sum(jnp.where(which == kind, value, 0.0), axis=1) for kind in range(2)]
    return jnp.concatenate(parts, axis=0) * (1.0 / PATCHES)


def image_inner(second, gains, shifts, biases, w_in, pooled, pooled_second, act):
    rows, width = second.shape
    units = pooled.shape[1]

    @chunks(rows, GROUP_PAD)
    def _(at):
        act[at, :] = norm_rows(second[at, :], gains[1:2, :], shifts[1:2, :])

    for start in range(0, width, 256):
        pooled_second[:, start : start + 256] = image_pool(second[:, start : start + 256])
    w_in = w_in()

    @chunks(units, 256)
    def _(at):
        hidden = gelu(matmul(act[...], w_in[:, at]) + biases[:, at]).astype(BF16).astype(F32)
        pooled[:, at] = image_pool(hidden)


def image_embed(pooled, pooled_second, biases, w_down, w_proj, emb):
    images, units = pooled.shape
    high, mid, unused = thirds(pooled[...])
    w_down = w_down()
    y = matmul(jnp.concatenate([high, mid], axis=0), w_down[...])
    y = y[:images] + y[images:] + pooled_second[...] + biases[:, units:]
    unit = unit_rows(matmul(y.astype(BF16), w_proj()[...]))[0].astype(BF16)
    to = lax.broadcasted_iota(jnp.int32, (images, images), 0)
    source = lax.broadcasted_iota(jnp.int32, (images, images), 1)
    half = images // 2
    order = (jnp.where(source >= half, 2 * (source - half) + 1, 2 * source) == to).astype(BF16)
    emb[...] = matmul(order, unit).astype(BF16)


def text_attention(x, caption_col, caption_row, gains, shifts, w_qkv, w_out, qkv, probs, mixed, second, act):
    rows, width = x.shape
    group = 2 * HEAD
    act[...] = norm_rows(x[...].astype(F32), gains[0:1, :], shifts[0:1, :])
    w_qkv = w_qkv()

    @chunks(3 * width, 256)
    def _(at):
        qkv[:, at] = matmul(act[...], w_qkv[:, at]).astype(BF16)

    masks = head_masks(BF16, 0.125)
    unit = 0
    for top in range(0, rows, group):
        at = slice(top, top + group)
        same = caption_col[at, :] == caption_row[:, at]
        mask = jnp.concatenate([same, same], axis=0)
        for start in range(0, width, 2 * HEAD):
            cols = slice(start, start + 2 * HEAD)
            keys = qkv[at, width + start : width + start + 2 * HEAD]
            values = qkv[at, 2 * width + start : 2 * width + start + 2 * HEAD]
            prob = softmax_unit(qkv[at, cols], keys, mask, masks)
            probs[unit] = prob
            unit += 1
            mixed[at, cols] = merge_heads(matmul(prob.astype(BF16), values)).astype(BF16)

    w_out = w_out()

    @chunks(width, 256)
    def _(at):
        second[:, at] = x[:, at].astype(F32) + matmul(mixed[...], w_out[:, at])


def caption_member(caption_row, captions):
    index = lax.broadcasted_iota(jnp.int32, (captions, caption_row.shape[1]), 0)
    return (index == caption_row[...]).astype(F32)


def text_inner(second, caption_row, gains, shifts, biases, w_in, hidden, slope, hidden_sum, act):
    units = hidden.shape[1]
    act[...] = norm_rows(second[...], gains[1:2, :], shifts[1:2, :])
    low = caption_member(caption_row, hidden_sum.shape[0]).astype(BF16)
    w_in = w_in()

    @chunks(units, 256)
    def _(at):
        z = matmul(act[...], w_in[:, at]) + biases[:, at]
        inside = jnp.tanh(0.7978845608028654 * (z + 0.044715 * z * z * z))
        value = (0.5 * z * (1.0 + inside)).astype(BF16)
        hidden[:, at] = value
        slope[:, at] = 0.5 * (1.0 + inside) + 0.5 * z * (1.0 - inside * inside) * (
            0.7978845608028654 * (1.0 + 3.0 * 0.044715 * z * z)
        )
        hidden_sum[:, at] = matmul(low, value).astype(BF16)


def text_outer(second, hidden, caption_row, biases, w_down, out, pool_low):
    width = second.shape[1]
    units = hidden.shape[1]
    member = caption_member(caption_row, pool_low.shape[0])
    low = member.astype(BF16)
    count = jnp.sum(member, axis=1, keepdims=True)
    w_down = w_down()

    @chunks(width, 256)
    def _(at):
        outer = biases[:, pl.ds(pl.multiple_of(units + at.start, 256), 256)]
        y = second[:, at] + matmul(hidden[...], w_down[:, at]) + outer
        out[:, at] = y.astype(BF16)
        total = sum(matmul(low, part) for part in thirds(y))
        pool_low[:, at] = (total / count).astype(BF16)


def head_kernel(
    table, scale_ref, pool_all, image_emb, pair_col, count, hidden_sum, pool_cols, w_proj,
    loss, d_mine, grad_proj, grad_down,
):
    scale = scale_ref[0]
    captions = d_mine.shape[0]
    w_proj = w_proj()
    proj = matmul(pool_all[...], w_proj[...])
    unit, factor = unit_rows(proj)
    sim = scale * dot_nt(unit.astype(BF16), image_emb[...])
    row_max = jnp.max(sim, axis=1, keepdims=True)
    row_lse = row_max + jnp.log(jnp.sum(jnp.exp(sim - row_max), axis=1, keepdims=True))
    col_max = jnp.max(sim, axis=0, keepdims=True)
    col_lse = col_max + jnp.log(jnp.sum(jnp.exp(sim - col_max), axis=0, keepdims=True))
    hit = pair_col[...] == lax.broadcasted_iota(jnp.int32, sim.shape, 1)
    both = 0.5 * jnp.exp(sim - row_lse) + 0.5 * jnp.exp(sim - col_lse)
    weights_sim = jnp.where(hit, both - 1.0, both).astype(BF16)
    pos = jnp.sum(jnp.where(hit, sim, 0.0), axis=1, keepdims=True)
    pair_lse = jnp.sum(jnp.where(hit, col_lse, 0.0), axis=1, keepdims=True)
    loss[...] = 0.5 * (row_lse - pos) + 0.5 * (pair_lse - pos)
    d_emb = scale * matmul(weights_sim, image_emb[...])
    inside = jnp.sum(d_emb * proj, axis=-1, keepdims=True)
    d_proj = (factor * d_emb - proj * (factor * factor * factor * inside)).astype(BF16)
    grad_proj[...] = dot_tn(pool_cols[...], d_proj)
    d_each = dot_nt(d_proj, w_proj[...]) / count[...]
    d_low = d_each.astype(BF16)
    grad_down[...] = dot_tn(hidden_sum[...], d_low)
    first = table[PLACE] * captions
    index = lax.broadcasted_iota(jnp.int32, (captions, d_each.shape[0]), 1)
    pick = (index == first + lax.broadcasted_iota(jnp.int32, (captions, d_each.shape[0]), 0)).astype(BF16)
    d_mine[...] = sum(matmul(pick, part) for part in thirds(d_each))


def text_front(
    x, caption_col, caption_row, gains, shifts, biases, w_qkv, w_out, w_in,
    qkv, probs, mixed, second, hidden, slope, hidden_sum, act,
):
    text_attention(x, caption_col, caption_row, gains, shifts, w_qkv, w_out, qkv, probs, mixed, second, act)
    text_inner(second, caption_row, gains, shifts, biases, w_in, hidden, slope, hidden_sum, act)


def image_rest(second, gains, shifts, biases, w_in, w_down, w_proj, emb, act, pooled, pooled_second):
    image_inner(second, gains, shifts, biases, w_in, pooled, pooled_second, act)
    image_embed(pooled, pooled_second, biases, w_down, w_proj, emb)


def pack_sums(sums_qkv, sums_out, sums_in, out):
    devices, width = out.shape[0], sums_out.shape[1]
    first, second = sums_qkv[...], sums_out[...]
    vectors = [
        jnp.concatenate([first[0:1], second[1:2]], axis=1),
        jnp.concatenate([first[1:2], second[2:3]], axis=1),
        jnp.concatenate([sums_in[...], second[0:1]], axis=1),
    ]
    for i, vector in enumerate(vectors):
        total = vector.shape[1]
        share = total // devices
        row = lax.broadcasted_iota(jnp.int32, (devices, total), 0)
        place = lax.broadcasted_iota(jnp.int32, (devices, total), 1) - row * share
        mine = jnp.where(place >= 0, jnp.where(place < share, vector, 0.0), 0.0)
        to = lax.broadcasted_iota(jnp.int32, (total, 128), 1)
        source = lax.broadcasted_iota(jnp.int32, (total, 128), 0)
        pick = (lax.rem(source, share) == to).astype(BF16)
        out[:, i * 128 : (i + 1) * 128] = sum(matmul(part, pick) for part in thirds(mine))


def core_split(table, value, devices, mine, theirs):
    own = value.shape[0] // devices
    value = value.reshape(devices // 2, 2, own, value.shape[1])
    first = table[CORE] == 0
    even = value[:, 0].reshape(-1, value.shape[3])
    odd = value[:, 1].reshape(-1, value.shape[3])
    mine[...] = jnp.where(first, even, odd).astype(BF16)
    theirs[...] = jnp.where(first, odd, even).astype(BF16)


def token_member(caption_col, captions):
    index = lax.broadcasted_iota(jnp.int32, (caption_col.shape[0], 3 * captions), 1)
    index = jnp.where(index >= captions, index - captions, index)
    index = jnp.where(index >= captions, index - captions, index)
    return (caption_col[...] == index).astype(BF16)


def back_inner(
    devices, table, each, caption_col, second, slope, gains, shifts, w_down,
    mine, theirs, d_inner, sums, act_t, act_u, both,
):
    rows, width = second.shape
    units = slope.shape[1]
    captions = each.shape[0]
    member = token_member(caption_col, captions)
    normed, rstd = normalize(second[...])
    act = normed * gains[1:2, :] + shifts[1:2, :]
    core_split(table, act.T, devices, act_t, act_u)
    each_low = each[...].astype(BF16)
    w_down = w_down()

    @chunks(units, 256)
    def _(at):
        both[:, at] = jnp.concatenate(thirds(dot_nt(each_low, w_down[at, :])), axis=0)

    @chunks(units, 256)
    def _(at):
        low = (matmul(member, both[:, at]) * slope[:, at]).astype(BF16)
        d_inner[:, at] = low
        sums[:, at] = jnp.sum(low.astype(F32), axis=0, keepdims=True)
        theirs[:, at] = matmul(act_u[...], low).astype(BF16)
        mine[:, at] = matmul(act_t[...], low).astype(BF16)


def back_second(each, d_inner, caption_col, second, gains, w_in, w_out, d_second, d_mixed, sums, d_act):
    width = second.shape[1]
    normed, rstd = normalize(second[...])
    d_y = matmul(token_member(caption_col, each.shape[0]), jnp.concatenate(thirds(each[...]), axis=0))
    sums[0:1, :] = jnp.sum(d_y, axis=0, keepdims=True)
    w_in = w_in()

    @chunks(width, 256)
    def _(at):
        d_act[:, at] = dot_nt(d_inner[...], w_in[at, :])

    grad = d_act[...]
    sums[1:2, :] = jnp.sum(grad * normed, axis=0, keepdims=True)
    sums[2:3, :] = jnp.sum(grad, axis=0, keepdims=True)
    d_two = d_y + norm_back(grad * gains[1:2, :], normed, rstd)
    d_second[...] = d_two
    d_mixed[...] = dot_nt(d_two.astype(BF16), w_out()[...]).astype(BF16)


def back_attention(d_mixed, qkv, probs, d_qkv):
    rows, width = d_mixed.shape
    group = 2 * HEAD
    ones = head_masks(BF16, 1.0)
    masks = head_masks(BF16, 0.125)
    unit = 0
    for top in range(0, rows, group):
        at = slice(top, top + group)
        for start in range(0, width, 2 * HEAD):
            cols = slice(start, start + 2 * HEAD)
            key_cols = slice(width + start, width + start + 2 * HEAD)
            value_cols = slice(2 * width + start, 2 * width + start + 2 * HEAD)
            prob = probs[unit]
            unit += 1
            d_out = both_heads(d_mixed[at, cols], ones)
            query = both_heads(qkv[at, cols], masks)
            d_qkv[at, value_cols] = dot_tn(prob.astype(BF16), d_out).astype(BF16)
            d_prob = dot_nt(d_out, qkv[at, value_cols])
            d_score = (prob * (d_prob - jnp.sum(prob * d_prob, axis=-1, keepdims=True))).astype(BF16)
            d_qkv[at, cols] = (0.125 * merge_heads(matmul(d_score, qkv[at, key_cols]))).astype(BF16)
            d_qkv[at, key_cols] = dot_tn(d_score, query).astype(BF16)


def back_weights(
    devices, table, x, d_second, d_qkv, mixed, gains, shifts,
    mine, theirs, act_t, act_u, mixed_t, mixed_u,
):
    width = x.shape[1]
    core_split(table, norm_rows(x[...].astype(F32), gains[0:1, :], shifts[0:1, :]).astype(F32).T, devices, act_t, act_u)
    core_split(table, mixed[...].astype(F32).T, devices, mixed_t, mixed_u)
    d_low = d_second[...].astype(BF16)
    for start in range(0, width, 256):
        at = slice(start, start + 256)
        to = slice(3 * width + start, 3 * width + start + 256)
        theirs[:, to] = matmul(mixed_u[...], d_low[:, at]).astype(BF16)
        mine[:, to] = matmul(mixed_t[...], d_low[:, at]).astype(BF16)

    @chunks(3 * width, 256)
    def _(at):
        theirs[:, at] = matmul(act_u[...], d_qkv[:, at]).astype(BF16)
        mine[:, at] = matmul(act_t[...], d_qkv[:, at]).astype(BF16)


def back_outer(x, d_second, d_qkv, gains, w_qkv, text_grad, sums, d_act):
    width = x.shape[1]
    normed, rstd = normalize(x[...].astype(F32))
    w_qkv = w_qkv()

    @chunks(width, 256)
    def _(at):
        d_act[:, at] = dot_nt(d_qkv[...], w_qkv[at, :])

    grad = d_act[...]
    sums[0:1, :] = jnp.sum(grad * normed, axis=0, keepdims=True)
    sums[1:2, :] = jnp.sum(grad, axis=0, keepdims=True)
    text_grad[...] = d_second[...] + norm_back(grad * gains[0:1, :], normed, rstd)


class Weight:
    def __init__(self, rows, cols):
        self.dims = (rows, cols)
        self.parts = []

    def add(self, array, lead, start, width, row=None, unit=0, below=0, col=None, beside=0):
        self.parts.append((array, lead, start, width, row, unit, below, col, beside))


def run(kernel, outs, scratch, table, operands, weights, us=5, passes_table=False, scalars=()):
    arrays = []
    for weight in weights:
        for part in weight.parts:
            if not any(part[0] is a for a in arrays):
                arrays.append(part[0])
    places = {id(a): i for i, a in enumerate(arrays)}
    n_s, n_op, n_arr, n_out, n_w = len(scalars), len(operands), len(arrays), len(outs), len(weights)

    def body(*refs):
        table_ref, refs = refs[0], refs[1:]
        ops, refs = refs[: n_s + n_op], refs[n_s + n_op :]
        arrs, refs = refs[:n_arr], refs[n_arr:]
        out, refs = refs[:n_out], refs[n_out:]
        held, refs = refs[:n_w], refs[n_w:]
        if n_w:
            sems, refs = refs[0], refs[1:]
        waits = []
        for i, weight in enumerate(weights):
            for array, lead, start, width, row, unit, below, col, beside in weight.parts:
                at = 0 if row is None else pl.multiple_of(table_ref[row] * unit + below, 16)
                to = beside
                if col is not None:
                    to = pl.multiple_of(table_ref[col] * (weight.dims[1] // 2) + beside, 128)
                pltpu.make_async_copy(
                    arrs[places[id(array)]].at[lead, :, pl.ds(start, width)],
                    held[i].at[pl.ds(at, array.shape[1]), pl.ds(to, width)],
                    sems.at[i],
                ).start()

            def wait(i=i):
                pltpu.make_async_copy(held[i], held[i], sems.at[i]).wait()
                return held[i]

            waits.append(wait)
        if passes_table:
            ops = (table_ref, *ops)
        kernel(*ops, *waits, *out, *refs)

    vmem = pl.BlockSpec(memory_space=pltpu.VMEM)
    return pl.pallas_call(
        body,
        out_shape=outs,
        in_specs=[pl.BlockSpec(memory_space=pltpu.SMEM)] * (1 + n_s) + [vmem] * n_op + [pl.BlockSpec(memory_space=pltpu.HBM)] * n_arr,
        out_specs=[vmem] * n_out,
        scratch_shapes=[pltpu.VMEM(w.dims, BF16) for w in weights]
        + ([pltpu.SemaphoreType.DMA((n_w,))] if n_w else [])
        + [pltpu.VMEM(*s) for s in scratch],
        compiler_params=pltpu.CompilerParams(vmem_limit_bytes=60 << 20),
        cost_estimate=pl.CostEstimate(flops=us * 2000000000, bytes_accessed=1000, transcendentals=0),
    )(table, *scalars, *operands, *arrays)


def shape(dims, dtype):
    return jax.ShapeDtypeStruct(dims, dtype)


class Grid:
    def __init__(self, devices, sizes):
        self.devices = devices
        self.sizes = sizes
        strides = []
        step = devices
        for size in sizes:
            step //= size
            strides.append(step)
        self.strides = strides
        self.regular = len(sizes) == 4 and sizes[1:] == [2, 2, 2]

    def place(self):
        index = lax.axis_index("blk")
        return [(index // st) % size for size, st in zip(self.sizes, self.strides)]

    def shift(self, value, axis, step):
        size, stride = self.sizes[axis], self.strides[axis]
        pairs = []
        for i in range(self.devices):
            at = (i // stride) % size
            pairs.append((i, i + ((at + step) % size - at) * stride))
        return lax.ppermute(value, "blk", pairs)

    def table(self):
        if len(self.sizes) != 4:
            index = lax.axis_index("blk")
            return jnp.stack([index % 2, 1 - index % 2, index]).astype(jnp.int32)
        place = self.place()
        chips = []
        for offset in self.offsets():
            origin = [
                d[1] if isinstance(d, tuple) else (p - d) % s for p, d, s in zip(place, offset, self.sizes)
            ]
            chips.append(sum(o * st for o, st in zip(origin, self.strides)) // 2)
        chips = jnp.stack(chips)
        core = place[3]
        return jnp.concatenate(
            [jnp.stack([core, 1 - core, lax.axis_index("blk"), *place[:3]]), chips, 2 * chips + core, 2 * chips + 1 - core]
        ).astype(jnp.int32)

    def offsets(self):
        z, y, x, unused = self.sizes
        zs = list(range(z)) + [("z", i) for i in range(z)]
        return [(dz, dy, dx) for dz in zs for dy in range(y) for dx in range(x)]

    def row_of(self, offset, kind):
        count = len(self.offsets())
        return FIRST_ROW + self.offsets().index(offset) + {"chip": 0, "own": count, "other": 2 * count}[kind]

    def line(self, value):
        return [value] + [self.shift(value, 0, k) for k in range(1, self.sizes[0])]

    def square(self, line):
        return self.shift(line, 2, 1), self.shift(line, 1, 1)

    def along_z(self, value):
        depth = self.sizes[0]
        groups = [[i + k * self.strides[0] for k in range(depth)] for i in range(self.strides[0])]
        return lax.all_to_all(
            jnp.broadcast_to(value[None], (depth, *value.shape)), "blk", 0, 0, axis_index_groups=groups
        )

    def across(self, *arrays):
        return [self.shift(a, 3, 1) for a in arrays]

    def parts(self, value):
        return value.reshape(*self.sizes[:3], -1, value.shape[1])

    def reduce_start(self, table, mine, got):
        mine, got = self.parts(mine), self.parts(got)
        depth, unused, unused, rows, cols = mine.shape
        sent = shape((depth, 2, rows, cols // 2), BF16)
        held = [((depth, 2, rows, cols // 2), BF16)] * 4
        to_x, to_y = fetching(sum_cores, [sent, sent], held, table, [mine, got])
        return (mine, got), (self.shift(to_x, 2, 1), self.shift(to_y, 1, 1)), (to_x, to_y)

    def reduce_next(self, table, held, came):
        depth, unused, unused, rows, cols = held[0].shape
        sent = shape((depth, rows, cols // 2), BF16)
        scratch = [((depth, rows, cols // 2), BF16)] * 6
        to_y, to_x = fetching(sum_sides, [sent, sent], scratch, table, [*held, *came])
        return (*held, *came), (self.shift(to_y, 1, 1), self.shift(to_x, 2, 1)), (to_y, to_x)

    def reduce_line(self, table, held, came):
        depth, unused, unused, rows, cols = held[0].shape
        sent = shape((rows, cols), BF16)
        scratch = [((depth, rows, cols // 2), BF16)] * 8
        outs = [shape((rows, cols), F32)] + [sent] * (depth - 1)
        kept, *to = fetching(sum_corner, outs, scratch, table, [*held, *came])
        return kept, [self.shift(value, 0, k) for k, value in enumerate(to, 1)]

    def reduce_end(self, table, kept, came, widths):
        kernel = functools.partial(sum_line, len(came))
        return run(kernel, [shape((kept.shape[0], w), F32) for w in widths], [], table, [kept, *came], [], us=1)


def wide(*values):
    return sum(v.astype(F32) for v in values)


def fetching(kernel, outs, scratch, table, arrays):
    count, n_out = len(arrays), len(outs)

    def body(*refs):
        table_ref, refs = refs[0], refs[1:]
        arrs, out, held, sems = refs[:count], refs[count : count + n_out], refs[count + n_out : -1], refs[-1]
        steps = kernel(table_ref, *arrs, *out)
        copies = [pltpu.make_async_copy(s, h, sems.at[i]) for i, (s, h) in enumerate(zip(next(steps), held))]
        for copy in copies:
            copy.start()
        for copy in copies:
            copy.wait()
        steps.send(held)

    vmem = pl.BlockSpec(memory_space=pltpu.VMEM)
    return pl.pallas_call(
        body,
        out_shape=outs,
        in_specs=[pl.BlockSpec(memory_space=pltpu.SMEM)] + [pl.BlockSpec(memory_space=pltpu.HBM)] * count,
        out_specs=[vmem] * n_out,
        scratch_shapes=[pltpu.VMEM(*s) for s in scratch] + [pltpu.SemaphoreType.DMA((len(scratch),))],
        compiler_params=pltpu.CompilerParams(vmem_limit_bytes=60 << 20),
        cost_estimate=pl.CostEstimate(flops=1000, bytes_accessed=1000, transcendentals=0),
    )(table, *arrays)


def sum_cores(table, mine, got, to_x, to_y):
    half = to_x.shape[3]
    other_y, other_x = 1 - table[AT_Y], 1 - table[AT_X]
    left, right = pl.ds(0, half), pl.ds(half, half)
    held = yield [
        mine.at[:, :, other_x, :, left],
        got.at[:, :, other_x, :, left],
        mine.at[:, other_y, :, :, right],
        got.at[:, other_y, :, :, right],
    ]
    for z in range(mine.shape[0]):
        for i in range(2):
            to_x[z, i] = wide(held[0][z, i], held[1][z, i]).astype(BF16)
            to_y[z, i] = wide(held[2][z, i], held[3][z, i]).astype(BF16)
    yield


def sum_sides(table, mine, got, by_x, by_y, to_y, to_x):
    half = to_x.shape[2]
    y, x = table[AT_Y], table[AT_X]
    left, right = pl.ds(0, half), pl.ds(half, half)
    held = yield [
        mine.at[:, 1 - y, x, :, left],
        got.at[:, 1 - y, x, :, left],
        by_x.at[:, 1 - y],
        mine.at[:, y, 1 - x, :, right],
        got.at[:, y, 1 - x, :, right],
        by_y.at[:, 1 - x],
    ]
    for z in range(mine.shape[0]):
        to_y[z] = wide(*[h[z] for h in held[:3]]).astype(BF16)
        to_x[z] = wide(*[h[z] for h in held[3:]]).astype(BF16)
    yield


def sum_corner(table, mine, got, by_x, by_y, left_by_y, right_by_x, kept, *to):
    depth = mine.shape[0]
    half = by_x.shape[3]
    y, x = table[AT_Y], table[AT_X]
    left, right = pl.ds(0, half), pl.ds(half, half)
    held = yield [
        mine.at[:, y, x, :, left],
        got.at[:, y, x, :, left],
        by_x.at[:, y],
        left_by_y,
        mine.at[:, y, x, :, right],
        got.at[:, y, x, :, right],
        by_y.at[:, x],
        right_by_x,
    ]
    for k in range(depth):
        z = lax.rem(table[AT_Z] + k, depth)
        out = to[k - 1] if k else kept
        out[:, :half] = wide(*[h[z] for h in held[:4]]).astype(out.dtype)
        out[:, half:] = wide(*[h[z] for h in held[4:]]).astype(out.dtype)
    yield


def sum_line(spans, kept, *refs):
    came = refs[:spans]
    start = 0
    for out in refs[spans:]:
        cols = slice(start, start + out.shape[1])
        start += out.shape[1]
        out[...] = kept[:, cols] + wide(*[c[:, cols] for c in came])


class Chunk:
    def __init__(self, grid, line, cut, ordered):
        self.grid, self.line, self.cut = grid, line, cut
        self.cols = line.shape[2]
        self.zs = [("z", z) if ordered else z for z in range(grid.sizes[0])]
        self.own, self.other = [], []

    def hold(self, mine, theirs, dy, dx, start, low, high):
        offsets = [(z, dy, dx) for z in self.zs]
        for pieces, array in ((self.own, mine), (self.other, theirs)):
            pieces.append((array, offsets, start, low, high))

    def halves(self, rows, cols, start):
        weight = Weight(rows, cols)
        for pieces, col in ((self.own, CORE), (self.other, OTHER)):
            for array, offsets, begin, low, high in pieces:
                left, right = max(low, start), min(high, start + cols // 2)
                if left < right:
                    for lead, offset in enumerate(offsets):
                        row = self.grid.row_of(offset, "chip")
                        at = begin + left - low
                        weight.add(array, lead, at, right - left, row, array.shape[1], 0, col, left - start)
        return weight

    def deep(self, rows, cols):
        weight = Weight(rows, cols)
        parts = self.cols // cols
        for pieces, kind in ((self.own, "own"), (self.other, "other")):
            for array, offsets, begin, low, high in pieces:
                for part in range(parts):
                    left, right = max(low, part * cols), min(high, part * cols + cols)
                    if left < right:
                        for lead, offset in enumerate(offsets):
                            row = self.grid.row_of(offset, kind)
                            high_rows = array.shape[1]
                            at = begin + left - low
                            weight.add(
                                array, lead, at, right - left, row, parts * high_rows, part * high_rows,
                                None, left - part * cols,
                            )
        return weight


def tie(*values):
    return lax.optimization_barrier(values)


def after_all(values, *earlier):
    return lax.optimization_barrier((*values, *earlier))[: len(values)]


def after(value, *earlier):
    return lax.optimization_barrier((value, *earlier))[0]


CORE = 0
OTHER = 1
PLACE = 2
AT_Z, AT_Y, AT_X = 3, 4, 5
FIRST_ROW = 6


def to_all(value, devices):
    return lax.all_to_all(jnp.broadcast_to(value[None], (devices, *value.shape)), "blk", 0, 0)


def pack_kernel(table, *refs):
    first = table[CORE] == 0
    keep, send = refs[-2:]
    start = 0
    for weight in refs[:-2]:
        half = weight.shape[1] // 2
        left, right = weight[:, :half], weight[:, half:]
        keep[:, start : start + half] = jnp.where(first, left, right)
        send[:, start : start + half] = jnp.where(first, right, left)
        start += half


def vector_pack_kernel(caption_row, pair_index, *refs):
    block, refs = refs[-1], refs[:-1]
    captions = pair_index.shape[1]
    pairs = pair_index[...].astype(F32)
    high = jnp.floor(pairs * (1.0 / 64.0))
    member = caption_member(caption_row, captions).astype(BF16)
    count = dot_nt(jnp.ones((8, caption_row.shape[1]), BF16), member)[0:1]
    rows = [r[...].astype(F32) for r in refs] + [high, pairs - 64.0 * high, count]
    rows = [jnp.concatenate([r, jnp.zeros((1, 128 - r.shape[1]), F32)], axis=1) for r in rows]
    rows.append(jnp.zeros((block.shape[0] - len(rows), 128), F32))
    block[...] = jnp.concatenate(rows, axis=0).astype(BF16)


def pair_kernel(table, keep, got, *outs):
    first = table[CORE] == 0
    start = 0
    for out in outs:
        cols = slice(start, start + out.shape[1])
        start += out.shape[1]
        one, two = keep[:, cols].astype(F32), got[:, cols].astype(F32)
        out[...] = jnp.concatenate([jnp.where(first, one, two), jnp.where(first, two, one)], axis=0).astype(BF16)


def pair_up(grid, table, groups):
    rows = groups[0][0].shape[0]
    widths = [sum(w.shape[1] for w in group) // 2 for group in groups]
    packed = shape((rows, sum(widths)), BF16)
    keep, send = run(
        pack_kernel, [packed, packed], [], table, [w for group in groups for w in group], [], us=1, passes_table=True
    )
    return run(
        pair_kernel,
        [shape((2 * rows, w), BF16) for w in widths],
        [],
        table,
        [keep, grid.shift(send, 3, 1)],
        [],
        us=1,
        passes_table=True,
    )


def copied(arrays, outs, moves):
    count = len(arrays)

    def kernel(*refs):
        sems = refs[-1]
        copies = [
            pltpu.make_async_copy(refs[a].at[source], refs[count + o].at[to], sems.at[i])
            for i, (a, source, o, to) in enumerate(moves)
        ]
        for copy in copies:
            copy.start()
        for copy in copies:
            copy.wait()

    anywhere = pl.BlockSpec(memory_space=pltpu.HBM)
    return pl.pallas_call(
        kernel,
        out_shape=outs,
        in_specs=[anywhere] * count,
        out_specs=[pl.BlockSpec(memory_space=pltpu.VMEM)] * len(outs),
        scratch_shapes=[pltpu.SemaphoreType.DMA((len(moves),))],
        cost_estimate=pl.CostEstimate(flops=1000, bytes_accessed=1000, transcendentals=0),
    )(*arrays)


def columns(start, stop):
    return (slice(None), slice(None), pl.ds(start, stop - start))


def side_operands(last, parts):
    chunk, by_x, by_y = last
    cut, end = chunk.cut, chunk.cols
    if parts is None:
        depth, rows = by_x.shape[:2]
        outs = [shape((depth, rows, end - cut), BF16), shape((depth, rows, cut), BF16)]
        moves = [(0, columns(cut, end), 0, columns(0, end - cut)), (1, columns(0, cut), 1, columns(0, cut))]
        return copied([by_y, by_x], outs, moves)
    line = None
    if len(parts) == 1:
        line = parts[0]
        depth, rows, cols = line.shape
        parts = [(0, columns(0, cols), columns(0, cols))]
        arrays = [line]
        outs = []
    else:
        arrays = list(parts)
        depth, (rows, cols) = len(parts), parts[0].shape
        outs = [shape((depth, rows, cols), BF16)]
        parts = [(i, (slice(None), slice(None)), (i, slice(None), pl.ds(0, cols))) for i in range(depth)]
    outs += [shape((depth, rows, cols + end - cut), BF16), shape((depth, rows, cols + cut), BF16)]
    count = len(arrays)
    moves = []
    for o in range(len(outs)):
        moves += [(a, source, o, to) for a, source, to in parts]
    moves.append((count, columns(cut, end), len(outs) - 2, columns(cols, cols + end - cut)))
    moves.append((count + 1, columns(0, cut), len(outs) - 1, columns(cols, cols + cut)))
    out = copied([*arrays, by_y, by_x], outs, moves)
    return out if line is None else [line, *out]


def beside(value):
    half = value.shape[0] // 2
    return jnp.concatenate([value[:half], value[half:]], axis=1)


def settle(chunk, last, mine, theirs):
    by_x, by_y = mine
    start = 0
    if chunk is not None:
        start = chunk.cols
        chunk.hold(by_x, theirs[0], 0, 1, 0, 0, chunk.cols)
        chunk.hold(by_y, theirs[1], 1, 0, 0, 0, chunk.cols)
    if last is not None:
        last.hold(by_x, theirs[0], 1, 1, start, last.cut, last.cols)
        last.hold(by_y, theirs[1], 1, 1, start, 0, last.cut)


def columns_of(whole, widths):
    weights = []
    start = 0
    array = whole[None]
    for width in widths:
        weight = Weight(whole.shape[0], width)
        weight.add(array, 0, start, width)
        weights.append(weight)
        start += width
    return weights


def gathered(part):
    full = lax.all_gather(part, "blk", axis=0, tiled=True)
    weight = Weight(*full.shape)
    weight.add(full[None], 0, 0, full.shape[1])
    return weight


def reduce_grads(grid, mine, theirs, width):
    own = width // grid.devices
    both = jnp.where(lax.axis_index("blk") % 2 == 0, jnp.stack([mine, theirs], 0), jnp.stack([theirs, mine], 0))
    both = both.reshape(2, grid.devices // 2, own, -1).transpose(1, 0, 2, 3).reshape(width, -1)
    return lax.psum_scatter(both, "blk", scatter_dimension=0, tiled=True).astype(F32)


def head_tile(proj, factor, image_emb, scale, row_lse, col_lse, pairs, sim):
    hit = pairs[:, None] == jnp.arange(image_emb.shape[0], dtype=jnp.int32)[None, :]
    weights_sim = (
        0.5 * jnp.exp(sim - row_lse[:, None]) + 0.5 * jnp.exp(sim - col_lse[None, :]) - hit.astype(F32)
    )
    d_emb = scale * matmul(weights_sim.astype(BF16), image_emb)
    d_proj = factor * d_emb - proj * (factor * factor * factor) * jnp.sum(d_emb * proj, axis=-1, keepdims=True)
    pos = jnp.sum(jnp.where(hit, sim, 0.0), axis=1)
    pair_col = jnp.sum(jnp.where(hit, col_lse[None, :], 0.0), axis=1)
    return (d_proj.astype(BF16), 0.5 * (row_lse - pos) + 0.5 * (pair_col - pos))


def head_tiled(total, captions, own, scale, pool_all, image_emb, every_pair, every_count, hidden_sum, w_proj):
    device = lax.axis_index("blk")
    col_max = jnp.full((total,), -1e30, F32)
    col_sum = jnp.zeros((total,), F32)
    held = []
    for start in range(0, total, TILE):
        proj = matmul(pool_all[start : start + TILE], w_proj)
        unit, factor = unit_rows(proj)
        sim = scale * dot_nt(unit.astype(BF16), image_emb)
        top = jnp.max(sim, axis=1)
        row_lse = top + jnp.log(jnp.sum(jnp.exp(sim - top[:, None]), axis=1))
        new_max = jnp.maximum(col_max, jnp.max(sim, axis=0))
        col_sum = col_sum * jnp.exp(col_max - new_max) + jnp.sum(jnp.exp(sim - new_max[None, :]), axis=0)
        col_max = new_max
        held.append((proj, factor, row_lse, sim))
    col_lse = col_max + jnp.log(col_sum)
    d_proj = []
    losses = []
    for start, (proj, factor, row_lse, sim) in zip(range(0, total, TILE), held):
        grad, loss = head_tile(
            proj, factor, image_emb, scale, row_lse, col_lse, every_pair[start : start + TILE], sim
        )
        d_proj.append(grad)
        losses.append(loss)
    d_proj = jnp.concatenate(d_proj)
    pair_loss = lax.dynamic_slice_in_dim(jnp.concatenate(losses), device * captions, captions)
    grad_proj = dot_tn(lax.dynamic_slice_in_dim(pool_all, device * own, own, axis=1), d_proj)
    d_each = dot_nt(d_proj, w_proj) / every_count[:, None]
    grad_down = dot_tn(hidden_sum, d_each.astype(BF16))
    d_mine = lax.dynamic_slice_in_dim(d_each, device * captions, captions)

    return pair_loss, d_mine, grad_proj, grad_down


def unpack_vectors(block, sizes, width):
    block = block.astype(F32)
    parts = [block[:, i, :size].reshape(-1) for i, size in enumerate(sizes)]
    pairs = parts[6].astype(jnp.int32) * 64 + parts[7].astype(jnp.int32)
    shapes = ((2, width), (2, width), (1, -1), (2, width), (2, width), (1, -1))
    vectors = [part.reshape(dims) for part, dims in zip(parts, shapes)]
    return [*vectors, pairs[:, None], parts[8][:, None]]


def on_device(grid, *args):
    (
        text_tokens,
        segment_ids,
        pair_index,
        image_tokens,
        logit_scale,
        img_gains,
        img_shifts,
        img_qkv,
        img_out,
        img_in,
        img_down,
        img_biases,
        img_proj,
        txt_gains,
        txt_shifts,
        txt_qkv,
        txt_out,
        txt_in,
        txt_down,
        txt_biases,
        txt_proj,
    ) = args
    devices = grid.devices
    width = text_tokens.shape[1]
    units = img_in.shape[1]
    scale = logit_scale[0]
    rows, length = segment_ids.shape
    tokens = rows * length
    captions = pair_index.shape[0]
    images = image_tokens.shape[0] // PATCHES
    device = lax.axis_index("blk")
    own = width // devices
    table = grid.table()

    caption_of = (jnp.arange(rows, dtype=jnp.int32)[:, None] * CAPS + segment_ids).reshape(tokens)
    caption_col, caption_row = caption_of[:, None], caption_of[None, :]
    member = (jnp.arange(captions, dtype=jnp.int32)[:, None] == caption_row).astype(F32)

    vec = (img_gains.shape[0], img_shifts.shape[0], img_biases.shape[0])
    vectors = [img_gains, img_shifts, img_biases, txt_gains, txt_shifts, txt_biases]
    (block,) = run(
        vector_pack_kernel,
        [shape((16, 128), BF16)],
        [],
        table,
        [caption_row, pair_index[None], *[v[None] for v in vectors]],
        [],
        us=1,
    )
    block = to_all(block, devices)
    pairs = images // 2
    padded = pairs * GROUP_PAD
    x_image = jnp.pad(
        image_tokens.reshape(pairs, 2 * PATCHES, width), ((0, 0), (0, GROUP_PAD - 2 * PATCHES), (0, 0))
    ).reshape(padded, width)
    regular = grid.regular and own % 8 == 0
    text_parts = [txt_qkv, txt_out, txt_in, txt_proj]
    if regular:
        line0 = grid.line(beside(img_down))
        pair1, pair2 = pair_up(grid, table, [[img_qkv, img_out], [img_in, img_proj]])
        *line0, pair1, pair2 = tie(*line0, pair1, pair2)

        chunk0 = Chunk(grid, jnp.stack(line0), width, False)
        side0 = grid.square(chunk0.line)
        line1 = grid.line(pair1)
        *side0, line1[1], line1[2], line1[3], block = tie(*side0, *line1[1:], block)
        text_all = lax.all_gather(
            after(jnp.concatenate(text_parts, axis=1), line1[1]), "blk", axis=0, tiled=True
        )
        text_w = columns_of(text_all, [w.shape[1] for w in text_parts])

        line1, *to = side_operands((chunk0, *side0), line1)
        chunk1 = Chunk(grid, line1, width, False)
        side1 = grid.shift(to[0], 2, 1), grid.shift(to[1], 1, 1)
        line2 = grid.line(pair2)
        vectors = unpack_vectors(block, vec + vec + (captions,) * 3, width)
        *side1, line2[1], line2[2], line2[3], x_image = tie(*side1, *line2[1:], x_image)

        line2, *to = side_operands((chunk1, *side1), line2)
        chunk2 = Chunk(grid, line2, 1024, False)
        side2 = grid.shift(to[0], 2, 1), grid.shift(to[1], 1, 1)
        other1 = grid.across(chunk1.line, *side1)
        tied = tie(*side2, *other1, *vectors)
        side2, other1, vectors = tied[:2], tied[2:5], tied[5:]

        to = side_operands((chunk2, *side2), None)
        side3 = grid.shift(to[0], 2, 1), grid.shift(to[1], 1, 1)
        other2 = grid.across(*after_all(side2, *to), chunk2.line)
        line3 = grid.line(after(beside(txt_down), *other2))
        chunk1.hold(chunk1.line, other1[0], 0, 0, 0, 0, chunk1.cols)
        settle(chunk1, chunk0, side1, other1[1:])
        settle(chunk2, chunk1, side2, other2[:2])
        chunk2.hold(chunk2.line, other2[2], 0, 0, 0, 0, chunk2.cols)
        image_w = [chunk1.halves(width, 3 * width, 0), chunk1.halves(width, width, 3 * width // 2)]
        where = after(table, *to)
    else:
        image_w = [gathered(w) for w in (img_qkv, img_out, img_in, img_proj, img_down)]
        text_w = [gathered(w) for w in (*text_parts, txt_down)]
        vectors = unpack_vectors(block, vec + vec + (captions,) * 3, width)
        where = table
    img_g, img_s, img_b, gains, shifts, biases, every_pair, every_count = vectors
    image_second = run(
        image_attention,
        [shape((padded, width), F32)],
        [((padded, width), BF16), ((padded, 3 * width), BF16), ((padded, width), BF16)],
        where,
        [x_image, img_g, img_s],
        image_w[:2],
        us=19,
    )[0]
    where = table
    if regular:
        tied = tie(*side3, image_second, *line3[1:])
        side3, image_second, line3 = tied[:2], tied[2], [line3[0], *tied[3:]]
        chunk3 = Chunk(grid, jnp.stack(line3), width, False)
        side4 = grid.square(chunk3.line)
        settle(None, chunk2, side3, grid.across(*after_all(side3, chunk3.line)))
        other0 = grid.across(chunk0.line, *after_all(side0, chunk3.line))
        chunk0.hold(chunk0.line, other0[0], 0, 0, 0, 0, chunk0.cols)
        settle(chunk0, None, side0, other0[1:])
        image_w += [
            chunk2.halves(width, units, 0),
            chunk2.halves(width, width, units // 2),
            chunk0.deep(units, width),
        ]
        where = after(table, chunk3.line)
    (image_emb,) = run(
        image_rest,
        [shape((images, width), BF16)],
        [((padded, width), BF16), ((images, units), F32), ((images, width), F32)],
        where,
        [image_second, img_g, img_s, img_b],
        [image_w[2], image_w[4], image_w[3]],
        us=18,
    )
    if regular:
        *side4, image_emb = tie(*side4, image_emb)
        to = side_operands((chunk3, *side4), None)
        side5 = grid.shift(to[0], 2, 1), grid.shift(to[1], 1, 1)
        other4 = grid.across(*after_all(side4, *to), chunk3.line)
        settle(chunk3, None, side4, other4[:2])
        chunk3.hold(chunk3.line, other4[2], 0, 0, 0, 0, chunk3.cols)
    image_all = to_all(image_emb, devices)
    where = after(table, *to) if regular else after(table, image_emb)

    heads = tokens // (2 * HEAD) * (width // (2 * HEAD))
    qkv, probs, mixed, second, hidden, slope, hidden_sum = run(
        text_front,
        [
            shape((tokens, 3 * width), BF16),
            shape((heads, 4 * HEAD, 2 * HEAD), F32),
            shape((tokens, width), BF16),
            shape((tokens, width), F32),
            shape((tokens, units), BF16),
            shape((tokens, units), F32),
            shape((captions, units), BF16),
        ],
        [((tokens, width), BF16)],
        where,
        [text_tokens, caption_col, caption_row, gains, shifts, biases],
        text_w[:3],
        us=17,
    )
    if regular:
        *side5, second = tie(*side5, second)
        settle(None, chunk3, side5, grid.across(*side5))
        text_w.append(chunk3.deep(units, width))
    text_out, pool_low = run(
        text_outer,
        [shape((tokens, width), BF16), shape((captions, width), BF16)],
        [],
        table,
        [second, hidden, caption_row, biases],
        text_w[4:5],
        us=5,
    )
    pool_low, image_emb = tie(pool_low, image_all)
    image_emb = image_emb.reshape(-1, width)
    wide_part = units // devices
    sent = jnp.concatenate(
        [
            jnp.broadcast_to(pool_low[None], (devices, captions, width)),
            hidden_sum.reshape(captions, devices, wide_part).transpose(1, 0, 2),
        ],
        axis=2,
    )
    sent = lax.all_to_all(sent, "blk", 0, 0).reshape(-1, width + wide_part)
    pool_all, hidden_sum = sent[:, :width], sent[:, width:]
    total = pool_all.shape[0]
    if total <= TILE:
        pool_cols = lax.dynamic_slice_in_dim(pool_all, device * own, own, axis=1)
        losses, d_mine, grad_proj, grad_down = run(
            head_kernel,
            [
                shape((total, 1), F32),
                shape((captions, width), F32),
                shape((own, width), F32),
                shape((units // devices, width), F32),
            ],
            [],
            table,
            [pool_all, image_emb, every_pair, every_count, hidden_sum, pool_cols],
            text_w[3:4],
            us=12,
            passes_table=True,
            scalars=[logit_scale],
        )
        pair_loss = lax.dynamic_slice_in_dim(losses[:, 0], device * captions, captions)
    else:
        w_proj = run(copy_weight, [shape((width, width), BF16)], [], table, [], text_w[3:4])[0]
        pair_loss, d_mine, grad_proj, grad_down = head_tiled(
            total, captions, own, scale, pool_all, image_emb, every_pair[:, 0], every_count[:, 0], hidden_sum, w_proj
        )

    half = width // 2
    mine_in, theirs_in, d_inner, sums_in = run(
        functools.partial(back_inner, devices),
        [
            shape((half, units), BF16),
            shape((half, units), BF16),
            shape((tokens, units), BF16),
            shape((1, units), F32),
        ],
        [((half, tokens), BF16), ((half, tokens), BF16), ((3 * captions, units), BF16)],
        table,
        [d_mine, caption_col, second, slope, gains, shifts],
        text_w[4:5],
        us=15,
        passes_table=True,
    )
    d_second, d_mixed, sums_out = run(
        back_second,
        [shape((tokens, width), F32), shape((tokens, width), BF16), shape((8, width), F32)],
        [((tokens, width), F32)],
        table,
        [d_mine, d_inner, caption_col, second, gains],
        [text_w[2], text_w[1]],
    )
    if regular:
        got_in, d_mixed = tie(grid.shift(theirs_in, 3, 1), d_mixed)
        held_in, got_in, sent = grid.reduce_start(table, mine_in, got_in)
    (d_qkv,) = run(back_attention, [shape((tokens, 3 * width), BF16)], [], table, [d_mixed, qkv, probs], [])
    where = table
    mine_qkv, theirs_qkv = run(
        functools.partial(back_weights, devices),
        [shape((half, 4 * width), BF16), shape((half, 4 * width), BF16)],
        [((half, tokens), BF16)] * 4,
        where,
        [text_tokens, d_second, d_qkv, mixed, gains, shifts],
        [],
        us=5,
        passes_table=True,
    )
    where = after(table, mine_qkv)
    if regular:
        *got_in, mine_qkv, theirs_qkv = tie(*got_in, mine_qkv, theirs_qkv)
        got_qkv = grid.shift(theirs_qkv, 3, 1)
        held_in, got_in, sent = grid.reduce_next(table, held_in, got_in)
    if regular:
        held_qkv, got_qkv, sent = grid.reduce_start(table, mine_qkv, got_qkv)
        where = after(table, *sent)
    text_grad, sums_qkv = run(
        back_outer,
        [shape((tokens, width), F32), shape((8, width), F32)],
        [((tokens, width), F32)],
        where,
        [text_tokens, d_second, d_qkv, gains],
        text_w[:1],
        us=5,
    )
    (sums,) = run(
        pack_sums, [shape((devices, 384), F32)], [], table, [sums_qkv, sums_out, sums_in], [], us=2
    )
    if not regular:
        sums = lax.all_to_all(sums, "blk", 0, 0, tiled=True)
    if regular:
        text_grad, sums, *got_in = tie(text_grad, sums, *got_in)
        kept_in, got_in = grid.reduce_line(table, held_in, got_in)
        kept_in, *got_qkv = tie(kept_in, *got_qkv)
        held_qkv, got_qkv, sent = grid.reduce_next(table, held_qkv, got_qkv)
        sums = lax.all_to_all(sums, "blk", 0, 0, tiled=True)
        kept_qkv, got_qkv = grid.reduce_line(table, held_qkv, got_qkv)
        sums, *got_in = tie(sums, *got_in)
        (grad_in,) = grid.reduce_end(table, kept_in, got_in, [units])
        grad_qkv, grad_out = grid.reduce_end(table, kept_qkv, got_qkv, [3 * width, width])
    else:
        grad_in = reduce_grads(grid, mine_in, theirs_in, width)
        grad_qkv = reduce_grads(grid, mine_qkv, theirs_qkv, width)
        grad_qkv, grad_out = grad_qkv[:, : 3 * width], grad_qkv[:, 3 * width :]
    sums = jnp.sum(sums, axis=0)
    return (
        pair_loss,
        text_out,
        text_grad,
        sums[: vec[0]],
        sums[128 : 128 + vec[1]],
        grad_qkv,
        grad_out,
        grad_in,
        grad_down,
        sums[256 : 256 + vec[2]],
        grad_proj,
    )


def copy_weight(weight, out):
    out[...] = weight()[...]


def axis_sizes(mesh):
    devices = list(mesh.devices.flat)
    places = [(*d.coords, d.core_on_chip) for d in devices]
    sizes = []
    stride = len(devices)
    left = [0, 1, 2, 3]
    while stride > 1 and left:
        for axis in left:
            size = 1 + max(p[axis] for p in places) - min(p[axis] for p in places)
            step = stride // size
            if size > 1 and all(
                p[axis] - places[0][axis] == (i // step) % size for i, p in enumerate(places)
            ):
                sizes.append(size)
                left.remove(axis)
                stride = step
                break
        else:
            return [len(devices)]
    return sizes


def solution(mesh):
    grid = Grid(mesh.shape["blk"], axis_sizes(mesh))
    row = P("blk", None)
    flat = P("blk")
    tower = (flat, flat, row, row, row, row, flat, row)

    def body(*args):
        return on_device(grid, *args)

    return jax.shard_map(
        body,
        mesh=mesh,
        in_specs=(row, row, flat, row, P()) + tower + tower,
        out_specs=(flat, row, row, flat, flat, row, row, row, row, flat, row),
        check_vma=False,
    )
```

```python
import functools

import jax
import jax.numpy as jnp
from jax import lax
from jax.experimental import pallas as pl
from jax.experimental.pallas import tpu as pltpu
from jax.sharding import PartitionSpec as P

HEAD = 64
PATCHES = 50
CAPS = 4
TILE = 512
GROUP_PAD = 112

F32 = jnp.float32
BF16 = jnp.bfloat16


def gelu(z):
    return 0.5 * z * (1.0 + jnp.tanh(0.7978845608028654 * (z + 0.044715 * z * z * z)))


def normalize(x):
    mean = jnp.mean(x, axis=-1, keepdims=True)
    cent = x - mean
    rstd = lax.rsqrt(jnp.mean(cent * cent, axis=-1, keepdims=True) + 1e-06)
    return (cent * rstd, rstd)


def norm_back(grad, normed, rstd):
    return rstd * (
        grad
        - jnp.mean(grad, axis=-1, keepdims=True)
        - normed * jnp.mean(grad * normed, axis=-1, keepdims=True)
    )


def unit_rows(proj):
    factor = lax.rsqrt(jnp.sum(proj * proj, axis=-1, keepdims=True) + 1e-06)
    return (proj * factor, factor)


def matmul(left, right):
    return jnp.dot(left, right, preferred_element_type=F32)


def dot_nt(left, right):
    return lax.dot_general(left, right, (((1,), (1,)), ((), ())), preferred_element_type=F32)


def dot_tn(left, right):
    return lax.dot_general(left, right, (((0,), (0,)), ((), ())), preferred_element_type=F32)


def chunks(total, size, unroll=True):
    def wrap(body):
        @pl.loop(0, total // size, unroll=unroll)
        def step(j):
            body(pl.ds(pl.multiple_of(j * size, size), size))

    return wrap


def thirds(value):
    high = value.astype(BF16)
    rest = value - high.astype(F32)
    mid = rest.astype(BF16)
    return high, mid, (rest - mid.astype(F32)).astype(BF16)


def norm_rows(x, gain, shift):
    normed, rstd = normalize(x)
    return (normed * gain + shift).astype(BF16)


def head_masks(dtype, value):
    lane = lax.broadcasted_iota(jnp.int32, (1, 2 * HEAD), 1)
    first = jnp.where(lane < HEAD, value, 0.0).astype(dtype)
    second = jnp.where(lane < HEAD, 0.0, value).astype(dtype)
    return first, second


def both_heads(block, masks):
    return jnp.concatenate([block * masks[0], block * masks[1]], axis=0)


def merge_heads(stacked):
    half = stacked.shape[0] // 2
    lane = lax.broadcasted_iota(jnp.int32, (1, 2 * HEAD), 1)
    return jnp.where(lane < HEAD, stacked[:half], stacked[half:])


def softmax_unit(query, keys, mask, masks):
    scores = dot_nt(both_heads(query, masks), keys)
    scores = jnp.where(mask, scores, -1000000000.0)
    top = jnp.max(scores, axis=-1, keepdims=True)
    expo = jnp.exp(scores - top)
    return expo * (1.0 / jnp.sum(expo, axis=-1, keepdims=True))


def image_attention(x, gains, shifts, w_qkv, w_out, second, act, qkv, mixed):
    rows, width = x.shape
    group = GROUP_PAD

    @chunks(rows, group)
    def _(at):
        act[at, :] = norm_rows(x[at, :].astype(F32), gains[0:1, :], shifts[0:1, :])

    w_qkv = w_qkv()

    @chunks(3 * width, 256)
    def _(at):
        qkv[:, at] = matmul(act[...], w_qkv[:, at]).astype(BF16)

    masks = head_masks(BF16, 0.125)
    own = lax.broadcasted_iota(jnp.int32, (2 * group, group), 0)
    own = jnp.where(own >= group, own - group, own)
    other = lax.broadcasted_iota(jnp.int32, (2 * group, group), 1)
    mask = picture(own) == picture(other)

    @chunks(rows, group, 2)
    def _(at):
        for start in range(0, width, 2 * HEAD):
            cols = slice(start, start + 2 * HEAD)
            keys = qkv[at, width + start : width + start + 2 * HEAD]
            values = qkv[at, 2 * width + start : 2 * width + start + 2 * HEAD]
            probs = softmax_unit(qkv[at, cols], keys, mask, masks)
            mixed[at, cols] = merge_heads(matmul(probs.astype(BF16), values)).astype(BF16)

    w_out = w_out()

    @chunks(width, 256)
    def _(at):
        second[:, at] = x[:, at].astype(F32) + matmul(mixed[...], w_out[:, at])


def picture(place):
    return jnp.where(place >= PATCHES, 1, 0) + jnp.where(place >= 2 * PATCHES, 1, 0)


def image_pool(value):
    value = value.reshape(-1, GROUP_PAD, value.shape[1])
    which = picture(lax.broadcasted_iota(jnp.int32, (1, GROUP_PAD, 1), 1))
    parts = [jnp.sum(jnp.where(which == kind, value, 0.0), axis=1) for kind in range(2)]
    return jnp.concatenate(parts, axis=0) * (1.0 / PATCHES)


def image_inner(second, gains, shifts, biases, w_in, pooled, pooled_second, act):
    rows, width = second.shape
    units = pooled.shape[1]

    @chunks(rows, GROUP_PAD)
    def _(at):
        act[at, :] = norm_rows(second[at, :], gains[1:2, :], shifts[1:2, :])

    for start in range(0, width, 256):
        pooled_second[:, start : start + 256] = image_pool(second[:, start : start + 256])
    w_in = w_in()

    @chunks(units, 256)
    def _(at):
        hidden = gelu(matmul(act[...], w_in[:, at]) + biases[:, at]).astype(BF16).astype(F32)
        pooled[:, at] = image_pool(hidden)


def image_embed(pooled, pooled_second, biases, w_down, w_proj, emb):
    images, units = pooled.shape
    high, mid, unused = thirds(pooled[...])
    w_down = w_down()
    y = matmul(jnp.concatenate([high, mid], axis=0), w_down[...])
    y = y[:images] + y[images:] + pooled_second[...] + biases[:, units:]
    unit = unit_rows(matmul(y.astype(BF16), w_proj()[...]))[0].astype(BF16)
    to = lax.broadcasted_iota(jnp.int32, (images, images), 0)
    source = lax.broadcasted_iota(jnp.int32, (images, images), 1)
    half = images // 2
    order = (jnp.where(source >= half, 2 * (source - half) + 1, 2 * source) == to).astype(BF16)
    emb[...] = matmul(order, unit).astype(BF16)


def text_attention(x, caption_col, caption_row, gains, shifts, w_qkv, w_out, qkv, probs, mixed, second, act):
    rows, width = x.shape
    group = 2 * HEAD
    act[...] = norm_rows(x[...].astype(F32), gains[0:1, :], shifts[0:1, :])
    w_qkv = w_qkv()

    @chunks(3 * width, 256)
    def _(at):
        qkv[:, at] = matmul(act[...], w_qkv[:, at]).astype(BF16)

    masks = head_masks(BF16, 0.125)
    unit = 0
    for top in range(0, rows, group):
        at = slice(top, top + group)
        same = caption_col[at, :] == caption_row[:, at]
        mask = jnp.concatenate([same, same], axis=0)
        for start in range(0, width, 2 * HEAD):
            cols = slice(start, start + 2 * HEAD)
            keys = qkv[at, width + start : width + start + 2 * HEAD]
            values = qkv[at, 2 * width + start : 2 * width + start + 2 * HEAD]
            prob = softmax_unit(qkv[at, cols], keys, mask, masks)
            probs[unit] = prob
            unit += 1
            mixed[at, cols] = merge_heads(matmul(prob.astype(BF16), values)).astype(BF16)

    w_out = w_out()

    @chunks(width, 256)
    def _(at):
        second[:, at] = x[:, at].astype(F32) + matmul(mixed[...], w_out[:, at])


def caption_member(caption_row, captions):
    index = lax.broadcasted_iota(jnp.int32, (captions, caption_row.shape[1]), 0)
    return (index == caption_row[...]).astype(F32)


def text_inner(second, caption_row, gains, shifts, biases, w_in, hidden, slope, hidden_sum, act):
    units = hidden.shape[1]
    act[...] = norm_rows(second[...], gains[1:2, :], shifts[1:2, :])
    low = caption_member(caption_row, hidden_sum.shape[0]).astype(BF16)
    w_in = w_in()

    @chunks(units, 256)
    def _(at):
        z = matmul(act[...], w_in[:, at]) + biases[:, at]
        inside = jnp.tanh(0.7978845608028654 * (z + 0.044715 * z * z * z))
        value = (0.5 * z * (1.0 + inside)).astype(BF16)
        hidden[:, at] = value
        slope[:, at] = 0.5 * (1.0 + inside) + 0.5 * z * (1.0 - inside * inside) * (
            0.7978845608028654 * (1.0 + 3.0 * 0.044715 * z * z)
        )
        hidden_sum[:, at] = matmul(low, value).astype(BF16)


def text_outer(second, hidden, caption_row, biases, w_down, out, pool_low):
    width = second.shape[1]
    units = hidden.shape[1]
    member = caption_member(caption_row, pool_low.shape[0])
    low = member.astype(BF16)
    count = jnp.sum(member, axis=1, keepdims=True)
    w_down = w_down()

    @chunks(width, 256)
    def _(at):
        outer = biases[:, pl.ds(pl.multiple_of(units + at.start, 256), 256)]
        y = second[:, at] + matmul(hidden[...], w_down[:, at]) + outer
        out[:, at] = y.astype(BF16)
        total = sum(matmul(low, part) for part in thirds(y))
        pool_low[:, at] = (total / count).astype(BF16)


def head_kernel(
    table, scale_ref, pool_all, image_emb, pair_col, count, hidden_sum, pool_cols, w_proj,
    loss, d_mine, grad_proj, grad_down,
):
    scale = scale_ref[0]
    captions = d_mine.shape[0]
    w_proj = w_proj()
    proj = matmul(pool_all[...], w_proj[...])
    unit, factor = unit_rows(proj)
    sim = scale * dot_nt(unit.astype(BF16), image_emb[...])
    row_max = jnp.max(sim, axis=1, keepdims=True)
    row_lse = row_max + jnp.log(jnp.sum(jnp.exp(sim - row_max), axis=1, keepdims=True))
    col_max = jnp.max(sim, axis=0, keepdims=True)
    col_lse = col_max + jnp.log(jnp.sum(jnp.exp(sim - col_max), axis=0, keepdims=True))
    hit = pair_col[...] == lax.broadcasted_iota(jnp.int32, sim.shape, 1)
    both = 0.5 * jnp.exp(sim - row_lse) + 0.5 * jnp.exp(sim - col_lse)
    weights_sim = jnp.where(hit, both - 1.0, both).astype(BF16)
    pos = jnp.sum(jnp.where(hit, sim, 0.0), axis=1, keepdims=True)
    pair_lse = jnp.sum(jnp.where(hit, col_lse, 0.0), axis=1, keepdims=True)
    loss[...] = 0.5 * (row_lse - pos) + 0.5 * (pair_lse - pos)
    d_emb = scale * matmul(weights_sim, image_emb[...])
    inside = jnp.sum(d_emb * proj, axis=-1, keepdims=True)
    d_proj = (factor * d_emb - proj * (factor * factor * factor * inside)).astype(BF16)
    grad_proj[...] = dot_tn(pool_cols[...], d_proj)
    d_each = dot_nt(d_proj, w_proj[...]) / count[...]
    d_low = d_each.astype(BF16)
    grad_down[...] = dot_tn(hidden_sum[...], d_low)
    first = table[PLACE] * captions
    index = lax.broadcasted_iota(jnp.int32, (captions, d_each.shape[0]), 1)
    pick = (index == first + lax.broadcasted_iota(jnp.int32, (captions, d_each.shape[0]), 0)).astype(BF16)
    d_mine[...] = sum(matmul(pick, part) for part in thirds(d_each))


def text_front(
    x, caption_col, caption_row, gains, shifts, biases, w_qkv, w_out, w_in,
    qkv, probs, mixed, second, hidden, slope, hidden_sum, act,
):
    text_attention(x, caption_col, caption_row, gains, shifts, w_qkv, w_out, qkv, probs, mixed, second, act)
    text_inner(second, caption_row, gains, shifts, biases, w_in, hidden, slope, hidden_sum, act)


def image_rest(second, gains, shifts, biases, w_in, w_down, w_proj, emb, act, pooled, pooled_second):
    image_inner(second, gains, shifts, biases, w_in, pooled, pooled_second, act)
    image_embed(pooled, pooled_second, biases, w_down, w_proj, emb)


def pack_sums(sums_qkv, sums_out, sums_in, out):
    devices, width = out.shape[0], sums_out.shape[1]
    first, second = sums_qkv[...], sums_out[...]
    vectors = [
        jnp.concatenate([first[0:1], second[1:2]], axis=1),
        jnp.concatenate([first[1:2], second[2:3]], axis=1),
        jnp.concatenate([sums_in[...], second[0:1]], axis=1),
    ]
    for i, vector in enumerate(vectors):
        total = vector.shape[1]
        share = total // devices
        row = lax.broadcasted_iota(jnp.int32, (devices, total), 0)
        place = lax.broadcasted_iota(jnp.int32, (devices, total), 1) - row * share
        mine = jnp.where(place >= 0, jnp.where(place < share, vector, 0.0), 0.0)
        to = lax.broadcasted_iota(jnp.int32, (total, 128), 1)
        source = lax.broadcasted_iota(jnp.int32, (total, 128), 0)
        pick = (lax.rem(source, share) == to).astype(BF16)
        out[:, i * 128 : (i + 1) * 128] = sum(matmul(part, pick) for part in thirds(mine))


def core_split(table, value, devices, mine, theirs):
    own = value.shape[0] // devices
    value = value.reshape(devices // 2, 2, own, value.shape[1])
    first = table[CORE] == 0
    even = value[:, 0].reshape(-1, value.shape[3])
    odd = value[:, 1].reshape(-1, value.shape[3])
    mine[...] = jnp.where(first, even, odd).astype(BF16)
    theirs[...] = jnp.where(first, odd, even).astype(BF16)


def token_member(caption_col, captions):
    index = lax.broadcasted_iota(jnp.int32, (caption_col.shape[0], 3 * captions), 1)
    index = jnp.where(index >= captions, index - captions, index)
    index = jnp.where(index >= captions, index - captions, index)
    return (caption_col[...] == index).astype(BF16)


def back_inner(
    devices, table, each, caption_col, second, slope, gains, shifts, w_down,
    mine, theirs, d_inner, sums, act_t, act_u, both,
):
    rows, width = second.shape
    units = slope.shape[1]
    captions = each.shape[0]
    member = token_member(caption_col, captions)
    normed, rstd = normalize(second[...])
    act = normed * gains[1:2, :] + shifts[1:2, :]
    core_split(table, act.T, devices, act_t, act_u)
    each_low = each[...].astype(BF16)
    w_down = w_down()

    @chunks(units, 256)
    def _(at):
        both[:, at] = jnp.concatenate(thirds(dot_nt(each_low, w_down[at, :])), axis=0)

    @chunks(units, 256)
    def _(at):
        low = (matmul(member, both[:, at]) * slope[:, at]).astype(BF16)
        d_inner[:, at] = low
        sums[:, at] = jnp.sum(low.astype(F32), axis=0, keepdims=True)
        theirs[:, at] = matmul(act_u[...], low).astype(BF16)
        mine[:, at] = matmul(act_t[...], low).astype(BF16)


def back_second(each, d_inner, caption_col, second, gains, w_in, w_out, d_second, d_mixed, sums, d_act):
    width = second.shape[1]
    normed, rstd = normalize(second[...])
    d_y = matmul(token_member(caption_col, each.shape[0]), jnp.concatenate(thirds(each[...]), axis=0))
    sums[0:1, :] = jnp.sum(d_y, axis=0, keepdims=True)
    w_in = w_in()

    @chunks(width, 256)
    def _(at):
        d_act[:, at] = dot_nt(d_inner[...], w_in[at, :])

    grad = d_act[...]
    sums[1:2, :] = jnp.sum(grad * normed, axis=0, keepdims=True)
    sums[2:3, :] = jnp.sum(grad, axis=0, keepdims=True)
    d_two = d_y + norm_back(grad * gains[1:2, :], normed, rstd)
    d_second[...] = d_two
    d_mixed[...] = dot_nt(d_two.astype(BF16), w_out()[...]).astype(BF16)


def back_attention(d_mixed, qkv, probs, d_qkv):
    rows, width = d_mixed.shape
    group = 2 * HEAD
    ones = head_masks(BF16, 1.0)
    masks = head_masks(BF16, 0.125)
    unit = 0
    for top in range(0, rows, group):
        at = slice(top, top + group)
        for start in range(0, width, 2 * HEAD):
            cols = slice(start, start + 2 * HEAD)
            key_cols = slice(width + start, width + start + 2 * HEAD)
            value_cols = slice(2 * width + start, 2 * width + start + 2 * HEAD)
            prob = probs[unit]
            unit += 1
            d_out = both_heads(d_mixed[at, cols], ones)
            query = both_heads(qkv[at, cols], masks)
            d_qkv[at, value_cols] = dot_tn(prob.astype(BF16), d_out).astype(BF16)
            d_prob = dot_nt(d_out, qkv[at, value_cols])
            d_score = (prob * (d_prob - jnp.sum(prob * d_prob, axis=-1, keepdims=True))).astype(BF16)
            d_qkv[at, cols] = (0.125 * merge_heads(matmul(d_score, qkv[at, key_cols]))).astype(BF16)
            d_qkv[at, key_cols] = dot_tn(d_score, query).astype(BF16)


def back_weights(
    devices, table, x, d_second, d_qkv, mixed, gains, shifts,
    mine, theirs, act_t, act_u, mixed_t, mixed_u,
):
    width = x.shape[1]
    core_split(table, norm_rows(x[...].astype(F32), gains[0:1, :], shifts[0:1, :]).astype(F32).T, devices, act_t, act_u)
    core_split(table, mixed[...].astype(F32).T, devices, mixed_t, mixed_u)
    d_low = d_second[...].astype(BF16)
    for start in range(0, width, 256):
        at = slice(start, start + 256)
        to = slice(3 * width + start, 3 * width + start + 256)
        theirs[:, to] = matmul(mixed_u[...], d_low[:, at]).astype(BF16)
        mine[:, to] = matmul(mixed_t[...], d_low[:, at]).astype(BF16)

    @chunks(3 * width, 256)
    def _(at):
        theirs[:, at] = matmul(act_u[...], d_qkv[:, at]).astype(BF16)
        mine[:, at] = matmul(act_t[...], d_qkv[:, at]).astype(BF16)


def back_outer(x, d_second, d_qkv, gains, w_qkv, text_grad, sums, d_act):
    width = x.shape[1]
    normed, rstd = normalize(x[...].astype(F32))
    w_qkv = w_qkv()

    @chunks(width, 256)
    def _(at):
        d_act[:, at] = dot_nt(d_qkv[...], w_qkv[at, :])

    grad = d_act[...]
    sums[0:1, :] = jnp.sum(grad * normed, axis=0, keepdims=True)
    sums[1:2, :] = jnp.sum(grad, axis=0, keepdims=True)
    text_grad[...] = d_second[...] + norm_back(grad * gains[0:1, :], normed, rstd)


class Weight:
    def __init__(self, rows, cols):
        self.dims = (rows, cols)
        self.parts = []

    def add(self, array, lead, start, width, row=None, unit=0, below=0, col=None, beside=0):
        self.parts.append((array, lead, start, width, row, unit, below, col, beside))


def run(kernel, outs, scratch, table, operands, weights, us=5, passes_table=False, scalars=()):
    arrays = []
    for weight in weights:
        for part in weight.parts:
            if not any(part[0] is a for a in arrays):
                arrays.append(part[0])
    places = {id(a): i for i, a in enumerate(arrays)}
    n_s, n_op, n_arr, n_out, n_w = len(scalars), len(operands), len(arrays), len(outs), len(weights)

    def body(*refs):
        table_ref, refs = refs[0], refs[1:]
        ops, refs = refs[: n_s + n_op], refs[n_s + n_op :]
        arrs, refs = refs[:n_arr], refs[n_arr:]
        out, refs = refs[:n_out], refs[n_out:]
        held, refs = refs[:n_w], refs[n_w:]
        if n_w:
            sems, refs = refs[0], refs[1:]
        waits = []
        for i, weight in enumerate(weights):
            for array, lead, start, width, row, unit, below, col, beside in weight.parts:
                at = 0 if row is None else pl.multiple_of(table_ref[row] * unit + below, 16)
                to = beside
                if col is not None:
                    to = pl.multiple_of(table_ref[col] * (weight.dims[1] // 2) + beside, 128)
                pltpu.make_async_copy(
                    arrs[places[id(array)]].at[lead, :, pl.ds(start, width)],
                    held[i].at[pl.ds(at, array.shape[1]), pl.ds(to, width)],
                    sems.at[i],
                ).start()

            def wait(i=i):
                pltpu.make_async_copy(held[i], held[i], sems.at[i]).wait()
                return held[i]

            waits.append(wait)
        if passes_table:
            ops = (table_ref, *ops)
        kernel(*ops, *waits, *out, *refs)

    vmem = pl.BlockSpec(memory_space=pltpu.VMEM)
    return pl.pallas_call(
        body,
        out_shape=outs,
        in_specs=[pl.BlockSpec(memory_space=pltpu.SMEM)] * (1 + n_s) + [vmem] * n_op + [pl.BlockSpec(memory_space=pltpu.HBM)] * n_arr,
        out_specs=[vmem] * n_out,
        scratch_shapes=[pltpu.VMEM(w.dims, BF16) for w in weights]
        + ([pltpu.SemaphoreType.DMA((n_w,))] if n_w else [])
        + [pltpu.VMEM(*s) for s in scratch],
        compiler_params=pltpu.CompilerParams(vmem_limit_bytes=60 << 20),
        cost_estimate=pl.CostEstimate(flops=us * 2000000000, bytes_accessed=1000, transcendentals=0),
    )(table, *scalars, *operands, *arrays)


def shape(dims, dtype):
    return jax.ShapeDtypeStruct(dims, dtype)


class Grid:
    def __init__(self, devices, sizes):
        self.devices = devices
        self.sizes = sizes
        strides = []
        step = devices
        for size in sizes:
            step //= size
            strides.append(step)
        self.strides = strides
        self.regular = len(sizes) == 4 and sizes[1:] == [2, 2, 2]

    def place(self):
        index = lax.axis_index("blk")
        return [(index // st) % size for size, st in zip(self.sizes, self.strides)]

    def shift(self, value, axis, step):
        size, stride = self.sizes[axis], self.strides[axis]
        pairs = []
        for i in range(self.devices):
            at = (i // stride) % size
            pairs.append((i, i + ((at + step) % size - at) * stride))
        return lax.ppermute(value, "blk", pairs)

    def table(self):
        if len(self.sizes) != 4:
            index = lax.axis_index("blk")
            return jnp.stack([index % 2, 1 - index % 2, index]).astype(jnp.int32)
        place = self.place()
        chips = []
        for offset in self.offsets():
            origin = [
                d[1] if isinstance(d, tuple) else (p - d) % s for p, d, s in zip(place, offset, self.sizes)
            ]
            chips.append(sum(o * st for o, st in zip(origin, self.strides)) // 2)
        chips = jnp.stack(chips)
        core = place[3]
        return jnp.concatenate(
            [jnp.stack([core, 1 - core, lax.axis_index("blk"), *place[:3]]), chips, 2 * chips + core, 2 * chips + 1 - core]
        ).astype(jnp.int32)

    def offsets(self):
        z, y, x, unused = self.sizes
        zs = list(range(z)) + [("z", i) for i in range(z)]
        return [(dz, dy, dx) for dz in zs for dy in range(y) for dx in range(x)]

    def row_of(self, offset, kind):
        count = len(self.offsets())
        return FIRST_ROW + self.offsets().index(offset) + {"chip": 0, "own": count, "other": 2 * count}[kind]

    def line(self, value):
        return [value] + [self.shift(value, 0, k) for k in range(1, self.sizes[0])]

    def square(self, line):
        return self.shift(line, 2, 1), self.shift(line, 1, 1)

    def along_z(self, value):
        depth = self.sizes[0]
        groups = [[i + k * self.strides[0] for k in range(depth)] for i in range(self.strides[0])]
        return lax.all_to_all(
            jnp.broadcast_to(value[None], (depth, *value.shape)), "blk", 0, 0, axis_index_groups=groups
        )

    def across(self, *arrays):
        return [self.shift(a, 3, 1) for a in arrays]

    def parts(self, value):
        return value.reshape(*self.sizes[:3], -1, value.shape[1])

    def reduce_start(self, table, mine, got):
        mine, got = self.parts(mine), self.parts(got)
        depth, unused, unused, rows, cols = mine.shape
        sent = shape((depth, 2, rows, cols // 2), BF16)
        held = [((depth, 2, rows, cols // 2), BF16)] * 4
        to_x, to_y = fetching(sum_cores, [sent, sent], held, table, [mine, got])
        return (mine, got), (self.shift(to_x, 2, 1), self.shift(to_y, 1, 1)), (to_x, to_y)

    def reduce_next(self, table, held, came):
        depth, unused, unused, rows, cols = held[0].shape
        sent = shape((depth, rows, cols // 2), BF16)
        scratch = [((depth, rows, cols // 2), BF16)] * 6
        to_y, to_x = fetching(sum_sides, [sent, sent], scratch, table, [*held, *came])
        return (*held, *came), (self.shift(to_y, 1, 1), self.shift(to_x, 2, 1)), (to_y, to_x)

    def reduce_line(self, table, held, came):
        depth, unused, unused, rows, cols = held[0].shape
        sent = shape((rows, cols), BF16)
        scratch = [((depth, rows, cols // 2), BF16)] * 8
        outs = [shape((rows, cols), F32)] + [sent] * (depth - 1)
        kept, *to = fetching(sum_corner, outs, scratch, table, [*held, *came])
        return kept, [self.shift(value, 0, k) for k, value in enumerate(to, 1)]

    def reduce_end(self, table, kept, came, widths):
        kernel = functools.partial(sum_line, len(came))
        return run(kernel, [shape((kept.shape[0], w), F32) for w in widths], [], table, [kept, *came], [], us=1)


def wide(*values):
    return sum(v.astype(F32) for v in values)


def fetching(kernel, outs, scratch, table, arrays):
    count, n_out = len(arrays), len(outs)

    def body(*refs):
        table_ref, refs = refs[0], refs[1:]
        arrs, out, held, sems = refs[:count], refs[count : count + n_out], refs[count + n_out : -1], refs[-1]
        steps = kernel(table_ref, *arrs, *out)
        copies = [pltpu.make_async_copy(s, h, sems.at[i]) for i, (s, h) in enumerate(zip(next(steps), held))]
        for copy in copies:
            copy.start()
        for copy in copies:
            copy.wait()
        steps.send(held)

    vmem = pl.BlockSpec(memory_space=pltpu.VMEM)
    return pl.pallas_call(
        body,
        out_shape=outs,
        in_specs=[pl.BlockSpec(memory_space=pltpu.SMEM)] + [pl.BlockSpec(memory_space=pltpu.HBM)] * count,
        out_specs=[vmem] * n_out,
        scratch_shapes=[pltpu.VMEM(*s) for s in scratch] + [pltpu.SemaphoreType.DMA((len(scratch),))],
        compiler_params=pltpu.CompilerParams(vmem_limit_bytes=60 << 20),
        cost_estimate=pl.CostEstimate(flops=1000, bytes_accessed=1000, transcendentals=0),
    )(table, *arrays)


def sum_cores(table, mine, got, to_x, to_y):
    half = to_x.shape[3]
    other_y, other_x = 1 - table[AT_Y], 1 - table[AT_X]
    left, right = pl.ds(0, half), pl.ds(half, half)
    held = yield [
        mine.at[:, :, other_x, :, left],
        got.at[:, :, other_x, :, left],
        mine.at[:, other_y, :, :, right],
        got.at[:, other_y, :, :, right],
    ]
    for z in range(mine.shape[0]):
        for i in range(2):
            to_x[z, i] = wide(held[0][z, i], held[1][z, i]).astype(BF16)
            to_y[z, i] = wide(held[2][z, i], held[3][z, i]).astype(BF16)
    yield


def sum_sides(table, mine, got, by_x, by_y, to_y, to_x):
    half = to_x.shape[2]
    y, x = table[AT_Y], table[AT_X]
    left, right = pl.ds(0, half), pl.ds(half, half)
    held = yield [
        mine.at[:, 1 - y, x, :, left],
        got.at[:, 1 - y, x, :, left],
        by_x.at[:, 1 - y],
        mine.at[:, y, 1 - x, :, right],
        got.at[:, y, 1 - x, :, right],
        by_y.at[:, 1 - x],
    ]
    for z in range(mine.shape[0]):
        to_y[z] = wide(*[h[z] for h in held[:3]]).astype(BF16)
        to_x[z] = wide(*[h[z] for h in held[3:]]).astype(BF16)
    yield


def sum_corner(table, mine, got, by_x, by_y, left_by_y, right_by_x, kept, *to):
    depth = mine.shape[0]
    half = by_x.shape[3]
    y, x = table[AT_Y], table[AT_X]
    left, right = pl.ds(0, half), pl.ds(half, half)
    held = yield [
        mine.at[:, y, x, :, left],
        got.at[:, y, x, :, left],
        by_x.at[:, y],
        left_by_y,
        mine.at[:, y, x, :, right],
        got.at[:, y, x, :, right],
        by_y.at[:, x],
        right_by_x,
    ]
    for k in range(depth):
        z = lax.rem(table[AT_Z] + k, depth)
        out = to[k - 1] if k else kept
        out[:, :half] = wide(*[h[z] for h in held[:4]]).astype(out.dtype)
        out[:, half:] = wide(*[h[z] for h in held[4:]]).astype(out.dtype)
    yield


def sum_line(spans, kept, *refs):
    came = refs[:spans]
    start = 0
    for out in refs[spans:]:
        cols = slice(start, start + out.shape[1])
        start += out.shape[1]
        out[...] = kept[:, cols] + wide(*[c[:, cols] for c in came])


class Chunk:
    def __init__(self, grid, line, cut, ordered):
        self.grid, self.line, self.cut = grid, line, cut
        self.cols = line.shape[2]
        self.zs = [("z", z) if ordered else z for z in range(grid.sizes[0])]
        self.own, self.other = [], []

    def hold(self, mine, theirs, dy, dx, start, low, high):
        offsets = [(z, dy, dx) for z in self.zs]
        for pieces, array in ((self.own, mine), (self.other, theirs)):
            pieces.append((array, offsets, start, low, high))

    def halves(self, rows, cols, start):
        weight = Weight(rows, cols)
        for pieces, col in ((self.own, CORE), (self.other, OTHER)):
            for array, offsets, begin, low, high in pieces:
                left, right = max(low, start), min(high, start + cols // 2)
                if left < right:
                    for lead, offset in enumerate(offsets):
                        row = self.grid.row_of(offset, "chip")
                        at = begin + left - low
                        weight.add(array, lead, at, right - left, row, array.shape[1], 0, col, left - start)
        return weight

    def deep(self, rows, cols):
        weight = Weight(rows, cols)
        parts = self.cols // cols
        for pieces, kind in ((self.own, "own"), (self.other, "other")):
            for array, offsets, begin, low, high in pieces:
                for part in range(parts):
                    left, right = max(low, part * cols), min(high, part * cols + cols)
                    if left < right:
                        for lead, offset in enumerate(offsets):
                            row = self.grid.row_of(offset, kind)
                            high_rows = array.shape[1]
                            at = begin + left - low
                            weight.add(
                                array, lead, at, right - left, row, parts * high_rows, part * high_rows,
                                None, left - part * cols,
                            )
        return weight


def tie(*values):
    return lax.optimization_barrier(values)


def after_all(values, *earlier):
    return lax.optimization_barrier((*values, *earlier))[: len(values)]


def after(value, *earlier):
    return lax.optimization_barrier((value, *earlier))[0]


CORE = 0
OTHER = 1
PLACE = 2
AT_Z, AT_Y, AT_X = 3, 4, 5
FIRST_ROW = 6


def to_all(value, devices):
    return lax.all_to_all(jnp.broadcast_to(value[None], (devices, *value.shape)), "blk", 0, 0)


def pack_kernel(table, *refs):
    first = table[CORE] == 0
    keep, send = refs[-2:]
    start = 0
    for weight in refs[:-2]:
        half = weight.shape[1] // 2
        left, right = weight[:, :half], weight[:, half:]
        keep[:, start : start + half] = jnp.where(first, left, right)
        send[:, start : start + half] = jnp.where(first, right, left)
        start += half


def vector_pack_kernel(caption_row, pair_index, *refs):
    block, refs = refs[-1], refs[:-1]
    captions = pair_index.shape[1]
    pairs = pair_index[...].astype(F32)
    high = jnp.floor(pairs * (1.0 / 64.0))
    member = caption_member(caption_row, captions).astype(BF16)
    count = dot_nt(jnp.ones((8, caption_row.shape[1]), BF16), member)[0:1]
    rows = [r[...].astype(F32) for r in refs] + [high, pairs - 64.0 * high, count]
    rows = [jnp.concatenate([r, jnp.zeros((1, 128 - r.shape[1]), F32)], axis=1) for r in rows]
    rows.append(jnp.zeros((block.shape[0] - len(rows), 128), F32))
    block[...] = jnp.concatenate(rows, axis=0).astype(BF16)


def pair_kernel(table, keep, got, *outs):
    first = table[CORE] == 0
    start = 0
    for out in outs:
        cols = slice(start, start + out.shape[1])
        start += out.shape[1]
        one, two = keep[:, cols].astype(F32), got[:, cols].astype(F32)
        out[...] = jnp.concatenate([jnp.where(first, one, two), jnp.where(first, two, one)], axis=0).astype(BF16)


def pair_up(grid, table, groups):
    rows = groups[0][0].shape[0]
    widths = [sum(w.shape[1] for w in group) // 2 for group in groups]
    packed = shape((rows, sum(widths)), BF16)
    keep, send = run(
        pack_kernel, [packed, packed], [], table, [w for group in groups for w in group], [], us=1, passes_table=True
    )
    return run(
        pair_kernel,
        [shape((2 * rows, w), BF16) for w in widths],
        [],
        table,
        [keep, grid.shift(send, 3, 1)],
        [],
        us=1,
        passes_table=True,
    )


def copied(arrays, outs, moves):
    count = len(arrays)

    def kernel(*refs):
        sems = refs[-1]
        copies = [
            pltpu.make_async_copy(refs[a].at[source], refs[count + o].at[to], sems.at[i])
            for i, (a, source, o, to) in enumerate(moves)
        ]
        for copy in copies:
            copy.start()
        for copy in copies:
            copy.wait()

    anywhere = pl.BlockSpec(memory_space=pltpu.HBM)
    return pl.pallas_call(
        kernel,
        out_shape=outs,
        in_specs=[anywhere] * count,
        out_specs=[pl.BlockSpec(memory_space=pltpu.VMEM)] * len(outs),
        scratch_shapes=[pltpu.SemaphoreType.DMA((len(moves),))],
        cost_estimate=pl.CostEstimate(flops=1000, bytes_accessed=1000, transcendentals=0),
    )(*arrays)


def columns(start, stop):
    return (slice(None), slice(None), pl.ds(start, stop - start))


def side_operands(last, parts):
    chunk, by_x, by_y = last
    cut, end = chunk.cut, chunk.cols
    if parts is None:
        depth, rows = by_x.shape[:2]
        outs = [shape((depth, rows, end - cut), BF16), shape((depth, rows, cut), BF16)]
        moves = [(0, columns(cut, end), 0, columns(0, end - cut)), (1, columns(0, cut), 1, columns(0, cut))]
        return copied([by_y, by_x], outs, moves)
    line = None
    if len(parts) == 1:
        line = parts[0]
        depth, rows, cols = line.shape
        parts = [(0, columns(0, cols), columns(0, cols))]
        arrays = [line]
        outs = []
    else:
        arrays = list(parts)
        depth, (rows, cols) = len(parts), parts[0].shape
        outs = [shape((depth, rows, cols), BF16)]
        parts = [(i, (slice(None), slice(None)), (i, slice(None), pl.ds(0, cols))) for i in range(depth)]
    outs += [shape((depth, rows, cols + end - cut), BF16), shape((depth, rows, cols + cut), BF16)]
    count = len(arrays)
    moves = []
    for o in range(len(outs)):
        moves += [(a, source, o, to) for a, source, to in parts]
    moves.append((count, columns(cut, end), len(outs) - 2, columns(cols, cols + end - cut)))
    moves.append((count + 1, columns(0, cut), len(outs) - 1, columns(cols, cols + cut)))
    out = copied([*arrays, by_y, by_x], outs, moves)
    return out if line is None else [line, *out]


def beside(value):
    half = value.shape[0] // 2
    return jnp.concatenate([value[:half], value[half:]], axis=1)


def settle(chunk, last, mine, theirs):
    by_x, by_y = mine
    start = 0
    if chunk is not None:
        start = chunk.cols
        chunk.hold(by_x, theirs[0], 0, 1, 0, 0, chunk.cols)
        chunk.hold(by_y, theirs[1], 1, 0, 0, 0, chunk.cols)
    if last is not None:
        last.hold(by_x, theirs[0], 1, 1, start, last.cut, last.cols)
        last.hold(by_y, theirs[1], 1, 1, start, 0, last.cut)


def columns_of(whole, widths):
    weights = []
    start = 0
    array = whole[None]
    for width in widths:
        weight = Weight(whole.shape[0], width)
        weight.add(array, 0, start, width)
        weights.append(weight)
        start += width
    return weights


def gathered(part):
    full = lax.all_gather(part, "blk", axis=0, tiled=True)
    weight = Weight(*full.shape)
    weight.add(full[None], 0, 0, full.shape[1])
    return weight


def reduce_grads(grid, mine, theirs, width):
    own = width // grid.devices
    both = jnp.where(lax.axis_index("blk") % 2 == 0, jnp.stack([mine, theirs], 0), jnp.stack([theirs, mine], 0))
    both = both.reshape(2, grid.devices // 2, own, -1).transpose(1, 0, 2, 3).reshape(width, -1)
    return lax.psum_scatter(both, "blk", scatter_dimension=0, tiled=True).astype(F32)


def head_tile(proj, factor, image_emb, scale, row_lse, col_lse, pairs, sim):
    hit = pairs[:, None] == jnp.arange(image_emb.shape[0], dtype=jnp.int32)[None, :]
    weights_sim = (
        0.5 * jnp.exp(sim - row_lse[:, None]) + 0.5 * jnp.exp(sim - col_lse[None, :]) - hit.astype(F32)
    )
    d_emb = scale * matmul(weights_sim.astype(BF16), image_emb)
    d_proj = factor * d_emb - proj * (factor * factor * factor) * jnp.sum(d_emb * proj, axis=-1, keepdims=True)
    pos = jnp.sum(jnp.where(hit, sim, 0.0), axis=1)
    pair_col = jnp.sum(jnp.where(hit, col_lse[None, :], 0.0), axis=1)
    return (d_proj.astype(BF16), 0.5 * (row_lse - pos) + 0.5 * (pair_col - pos))


def head_tiled(total, captions, own, scale, pool_all, image_emb, every_pair, every_count, hidden_sum, w_proj):
    device = lax.axis_index("blk")
    col_max = jnp.full((total,), -1e30, F32)
    col_sum = jnp.zeros((total,), F32)
    held = []
    for start in range(0, total, TILE):
        proj = matmul(pool_all[start : start + TILE], w_proj)
        unit, factor = unit_rows(proj)
        sim = scale * dot_nt(unit.astype(BF16), image_emb)
        top = jnp.max(sim, axis=1)
        row_lse = top + jnp.log(jnp.sum(jnp.exp(sim - top[:, None]), axis=1))
        new_max = jnp.maximum(col_max, jnp.max(sim, axis=0))
        col_sum = col_sum * jnp.exp(col_max - new_max) + jnp.sum(jnp.exp(sim - new_max[None, :]), axis=0)
        col_max = new_max
        held.append((proj, factor, row_lse, sim))
    col_lse = col_max + jnp.log(col_sum)
    d_proj = []
    losses = []
    for start, (proj, factor, row_lse, sim) in zip(range(0, total, TILE), held):
        grad, loss = head_tile(
            proj, factor, image_emb, scale, row_lse, col_lse, every_pair[start : start + TILE], sim
        )
        d_proj.append(grad)
        losses.append(loss)
    d_proj = jnp.concatenate(d_proj)
    pair_loss = lax.dynamic_slice_in_dim(jnp.concatenate(losses), device * captions, captions)
    grad_proj = dot_tn(lax.dynamic_slice_in_dim(pool_all, device * own, own, axis=1), d_proj)
    d_each = dot_nt(d_proj, w_proj) / every_count[:, None]
    grad_down = dot_tn(hidden_sum, d_each.astype(BF16))
    d_mine = lax.dynamic_slice_in_dim(d_each, device * captions, captions)

    return pair_loss, d_mine, grad_proj, grad_down


def unpack_vectors(block, sizes, width):
    block = block.astype(F32)
    parts = [block[:, i, :size].reshape(-1) for i, size in enumerate(sizes)]
    pairs = parts[6].astype(jnp.int32) * 64 + parts[7].astype(jnp.int32)
    shapes = ((2, width), (2, width), (1, -1), (2, width), (2, width), (1, -1))
    vectors = [part.reshape(dims) for part, dims in zip(parts, shapes)]
    return [*vectors, pairs[:, None], parts[8][:, None]]


def on_device(grid, *args):
    (
        text_tokens,
        segment_ids,
        pair_index,
        image_tokens,
        logit_scale,
        img_gains,
        img_shifts,
        img_qkv,
        img_out,
        img_in,
        img_down,
        img_biases,
        img_proj,
        txt_gains,
        txt_shifts,
        txt_qkv,
        txt_out,
        txt_in,
        txt_down,
        txt_biases,
        txt_proj,
    ) = args
    devices = grid.devices
    width = text_tokens.shape[1]
    units = img_in.shape[1]
    scale = logit_scale[0]
    rows, length = segment_ids.shape
    tokens = rows * length
    captions = pair_index.shape[0]
    images = image_tokens.shape[0] // PATCHES
    device = lax.axis_index("blk")
    own = width // devices
    table = grid.table()

    caption_of = (jnp.arange(rows, dtype=jnp.int32)[:, None] * CAPS + segment_ids).reshape(tokens)
    caption_col, caption_row = caption_of[:, None], caption_of[None, :]
    member = (jnp.arange(captions, dtype=jnp.int32)[:, None] == caption_row).astype(F32)

    vec = (img_gains.shape[0], img_shifts.shape[0], img_biases.shape[0])
    vectors = [img_gains, img_shifts, img_biases, txt_gains, txt_shifts, txt_biases]
    (block,) = run(
        vector_pack_kernel,
        [shape((16, 128), BF16)],
        [],
        table,
        [caption_row, pair_index[None], *[v[None] for v in vectors]],
        [],
        us=1,
    )
    block = to_all(block, devices)
    pairs = images // 2
    padded = pairs * GROUP_PAD
    x_image = jnp.pad(
        image_tokens.reshape(pairs, 2 * PATCHES, width), ((0, 0), (0, GROUP_PAD - 2 * PATCHES), (0, 0))
    ).reshape(padded, width)
    regular = grid.regular and own % 8 == 0
    text_parts = [txt_qkv, txt_out, txt_in, txt_proj]
    if regular:
        line0 = grid.line(beside(img_down))
        pair1, pair2 = pair_up(grid, table, [[img_qkv, img_out], [img_in, img_proj]])
        *line0, pair1, pair2 = tie(*line0, pair1, pair2)

        chunk0 = Chunk(grid, jnp.stack(line0), width, False)
        side0 = grid.square(chunk0.line)
        line1 = grid.line(pair1)
        *side0, line1[1], line1[2], line1[3], block = tie(*side0, *line1[1:], block)
        text_all = lax.all_gather(
            after(jnp.concatenate(text_parts, axis=1), line1[1]), "blk", axis=0, tiled=True
        )
        text_w = columns_of(text_all, [w.shape[1] for w in text_parts])

        line1, *to = side_operands((chunk0, *side0), line1)
        chunk1 = Chunk(grid, line1, width, False)
        side1 = grid.shift(to[0], 2, 1), grid.shift(to[1], 1, 1)
        line2 = grid.line(pair2)
        vectors = unpack_vectors(block, vec + vec + (captions,) * 3, width)
        *side1, line2[1], line2[2], line2[3], x_image = tie(*side1, *line2[1:], x_image)

        line2, *to = side_operands((chunk1, *side1), line2)
        chunk2 = Chunk(grid, line2, 1024, False)
        side2 = grid.shift(to[0], 2, 1), grid.shift(to[1], 1, 1)
        other1 = grid.across(chunk1.line, *side1)
        line3 = grid.line(beside(txt_down))
        tied = tie(*side2, *line3[1:], *other1, *vectors)
        side2, line3, other1, vectors = tied[:2], [line3[0], *tied[2:5]], tied[5:8], tied[8:]

        to = side_operands((chunk2, *side2), None)
        side3 = grid.shift(to[0], 2, 1), grid.shift(to[1], 1, 1)
        other2 = grid.across(*after_all(side2, *to), chunk2.line)
        chunk3 = Chunk(grid, jnp.stack(line3), width, False)
        chunk1.hold(chunk1.line, other1[0], 0, 0, 0, 0, chunk1.cols)
        settle(chunk1, chunk0, side1, other1[1:])
        settle(chunk2, chunk1, side2, other2[:2])
        chunk2.hold(chunk2.line, other2[2], 0, 0, 0, 0, chunk2.cols)
        image_w = [chunk1.halves(width, 3 * width, 0), chunk1.halves(width, width, 3 * width // 2)]
        where = after(table, *to)
    else:
        image_w = [gathered(w) for w in (img_qkv, img_out, img_in, img_proj, img_down)]
        text_w = [gathered(w) for w in (*text_parts, txt_down)]
        vectors = unpack_vectors(block, vec + vec + (captions,) * 3, width)
        where = table
    img_g, img_s, img_b, gains, shifts, biases, every_pair, every_count = vectors
    image_second = run(
        image_attention,
        [shape((padded, width), F32)],
        [((padded, width), BF16), ((padded, 3 * width), BF16), ((padded, width), BF16)],
        where,
        [x_image, img_g, img_s],
        image_w[:2],
        us=19,
    )[0]
    where = table
    if regular:
        *side3, image_second = tie(*side3, image_second)
        side4 = grid.square(after(chunk3.line, image_second))
        settle(None, chunk2, side3, grid.across(*after_all(side3, chunk3.line)))
        other0 = grid.across(*after_all((chunk0.line, *side0), image_second))
        chunk0.hold(chunk0.line, other0[0], 0, 0, 0, 0, chunk0.cols)
        settle(chunk0, None, side0, other0[1:])
        image_w += [
            chunk2.halves(width, units, 0),
            chunk2.halves(width, width, units // 2),
            chunk0.deep(units, width),
        ]
        where = after(table, chunk3.line)
    (image_emb,) = run(
        image_rest,
        [shape((images, width), BF16)],
        [((padded, width), BF16), ((images, units), F32), ((images, width), F32)],
        where,
        [image_second, img_g, img_s, img_b],
        [image_w[2], image_w[4], image_w[3]],
        us=18,
    )
    if regular:
        *side4, image_emb = tie(*side4, image_emb)
        to = side_operands((chunk3, *side4), None)
        side5 = grid.shift(to[0], 2, 1), grid.shift(to[1], 1, 1)
        other4 = grid.across(*after_all(side4, *to), chunk3.line)
        settle(chunk3, None, side4, other4[:2])
        chunk3.hold(chunk3.line, other4[2], 0, 0, 0, 0, chunk3.cols)
    image_all = to_all(image_emb, devices)
    where = after(table, *to) if regular else after(table, image_emb)

    heads = tokens // (2 * HEAD) * (width // (2 * HEAD))
    qkv, probs, mixed, second, hidden, slope, hidden_sum = run(
        text_front,
        [
            shape((tokens, 3 * width), BF16),
            shape((heads, 4 * HEAD, 2 * HEAD), F32),
            shape((tokens, width), BF16),
            shape((tokens, width), F32),
            shape((tokens, units), BF16),
            shape((tokens, units), F32),
            shape((captions, units), BF16),
        ],
        [((tokens, width), BF16)],
        where,
        [text_tokens, caption_col, caption_row, gains, shifts, biases],
        text_w[:3],
        us=17,
    )
    if regular:
        *side5, second = tie(*side5, second)
        settle(None, chunk3, side5, grid.across(*side5))
        text_w.append(chunk3.deep(units, width))
    text_out, pool_low = run(
        text_outer,
        [shape((tokens, width), BF16), shape((captions, width), BF16)],
        [],
        table,
        [second, hidden, caption_row, biases],
        text_w[4:5],
        us=5,
    )
    pool_low, image_emb = tie(pool_low, image_all)
    image_emb = image_emb.reshape(-1, width)
    wide_part = units // devices
    sent = jnp.concatenate(
        [
            jnp.broadcast_to(pool_low[None], (devices, captions, width)),
            hidden_sum.reshape(captions, devices, wide_part).transpose(1, 0, 2),
        ],
        axis=2,
    )
    sent = lax.all_to_all(sent, "blk", 0, 0).reshape(-1, width + wide_part)
    pool_all, hidden_sum = sent[:, :width], sent[:, width:]
    total = pool_all.shape[0]
    if total <= TILE:
        pool_cols = lax.dynamic_slice_in_dim(pool_all, device * own, own, axis=1)
        losses, d_mine, grad_proj, grad_down = run(
            head_kernel,
            [
                shape((total, 1), F32),
                shape((captions, width), F32),
                shape((own, width), F32),
                shape((units // devices, width), F32),
            ],
            [],
            table,
            [pool_all, image_emb, every_pair, every_count, hidden_sum, pool_cols],
            text_w[3:4],
            us=12,
            passes_table=True,
            scalars=[logit_scale],
        )
        pair_loss = lax.dynamic_slice_in_dim(losses[:, 0], device * captions, captions)
    else:
        w_proj = run(copy_weight, [shape((width, width), BF16)], [], table, [], text_w[3:4])[0]
        pair_loss, d_mine, grad_proj, grad_down = head_tiled(
            total, captions, own, scale, pool_all, image_emb, every_pair[:, 0], every_count[:, 0], hidden_sum, w_proj
        )

    half = width // 2
    mine_in, theirs_in, d_inner, sums_in = run(
        functools.partial(back_inner, devices),
        [
            shape((half, units), BF16),
            shape((half, units), BF16),
            shape((tokens, units), BF16),
            shape((1, units), F32),
        ],
        [((half, tokens), BF16), ((half, tokens), BF16), ((3 * captions, units), BF16)],
        table,
        [d_mine, caption_col, second, slope, gains, shifts],
        text_w[4:5],
        us=15,
        passes_table=True,
    )
    d_second, d_mixed, sums_out = run(
        back_second,
        [shape((tokens, width), F32), shape((tokens, width), BF16), shape((8, width), F32)],
        [((tokens, width), F32)],
        table,
        [d_mine, d_inner, caption_col, second, gains],
        [text_w[2], text_w[1]],
    )
    if regular:
        got_in, d_mixed = tie(grid.shift(theirs_in, 3, 1), d_mixed)
        held_in, got_in, sent = grid.reduce_start(table, mine_in, got_in)
    (d_qkv,) = run(back_attention, [shape((tokens, 3 * width), BF16)], [], table, [d_mixed, qkv, probs], [])
    where = table
    mine_qkv, theirs_qkv = run(
        functools.partial(back_weights, devices),
        [shape((half, 4 * width), BF16), shape((half, 4 * width), BF16)],
        [((half, tokens), BF16)] * 4,
        where,
        [text_tokens, d_second, d_qkv, mixed, gains, shifts],
        [],
        us=5,
        passes_table=True,
    )
    where = after(table, mine_qkv)
    if regular:
        *got_in, mine_qkv, theirs_qkv = tie(*got_in, mine_qkv, theirs_qkv)
        got_qkv = grid.shift(theirs_qkv, 3, 1)
        held_in, got_in, sent = grid.reduce_next(table, held_in, got_in)
    if regular:
        held_qkv, got_qkv, sent = grid.reduce_start(table, mine_qkv, got_qkv)
        where = after(table, *sent)
    text_grad, sums_qkv = run(
        back_outer,
        [shape((tokens, width), F32), shape((8, width), F32)],
        [((tokens, width), F32)],
        where,
        [text_tokens, d_second, d_qkv, gains],
        text_w[:1],
        us=5,
    )
    (sums,) = run(
        pack_sums, [shape((devices, 384), F32)], [], table, [sums_qkv, sums_out, sums_in], [], us=2
    )
    if not regular:
        sums = lax.all_to_all(sums, "blk", 0, 0, tiled=True)
    if regular:
        text_grad, sums, *got_in = tie(text_grad, sums, *got_in)
        kept_in, got_in = grid.reduce_line(table, held_in, got_in)
        kept_in, *got_qkv = tie(kept_in, *got_qkv)
        held_qkv, got_qkv, sent = grid.reduce_next(table, held_qkv, got_qkv)
        sums = lax.all_to_all(sums, "blk", 0, 0, tiled=True)
        kept_qkv, got_qkv = grid.reduce_line(table, held_qkv, got_qkv)
        sums, *got_in = tie(sums, *got_in)
        (grad_in,) = grid.reduce_end(table, kept_in, got_in, [units])
        grad_qkv, grad_out = grid.reduce_end(table, kept_qkv, got_qkv, [3 * width, width])
    else:
        grad_in = reduce_grads(grid, mine_in, theirs_in, width)
        grad_qkv = reduce_grads(grid, mine_qkv, theirs_qkv, width)
        grad_qkv, grad_out = grad_qkv[:, : 3 * width], grad_qkv[:, 3 * width :]
    sums = jnp.sum(sums, axis=0)
    return (
        pair_loss,
        text_out,
        text_grad,
        sums[: vec[0]],
        sums[128 : 128 + vec[1]],
        grad_qkv,
        grad_out,
        grad_in,
        grad_down,
        sums[256 : 256 + vec[2]],
        grad_proj,
    )


def copy_weight(weight, out):
    out[...] = weight()[...]


def axis_sizes(mesh):
    devices = list(mesh.devices.flat)
    places = [(*d.coords, d.core_on_chip) for d in devices]
    sizes = []
    stride = len(devices)
    left = [0, 1, 2, 3]
    while stride > 1 and left:
        for axis in left:
            size = 1 + max(p[axis] for p in places) - min(p[axis] for p in places)
            step = stride // size
            if size > 1 and all(
                p[axis] - places[0][axis] == (i // step) % size for i, p in enumerate(places)
            ):
                sizes.append(size)
                left.remove(axis)
                stride = step
                break
        else:
            return [len(devices)]
    return sizes


def solution(mesh):
    grid = Grid(mesh.shape["blk"], axis_sizes(mesh))
    row = P("blk", None)
    flat = P("blk")
    tower = (flat, flat, row, row, row, row, flat, row)

    def body(*args):
        return on_device(grid, *args)

    return jax.shard_map(
        body,
        mesh=mesh,
        in_specs=(row, row, flat, row, P()) + tower + tower,
        out_specs=(flat, row, row, flat, flat, row, row, row, row, flat, row),
        check_vma=False,
    )
```

```python
import functools

import jax
import jax.numpy as jnp
from jax import lax
from jax.experimental import pallas as pl
from jax.experimental.pallas import tpu as pltpu
from jax.sharding import PartitionSpec as P

HEAD = 64
PATCHES = 50
CAPS = 4
TILE = 512
GROUP_PAD = 112

F32 = jnp.float32
BF16 = jnp.bfloat16


def gelu(z):
    return 0.5 * z * (1.0 + jnp.tanh(0.7978845608028654 * (z + 0.044715 * z * z * z)))


def normalize(x):
    mean = jnp.mean(x, axis=-1, keepdims=True)
    cent = x - mean
    rstd = lax.rsqrt(jnp.mean(cent * cent, axis=-1, keepdims=True) + 1e-06)
    return (cent * rstd, rstd)


def norm_back(grad, normed, rstd):
    return rstd * (
        grad
        - jnp.mean(grad, axis=-1, keepdims=True)
        - normed * jnp.mean(grad * normed, axis=-1, keepdims=True)
    )


def unit_rows(proj):
    factor = lax.rsqrt(jnp.sum(proj * proj, axis=-1, keepdims=True) + 1e-06)
    return (proj * factor, factor)


def matmul(left, right):
    return jnp.dot(left, right, preferred_element_type=F32)


def dot_nt(left, right):
    return lax.dot_general(left, right, (((1,), (1,)), ((), ())), preferred_element_type=F32)


def dot_tn(left, right):
    return lax.dot_general(left, right, (((0,), (0,)), ((), ())), preferred_element_type=F32)


def chunks(total, size, unroll=True):
    def wrap(body):
        @pl.loop(0, total // size, unroll=unroll)
        def step(j):
            body(pl.ds(pl.multiple_of(j * size, size), size))

    return wrap


def thirds(value):
    high = value.astype(BF16)
    rest = value - high.astype(F32)
    mid = rest.astype(BF16)
    return high, mid, (rest - mid.astype(F32)).astype(BF16)


def norm_rows(x, gain, shift):
    normed, rstd = normalize(x)
    return (normed * gain + shift).astype(BF16)


def head_masks(dtype, value):
    lane = lax.broadcasted_iota(jnp.int32, (1, 2 * HEAD), 1)
    first = jnp.where(lane < HEAD, value, 0.0).astype(dtype)
    second = jnp.where(lane < HEAD, 0.0, value).astype(dtype)
    return first, second


def both_heads(block, masks):
    return jnp.concatenate([block * masks[0], block * masks[1]], axis=0)


def merge_heads(stacked):
    half = stacked.shape[0] // 2
    lane = lax.broadcasted_iota(jnp.int32, (1, 2 * HEAD), 1)
    return jnp.where(lane < HEAD, stacked[:half], stacked[half:])


def softmax_unit(query, keys, mask, masks):
    scores = dot_nt(both_heads(query, masks), keys)
    scores = jnp.where(mask, scores, -1000000000.0)
    top = jnp.max(scores, axis=-1, keepdims=True)
    expo = jnp.exp(scores - top)
    return expo * (1.0 / jnp.sum(expo, axis=-1, keepdims=True))


def image_attention(x, gains, shifts, w_qkv, w_out, second, act, qkv, mixed):
    rows, width = x.shape
    group = GROUP_PAD

    @chunks(rows, group)
    def _(at):
        act[at, :] = norm_rows(x[at, :].astype(F32), gains[0:1, :], shifts[0:1, :])

    w_qkv = w_qkv()

    @chunks(3 * width, 256)
    def _(at):
        qkv[:, at] = matmul(act[...], w_qkv[:, at]).astype(BF16)

    masks = head_masks(BF16, 0.125)
    own = lax.broadcasted_iota(jnp.int32, (2 * group, group), 0)
    own = jnp.where(own >= group, own - group, own)
    other = lax.broadcasted_iota(jnp.int32, (2 * group, group), 1)
    mask = picture(own) == picture(other)

    @chunks(rows, group, 2)
    def _(at):
        for start in range(0, width, 2 * HEAD):
            cols = slice(start, start + 2 * HEAD)
            keys = qkv[at, width + start : width + start + 2 * HEAD]
            values = qkv[at, 2 * width + start : 2 * width + start + 2 * HEAD]
            probs = softmax_unit(qkv[at, cols], keys, mask, masks)
            mixed[at, cols] = merge_heads(matmul(probs.astype(BF16), values)).astype(BF16)

    w_out = w_out()

    @chunks(width, 256)
    def _(at):
        second[:, at] = x[:, at].astype(F32) + matmul(mixed[...], w_out[:, at])


def picture(place):
    return jnp.where(place >= PATCHES, 1, 0) + jnp.where(place >= 2 * PATCHES, 1, 0)


def image_pool(value):
    value = value.reshape(-1, GROUP_PAD, value.shape[1])
    which = picture(lax.broadcasted_iota(jnp.int32, (1, GROUP_PAD, 1), 1))
    parts = [jnp.sum(jnp.where(which == kind, value, 0.0), axis=1) for kind in range(2)]
    return jnp.concatenate(parts, axis=0) * (1.0 / PATCHES)


def image_inner(second, gains, shifts, biases, w_in, pooled, pooled_second, act):
    rows, width = second.shape
    units = pooled.shape[1]

    @chunks(rows, GROUP_PAD)
    def _(at):
        act[at, :] = norm_rows(second[at, :], gains[1:2, :], shifts[1:2, :])

    for start in range(0, width, 256):
        pooled_second[:, start : start + 256] = image_pool(second[:, start : start + 256])
    w_in = w_in()

    @chunks(units, 256)
    def _(at):
        hidden = gelu(matmul(act[...], w_in[:, at]) + biases[:, at]).astype(BF16).astype(F32)
        pooled[:, at] = image_pool(hidden)


def image_embed(pooled, pooled_second, biases, w_down, w_proj, emb):
    images, units = pooled.shape
    high, mid, unused = thirds(pooled[...])
    w_down = w_down()
    y = matmul(jnp.concatenate([high, mid], axis=0), w_down[...])
    y = y[:images] + y[images:] + pooled_second[...] + biases[:, units:]
    unit = unit_rows(matmul(y.astype(BF16), w_proj()[...]))[0].astype(BF16)
    to = lax.broadcasted_iota(jnp.int32, (images, images), 0)
    source = lax.broadcasted_iota(jnp.int32, (images, images), 1)
    half = images // 2
    order = (jnp.where(source >= half, 2 * (source - half) + 1, 2 * source) == to).astype(BF16)
    emb[...] = matmul(order, unit).astype(BF16)


def text_attention(x, caption_col, caption_row, gains, shifts, w_qkv, w_out, qkv, probs, mixed, second, act):
    rows, width = x.shape
    group = 2 * HEAD
    act[...] = norm_rows(x[...].astype(F32), gains[0:1, :], shifts[0:1, :])
    w_qkv = w_qkv()

    @chunks(3 * width, 256)
    def _(at):
        qkv[:, at] = matmul(act[...], w_qkv[:, at]).astype(BF16)

    masks = head_masks(BF16, 0.125)
    unit = 0
    for top in range(0, rows, group):
        at = slice(top, top + group)
        same = caption_col[at, :] == caption_row[:, at]
        mask = jnp.concatenate([same, same], axis=0)
        for start in range(0, width, 2 * HEAD):
            cols = slice(start, start + 2 * HEAD)
            keys = qkv[at, width + start : width + start + 2 * HEAD]
            values = qkv[at, 2 * width + start : 2 * width + start + 2 * HEAD]
            prob = softmax_unit(qkv[at, cols], keys, mask, masks)
            probs[unit] = prob
            unit += 1
            mixed[at, cols] = merge_heads(matmul(prob.astype(BF16), values)).astype(BF16)

    w_out = w_out()

    @chunks(width, 256)
    def _(at):
        second[:, at] = x[:, at].astype(F32) + matmul(mixed[...], w_out[:, at])


def caption_member(caption_row, captions):
    index = lax.broadcasted_iota(jnp.int32, (captions, caption_row.shape[1]), 0)
    return (index == caption_row[...]).astype(F32)


def text_inner(second, caption_row, gains, shifts, biases, w_in, hidden, slope, hidden_sum, act):
    units = hidden.shape[1]
    act[...] = norm_rows(second[...], gains[1:2, :], shifts[1:2, :])
    low = caption_member(caption_row, hidden_sum.shape[0]).astype(BF16)
    w_in = w_in()

    @chunks(units, 256)
    def _(at):
        z = matmul(act[...], w_in[:, at]) + biases[:, at]
        inside = jnp.tanh(0.7978845608028654 * (z + 0.044715 * z * z * z))
        value = (0.5 * z * (1.0 + inside)).astype(BF16)
        hidden[:, at] = value
        slope[:, at] = 0.5 * (1.0 + inside) + 0.5 * z * (1.0 - inside * inside) * (
            0.7978845608028654 * (1.0 + 3.0 * 0.044715 * z * z)
        )
        hidden_sum[:, at] = matmul(low, value).astype(BF16)


def text_outer(second, hidden, caption_row, biases, w_down, out, pool_low):
    width = second.shape[1]
    units = hidden.shape[1]
    member = caption_member(caption_row, pool_low.shape[0])
    low = member.astype(BF16)
    count = jnp.sum(member, axis=1, keepdims=True)
    w_down = w_down()

    @chunks(width, 256)
    def _(at):
        outer = biases[:, pl.ds(pl.multiple_of(units + at.start, 256), 256)]
        y = second[:, at] + matmul(hidden[...], w_down[:, at]) + outer
        out[:, at] = y.astype(BF16)
        total = sum(matmul(low, part) for part in thirds(y))
        pool_low[:, at] = (total / count).astype(BF16)


def head_kernel(
    table, scale_ref, pool_all, image_emb, pair_col, count, hidden_sum, pool_cols, w_proj,
    loss, d_mine, grad_proj, grad_down,
):
    scale = scale_ref[0]
    captions = d_mine.shape[0]
    w_proj = w_proj()
    proj = matmul(pool_all[...], w_proj[...])
    unit, factor = unit_rows(proj)
    sim = scale * dot_nt(unit.astype(BF16), image_emb[...])
    row_max = jnp.max(sim, axis=1, keepdims=True)
    row_lse = row_max + jnp.log(jnp.sum(jnp.exp(sim - row_max), axis=1, keepdims=True))
    col_max = jnp.max(sim, axis=0, keepdims=True)
    col_lse = col_max + jnp.log(jnp.sum(jnp.exp(sim - col_max), axis=0, keepdims=True))
    hit = pair_col[...] == lax.broadcasted_iota(jnp.int32, sim.shape, 1)
    both = 0.5 * jnp.exp(sim - row_lse) + 0.5 * jnp.exp(sim - col_lse)
    weights_sim = jnp.where(hit, both - 1.0, both).astype(BF16)
    pos = jnp.sum(jnp.where(hit, sim, 0.0), axis=1, keepdims=True)
    pair_lse = jnp.sum(jnp.where(hit, col_lse, 0.0), axis=1, keepdims=True)
    loss[...] = 0.5 * (row_lse - pos) + 0.5 * (pair_lse - pos)
    d_emb = scale * matmul(weights_sim, image_emb[...])
    inside = jnp.sum(d_emb * proj, axis=-1, keepdims=True)
    d_proj = (factor * d_emb - proj * (factor * factor * factor * inside)).astype(BF16)
    grad_proj[...] = dot_tn(pool_cols[...], d_proj)
    d_each = dot_nt(d_proj, w_proj[...]) / count[...]
    d_low = d_each.astype(BF16)
    grad_down[...] = dot_tn(hidden_sum[...], d_low)
    first = table[PLACE] * captions
    index = lax.broadcasted_iota(jnp.int32, (captions, d_each.shape[0]), 1)
    pick = (index == first + lax.broadcasted_iota(jnp.int32, (captions, d_each.shape[0]), 0)).astype(BF16)
    d_mine[...] = sum(matmul(pick, part) for part in thirds(d_each))


def text_front(
    x, caption_col, caption_row, gains, shifts, biases, w_qkv, w_out, w_in,
    qkv, probs, mixed, second, hidden, slope, hidden_sum, act,
):
    text_attention(x, caption_col, caption_row, gains, shifts, w_qkv, w_out, qkv, probs, mixed, second, act)
    text_inner(second, caption_row, gains, shifts, biases, w_in, hidden, slope, hidden_sum, act)


def image_rest(second, gains, shifts, biases, w_in, w_down, w_proj, emb, act, pooled, pooled_second):
    image_inner(second, gains, shifts, biases, w_in, pooled, pooled_second, act)
    image_embed(pooled, pooled_second, biases, w_down, w_proj, emb)


def pack_sums(sums_qkv, sums_out, sums_in, out):
    devices, width = out.shape[0], sums_out.shape[1]
    first, second = sums_qkv[...], sums_out[...]
    vectors = [
        jnp.concatenate([first[0:1], second[1:2]], axis=1),
        jnp.concatenate([first[1:2], second[2:3]], axis=1),
        jnp.concatenate([sums_in[...], second[0:1]], axis=1),
    ]
    for i, vector in enumerate(vectors):
        total = vector.shape[1]
        share = total // devices
        row = lax.broadcasted_iota(jnp.int32, (devices, total), 0)
        place = lax.broadcasted_iota(jnp.int32, (devices, total), 1) - row * share
        mine = jnp.where(place >= 0, jnp.where(place < share, vector, 0.0), 0.0)
        to = lax.broadcasted_iota(jnp.int32, (total, 128), 1)
        source = lax.broadcasted_iota(jnp.int32, (total, 128), 0)
        pick = (lax.rem(source, share) == to).astype(BF16)
        out[:, i * 128 : (i + 1) * 128] = sum(matmul(part, pick) for part in thirds(mine))


def head_back(
    devices, table, scale, pool_all, image_emb, pair_col, count, hidden_sum, pool_cols,
    caption_col, second, slope, gains, shifts, w_proj, w_down,
    loss, d_mine, grad_proj, grad_down, mine, theirs, d_inner, sums, act_t, act_u, both,
):
    head_kernel(
        table, scale, pool_all, image_emb, pair_col, count, hidden_sum, pool_cols, w_proj,
        loss, d_mine, grad_proj, grad_down,
    )
    back_inner(
        devices, table, d_mine, caption_col, second, slope, gains, shifts, w_down,
        mine, theirs, d_inner, sums, act_t, act_u, both,
    )


def core_split(table, value, devices, mine, theirs):
    own = value.shape[0] // devices
    value = value.reshape(devices // 2, 2, own, value.shape[1])
    first = table[CORE] == 0
    even = value[:, 0].reshape(-1, value.shape[3])
    odd = value[:, 1].reshape(-1, value.shape[3])
    mine[...] = jnp.where(first, even, odd).astype(BF16)
    theirs[...] = jnp.where(first, odd, even).astype(BF16)


def token_member(caption_col, captions):
    index = lax.broadcasted_iota(jnp.int32, (caption_col.shape[0], 3 * captions), 1)
    index = jnp.where(index >= captions, index - captions, index)
    index = jnp.where(index >= captions, index - captions, index)
    return (caption_col[...] == index).astype(BF16)


def back_inner(
    devices, table, each, caption_col, second, slope, gains, shifts, w_down,
    mine, theirs, d_inner, sums, act_t, act_u, both,
):
    rows, width = second.shape
    units = slope.shape[1]
    captions = each.shape[0]
    member = token_member(caption_col, captions)
    normed, rstd = normalize(second[...])
    act = normed * gains[1:2, :] + shifts[1:2, :]
    core_split(table, act.T, devices, act_t, act_u)
    each_low = each[...].astype(BF16)
    w_down = w_down()

    @chunks(units, 256)
    def _(at):
        both[:, at] = jnp.concatenate(thirds(dot_nt(each_low, w_down[at, :])), axis=0)

    @chunks(units, 256)
    def _(at):
        low = (matmul(member, both[:, at]) * slope[:, at]).astype(BF16)
        d_inner[:, at] = low
        sums[:, at] = jnp.sum(low.astype(F32), axis=0, keepdims=True)
        theirs[:, at] = matmul(act_u[...], low).astype(BF16)
        mine[:, at] = matmul(act_t[...], low).astype(BF16)


def back_second(each, d_inner, caption_col, second, gains, w_in, w_out, d_second, d_mixed, sums, d_act):
    width = second.shape[1]
    normed, rstd = normalize(second[...])
    d_y = matmul(token_member(caption_col, each.shape[0]), jnp.concatenate(thirds(each[...]), axis=0))
    sums[0:1, :] = jnp.sum(d_y, axis=0, keepdims=True)
    w_in = w_in()

    @chunks(width, 256)
    def _(at):
        d_act[:, at] = dot_nt(d_inner[...], w_in[at, :])

    grad = d_act[...]
    sums[1:2, :] = jnp.sum(grad * normed, axis=0, keepdims=True)
    sums[2:3, :] = jnp.sum(grad, axis=0, keepdims=True)
    d_two = d_y + norm_back(grad * gains[1:2, :], normed, rstd)
    d_second[...] = d_two
    d_mixed[...] = dot_nt(d_two.astype(BF16), w_out()[...]).astype(BF16)


def back_attention(d_mixed, qkv, probs, d_qkv):
    rows, width = d_mixed.shape
    group = 2 * HEAD
    ones = head_masks(BF16, 1.0)
    masks = head_masks(BF16, 0.125)
    unit = 0
    for top in range(0, rows, group):
        at = slice(top, top + group)
        for start in range(0, width, 2 * HEAD):
            cols = slice(start, start + 2 * HEAD)
            key_cols = slice(width + start, width + start + 2 * HEAD)
            value_cols = slice(2 * width + start, 2 * width + start + 2 * HEAD)
            prob = probs[unit]
            unit += 1
            d_out = both_heads(d_mixed[at, cols], ones)
            query = both_heads(qkv[at, cols], masks)
            d_qkv[at, value_cols] = dot_tn(prob.astype(BF16), d_out).astype(BF16)
            d_prob = dot_nt(d_out, qkv[at, value_cols])
            d_score = (prob * (d_prob - jnp.sum(prob * d_prob, axis=-1, keepdims=True))).astype(BF16)
            d_qkv[at, cols] = (0.125 * merge_heads(matmul(d_score, qkv[at, key_cols]))).astype(BF16)
            d_qkv[at, key_cols] = dot_tn(d_score, query).astype(BF16)


def back_weights(
    devices, table, x, d_second, d_qkv, mixed, gains, shifts,
    mine, theirs, act_t, act_u, mixed_t, mixed_u,
):
    width = x.shape[1]
    core_split(table, norm_rows(x[...].astype(F32), gains[0:1, :], shifts[0:1, :]).astype(F32).T, devices, act_t, act_u)
    core_split(table, mixed[...].astype(F32).T, devices, mixed_t, mixed_u)
    d_low = d_second[...].astype(BF16)
    for start in range(0, width, 256):
        at = slice(start, start + 256)
        to = slice(3 * width + start, 3 * width + start + 256)
        theirs[:, to] = matmul(mixed_u[...], d_low[:, at]).astype(BF16)
        mine[:, to] = matmul(mixed_t[...], d_low[:, at]).astype(BF16)

    @chunks(3 * width, 256)
    def _(at):
        theirs[:, at] = matmul(act_u[...], d_qkv[:, at]).astype(BF16)
        mine[:, at] = matmul(act_t[...], d_qkv[:, at]).astype(BF16)


def back_outer(x, d_second, d_qkv, gains, w_qkv, text_grad, sums, d_act):
    width = x.shape[1]
    normed, rstd = normalize(x[...].astype(F32))
    w_qkv = w_qkv()

    @chunks(width, 256)
    def _(at):
        d_act[:, at] = dot_nt(d_qkv[...], w_qkv[at, :])

    grad = d_act[...]
    sums[0:1, :] = jnp.sum(grad * normed, axis=0, keepdims=True)
    sums[1:2, :] = jnp.sum(grad, axis=0, keepdims=True)
    text_grad[...] = d_second[...] + norm_back(grad * gains[0:1, :], normed, rstd)


class Weight:
    def __init__(self, rows, cols):
        self.dims = (rows, cols)
        self.parts = []

    def add(self, array, lead, start, width, row=None, unit=0, below=0, col=None, beside=0):
        self.parts.append((array, lead, start, width, row, unit, below, col, beside))


def run(kernel, outs, scratch, table, operands, weights, us=5, passes_table=False, scalars=()):
    arrays = []
    for weight in weights:
        for part in weight.parts:
            if not any(part[0] is a for a in arrays):
                arrays.append(part[0])
    places = {id(a): i for i, a in enumerate(arrays)}
    n_s, n_op, n_arr, n_out, n_w = len(scalars), len(operands), len(arrays), len(outs), len(weights)

    def body(*refs):
        table_ref, refs = refs[0], refs[1:]
        ops, refs = refs[: n_s + n_op], refs[n_s + n_op :]
        arrs, refs = refs[:n_arr], refs[n_arr:]
        out, refs = refs[:n_out], refs[n_out:]
        held, refs = refs[:n_w], refs[n_w:]
        if n_w:
            sems, refs = refs[0], refs[1:]
        waits = []
        for i, weight in enumerate(weights):
            for array, lead, start, width, row, unit, below, col, beside in weight.parts:
                at = 0 if row is None else pl.multiple_of(table_ref[row] * unit + below, 16)
                to = beside
                if col is not None:
                    to = pl.multiple_of(table_ref[col] * (weight.dims[1] // 2) + beside, 128)
                pltpu.make_async_copy(
                    arrs[places[id(array)]].at[lead, :, pl.ds(start, width)],
                    held[i].at[pl.ds(at, array.shape[1]), pl.ds(to, width)],
                    sems.at[i],
                ).start()

            def wait(i=i):
                pltpu.make_async_copy(held[i], held[i], sems.at[i]).wait()
                return held[i]

            waits.append(wait)
        if passes_table:
            ops = (table_ref, *ops)
        kernel(*ops, *waits, *out, *refs)

    vmem = pl.BlockSpec(memory_space=pltpu.VMEM)
    return pl.pallas_call(
        body,
        out_shape=outs,
        in_specs=[pl.BlockSpec(memory_space=pltpu.SMEM)] * (1 + n_s) + [vmem] * n_op + [pl.BlockSpec(memory_space=pltpu.HBM)] * n_arr,
        out_specs=[vmem] * n_out,
        scratch_shapes=[pltpu.VMEM(w.dims, BF16) for w in weights]
        + ([pltpu.SemaphoreType.DMA((n_w,))] if n_w else [])
        + [pltpu.VMEM(*s) for s in scratch],
        compiler_params=pltpu.CompilerParams(vmem_limit_bytes=60 << 20),
        cost_estimate=pl.CostEstimate(flops=us * 2000000000, bytes_accessed=1000, transcendentals=0),
    )(table, *scalars, *operands, *arrays)


def shape(dims, dtype):
    return jax.ShapeDtypeStruct(dims, dtype)


class Grid:
    def __init__(self, devices, sizes):
        self.devices = devices
        self.sizes = sizes
        strides = []
        step = devices
        for size in sizes:
            step //= size
            strides.append(step)
        self.strides = strides
        self.regular = len(sizes) == 4 and sizes[1:] == [2, 2, 2]

    def place(self):
        index = lax.axis_index("blk")
        return [(index // st) % size for size, st in zip(self.sizes, self.strides)]

    def shift(self, value, axis, step):
        size, stride = self.sizes[axis], self.strides[axis]
        pairs = []
        for i in range(self.devices):
            at = (i // stride) % size
            pairs.append((i, i + ((at + step) % size - at) * stride))
        return lax.ppermute(value, "blk", pairs)

    def table(self):
        if len(self.sizes) != 4:
            index = lax.axis_index("blk")
            return jnp.stack([index % 2, 1 - index % 2, index]).astype(jnp.int32)
        place = self.place()
        chips = []
        for offset in self.offsets():
            origin = [
                d[1] if isinstance(d, tuple) else (p - d) % s for p, d, s in zip(place, offset, self.sizes)
            ]
            chips.append(sum(o * st for o, st in zip(origin, self.strides)) // 2)
        chips = jnp.stack(chips)
        core = place[3]
        return jnp.concatenate(
            [jnp.stack([core, 1 - core, lax.axis_index("blk"), *place[:3]]), chips, 2 * chips + core, 2 * chips + 1 - core]
        ).astype(jnp.int32)

    def offsets(self):
        z, y, x, unused = self.sizes
        zs = list(range(z)) + [("z", i) for i in range(z)]
        return [(dz, dy, dx) for dz in zs for dy in range(y) for dx in range(x)]

    def row_of(self, offset, kind):
        count = len(self.offsets())
        return FIRST_ROW + self.offsets().index(offset) + {"chip": 0, "own": count, "other": 2 * count}[kind]

    def line(self, value):
        return [value] + [self.shift(value, 0, k) for k in range(1, self.sizes[0])]

    def square(self, line):
        return self.shift(line, 2, 1), self.shift(line, 1, 1)

    def along_z(self, value):
        depth = self.sizes[0]
        groups = [[i + k * self.strides[0] for k in range(depth)] for i in range(self.strides[0])]
        return lax.all_to_all(
            jnp.broadcast_to(value[None], (depth, *value.shape)), "blk", 0, 0, axis_index_groups=groups
        )

    def across(self, *arrays):
        return [self.shift(a, 3, 1) for a in arrays]

    def parts(self, value):
        return value.reshape(*self.sizes[:3], -1, value.shape[1])

    def reduce_start(self, table, mine, got):
        mine, got = self.parts(mine), self.parts(got)
        depth, unused, unused, rows, cols = mine.shape
        sent = shape((depth, 2, rows, cols // 2), BF16)
        held = [((depth, 2, rows, cols // 2), BF16)] * 4
        to_x, to_y = fetching(sum_cores, [sent, sent], held, table, [mine, got])
        return (mine, got), (self.shift(to_x, 2, 1), self.shift(to_y, 1, 1)), (to_x, to_y)

    def reduce_next(self, table, held, came):
        depth, unused, unused, rows, cols = held[0].shape
        sent = shape((depth, rows, cols // 2), BF16)
        scratch = [((depth, rows, cols // 2), BF16)] * 6
        to_y, to_x = fetching(sum_sides, [sent, sent], scratch, table, [*held, *came])
        return (*held, *came), (self.shift(to_y, 1, 1), self.shift(to_x, 2, 1)), (to_y, to_x)

    def reduce_line(self, table, held, came):
        depth, unused, unused, rows, cols = held[0].shape
        sent = shape((rows, cols), BF16)
        scratch = [((depth, rows, cols // 2), BF16)] * 8
        outs = [shape((rows, cols), F32)] + [sent] * (depth - 1)
        kept, *to = fetching(sum_corner, outs, scratch, table, [*held, *came])
        return kept, [self.shift(value, 0, k) for k, value in enumerate(to, 1)]

    def reduce_end(self, table, kept, came, widths):
        kernel = functools.partial(sum_line, len(came))
        return run(kernel, [shape((kept.shape[0], w), F32) for w in widths], [], table, [kept, *came], [], us=1)


def wide(*values):
    return sum(v.astype(F32) for v in values)


def fetching(kernel, outs, scratch, table, arrays):
    count, n_out = len(arrays), len(outs)

    def body(*refs):
        table_ref, refs = refs[0], refs[1:]
        arrs, out, held, sems = refs[:count], refs[count : count + n_out], refs[count + n_out : -1], refs[-1]
        steps = kernel(table_ref, *arrs, *out)
        copies = [pltpu.make_async_copy(s, h, sems.at[i]) for i, (s, h) in enumerate(zip(next(steps), held))]
        for copy in copies:
            copy.start()
        for copy in copies:
            copy.wait()
        steps.send(held)

    vmem = pl.BlockSpec(memory_space=pltpu.VMEM)
    return pl.pallas_call(
        body,
        out_shape=outs,
        in_specs=[pl.BlockSpec(memory_space=pltpu.SMEM)] + [pl.BlockSpec(memory_space=pltpu.HBM)] * count,
        out_specs=[vmem] * n_out,
        scratch_shapes=[pltpu.VMEM(*s) for s in scratch] + [pltpu.SemaphoreType.DMA((len(scratch),))],
        compiler_params=pltpu.CompilerParams(vmem_limit_bytes=24 << 20),
        cost_estimate=pl.CostEstimate(flops=1000, bytes_accessed=1000, transcendentals=0),
    )(table, *arrays)


def sum_cores(table, mine, got, to_x, to_y):
    half = to_x.shape[3]
    other_y, other_x = 1 - table[AT_Y], 1 - table[AT_X]
    left, right = pl.ds(0, half), pl.ds(half, half)
    held = yield [
        mine.at[:, :, other_x, :, left],
        got.at[:, :, other_x, :, left],
        mine.at[:, other_y, :, :, right],
        got.at[:, other_y, :, :, right],
    ]
    for z in range(mine.shape[0]):
        for i in range(2):
            to_x[z, i] = wide(held[0][z, i], held[1][z, i]).astype(BF16)
            to_y[z, i] = wide(held[2][z, i], held[3][z, i]).astype(BF16)
    yield


def sum_sides(table, mine, got, by_x, by_y, to_y, to_x):
    half = to_x.shape[2]
    y, x = table[AT_Y], table[AT_X]
    left, right = pl.ds(0, half), pl.ds(half, half)
    held = yield [
        mine.at[:, 1 - y, x, :, left],
        got.at[:, 1 - y, x, :, left],
        by_x.at[:, 1 - y],
        mine.at[:, y, 1 - x, :, right],
        got.at[:, y, 1 - x, :, right],
        by_y.at[:, 1 - x],
    ]
    for z in range(mine.shape[0]):
        to_y[z] = wide(*[h[z] for h in held[:3]]).astype(BF16)
        to_x[z] = wide(*[h[z] for h in held[3:]]).astype(BF16)
    yield


def sum_corner(table, mine, got, by_x, by_y, left_by_y, right_by_x, kept, *to):
    depth = mine.shape[0]
    half = by_x.shape[3]
    y, x = table[AT_Y], table[AT_X]
    left, right = pl.ds(0, half), pl.ds(half, half)
    held = yield [
        mine.at[:, y, x, :, left],
        got.at[:, y, x, :, left],
        by_x.at[:, y],
        left_by_y,
        mine.at[:, y, x, :, right],
        got.at[:, y, x, :, right],
        by_y.at[:, x],
        right_by_x,
    ]
    for k in range(depth):
        z = lax.rem(table[AT_Z] + k, depth)
        out = to[k - 1] if k else kept
        out[:, :half] = wide(*[h[z] for h in held[:4]]).astype(out.dtype)
        out[:, half:] = wide(*[h[z] for h in held[4:]]).astype(out.dtype)
    yield


def sum_line(spans, kept, *refs):
    came = refs[:spans]
    start = 0
    for out in refs[spans:]:
        cols = slice(start, start + out.shape[1])
        start += out.shape[1]
        out[...] = kept[:, cols] + wide(*[c[:, cols] for c in came])


class Chunk:
    def __init__(self, grid, line, cut, ordered):
        self.grid, self.line, self.cut = grid, line, cut
        self.cols = line.shape[2]
        self.zs = [("z", z) if ordered else z for z in range(grid.sizes[0])]
        self.own, self.other = [], []

    def hold(self, mine, theirs, dy, dx, start, low, high):
        offsets = [(z, dy, dx) for z in self.zs]
        for pieces, array in ((self.own, mine), (self.other, theirs)):
            pieces.append((array, offsets, start, low, high))

    def halves(self, rows, cols, start):
        weight = Weight(rows, cols)
        for pieces, col in ((self.own, CORE), (self.other, OTHER)):
            for array, offsets, begin, low, high in pieces:
                left, right = max(low, start), min(high, start + cols // 2)
                if left < right:
                    for lead, offset in enumerate(offsets):
                        row = self.grid.row_of(offset, "chip")
                        at = begin + left - low
                        weight.add(array, lead, at, right - left, row, array.shape[1], 0, col, left - start)
        return weight

    def deep(self, rows, cols):
        weight = Weight(rows, cols)
        parts = self.cols // cols
        for pieces, kind in ((self.own, "own"), (self.other, "other")):
            for array, offsets, begin, low, high in pieces:
                for part in range(parts):
                    left, right = max(low, part * cols), min(high, part * cols + cols)
                    if left < right:
                        for lead, offset in enumerate(offsets):
                            row = self.grid.row_of(offset, kind)
                            high_rows = array.shape[1]
                            at = begin + left - low
                            weight.add(
                                array, lead, at, right - left, row, parts * high_rows, part * high_rows,
                                None, left - part * cols,
                            )
        return weight


def tie(*values):
    return lax.optimization_barrier(values)


def after_all(values, *earlier):
    return lax.optimization_barrier((*values, *earlier))[: len(values)]


def after(value, *earlier):
    return lax.optimization_barrier((value, *earlier))[0]


CORE = 0
OTHER = 1
PLACE = 2
AT_Z, AT_Y, AT_X = 3, 4, 5
FIRST_ROW = 6


def to_all(value, devices):
    return lax.all_to_all(jnp.broadcast_to(value[None], (devices, *value.shape)), "blk", 0, 0)


def pack_kernel(table, *refs):
    first = table[CORE] == 0
    keep, send = refs[-2:]
    start = 0
    for weight in refs[:-2]:
        half = weight.shape[1] // 2
        left, right = weight[:, :half], weight[:, half:]
        keep[:, start : start + half] = jnp.where(first, left, right)
        send[:, start : start + half] = jnp.where(first, right, left)
        start += half


def vector_pack_kernel(caption_row, pair_index, *refs):
    block, refs = refs[-1], refs[:-1]
    captions = pair_index.shape[1]
    pairs = pair_index[...].astype(F32)
    high = jnp.floor(pairs * (1.0 / 64.0))
    member = caption_member(caption_row, captions).astype(BF16)
    count = dot_nt(jnp.ones((8, caption_row.shape[1]), BF16), member)[0:1]
    rows = [r[...].astype(F32) for r in refs] + [high, pairs - 64.0 * high, count]
    rows = [jnp.concatenate([r, jnp.zeros((1, 128 - r.shape[1]), F32)], axis=1) for r in rows]
    rows.append(jnp.zeros((block.shape[0] - len(rows), 128), F32))
    block[...] = jnp.concatenate(rows, axis=0).astype(BF16)


def pair_kernel(table, keep, got, *outs):
    first = table[CORE] == 0
    start = 0
    for out in outs:
        cols = slice(start, start + out.shape[1])
        start += out.shape[1]
        one, two = keep[:, cols].astype(F32), got[:, cols].astype(F32)
        out[...] = jnp.concatenate([jnp.where(first, one, two), jnp.where(first, two, one)], axis=0).astype(BF16)


def pair_up(grid, table, groups):
    rows = groups[0][0].shape[0]
    widths = [sum(w.shape[1] for w in group) // 2 for group in groups]
    packed = shape((rows, sum(widths)), BF16)
    keep, send = run(
        pack_kernel, [packed, packed], [], table, [w for group in groups for w in group], [], us=1, passes_table=True
    )
    return run(
        pair_kernel,
        [shape((2 * rows, w), BF16) for w in widths],
        [],
        table,
        [keep, grid.shift(send, 3, 1)],
        [],
        us=1,
        passes_table=True,
    )


def copied(arrays, outs, moves):
    count = len(arrays)

    def kernel(*refs):
        sems = refs[-1]
        copies = [
            pltpu.make_async_copy(refs[a].at[source], refs[count + o].at[to], sems.at[i])
            for i, (a, source, o, to) in enumerate(moves)
        ]
        for copy in copies:
            copy.start()
        for copy in copies:
            copy.wait()

    anywhere = pl.BlockSpec(memory_space=pltpu.HBM)
    return pl.pallas_call(
        kernel,
        out_shape=outs,
        in_specs=[anywhere] * count,
        out_specs=[pl.BlockSpec(memory_space=pltpu.VMEM)] * len(outs),
        scratch_shapes=[pltpu.SemaphoreType.DMA((len(moves),))],
        cost_estimate=pl.CostEstimate(flops=1000, bytes_accessed=1000, transcendentals=0),
    )(*arrays)


def columns(start, stop):
    return (slice(None), slice(None), pl.ds(start, stop - start))


def side_operands(last, parts):
    chunk, by_x, by_y = last
    cut, end = chunk.cut, chunk.cols
    if parts is None:
        depth, rows = by_x.shape[:2]
        outs = [shape((depth, rows, end - cut), BF16), shape((depth, rows, cut), BF16)]
        moves = [(0, columns(cut, end), 0, columns(0, end - cut)), (1, columns(0, cut), 1, columns(0, cut))]
        return copied([by_y, by_x], outs, moves)
    line = None
    if len(parts) == 1:
        line = parts[0]
        depth, rows, cols = line.shape
        parts = [(0, columns(0, cols), columns(0, cols))]
        arrays = [line]
        outs = []
    else:
        arrays = list(parts)
        depth, (rows, cols) = len(parts), parts[0].shape
        outs = [shape((depth, rows, cols), BF16)]
        parts = [(i, (slice(None), slice(None)), (i, slice(None), pl.ds(0, cols))) for i in range(depth)]
    outs += [shape((depth, rows, cols + end - cut), BF16), shape((depth, rows, cols + cut), BF16)]
    count = len(arrays)
    moves = []
    for o in range(len(outs)):
        moves += [(a, source, o, to) for a, source, to in parts]
    moves.append((count, columns(cut, end), len(outs) - 2, columns(cols, cols + end - cut)))
    moves.append((count + 1, columns(0, cut), len(outs) - 1, columns(cols, cols + cut)))
    out = copied([*arrays, by_y, by_x], outs, moves)
    return out if line is None else [line, *out]


def beside(value):
    half = value.shape[0] // 2
    return jnp.concatenate([value[:half], value[half:]], axis=1)


def settle(chunk, last, mine, theirs):
    by_x, by_y = mine
    start = 0
    if chunk is not None:
        start = chunk.cols
        chunk.hold(by_x, theirs[0], 0, 1, 0, 0, chunk.cols)
        chunk.hold(by_y, theirs[1], 1, 0, 0, 0, chunk.cols)
    if last is not None:
        last.hold(by_x, theirs[0], 1, 1, start, last.cut, last.cols)
        last.hold(by_y, theirs[1], 1, 1, start, 0, last.cut)


def columns_of(whole, widths):
    weights = []
    start = 0
    array = whole[None]
    for width in widths:
        weight = Weight(whole.shape[0], width)
        weight.add(array, 0, start, width)
        weights.append(weight)
        start += width
    return weights


def gathered(part):
    full = lax.all_gather(part, "blk", axis=0, tiled=True)
    weight = Weight(*full.shape)
    weight.add(full[None], 0, 0, full.shape[1])
    return weight


def reduce_grads(grid, mine, theirs, width):
    own = width // grid.devices
    both = jnp.where(lax.axis_index("blk") % 2 == 0, jnp.stack([mine, theirs], 0), jnp.stack([theirs, mine], 0))
    both = both.reshape(2, grid.devices // 2, own, -1).transpose(1, 0, 2, 3).reshape(width, -1)
    return lax.psum_scatter(both, "blk", scatter_dimension=0, tiled=True).astype(F32)


def head_tile(proj, factor, image_emb, scale, row_lse, col_lse, pairs, sim):
    hit = pairs[:, None] == jnp.arange(image_emb.shape[0], dtype=jnp.int32)[None, :]
    weights_sim = (
        0.5 * jnp.exp(sim - row_lse[:, None]) + 0.5 * jnp.exp(sim - col_lse[None, :]) - hit.astype(F32)
    )
    d_emb = scale * matmul(weights_sim.astype(BF16), image_emb)
    d_proj = factor * d_emb - proj * (factor * factor * factor) * jnp.sum(d_emb * proj, axis=-1, keepdims=True)
    pos = jnp.sum(jnp.where(hit, sim, 0.0), axis=1)
    pair_col = jnp.sum(jnp.where(hit, col_lse[None, :], 0.0), axis=1)
    return (d_proj.astype(BF16), 0.5 * (row_lse - pos) + 0.5 * (pair_col - pos))


def head_tiled(total, captions, own, scale, pool_all, image_emb, every_pair, every_count, hidden_sum, w_proj):
    device = lax.axis_index("blk")
    col_max = jnp.full((total,), -1e30, F32)
    col_sum = jnp.zeros((total,), F32)
    held = []
    for start in range(0, total, TILE):
        proj = matmul(pool_all[start : start + TILE], w_proj)
        unit, factor = unit_rows(proj)
        sim = scale * dot_nt(unit.astype(BF16), image_emb)
        top = jnp.max(sim, axis=1)
        row_lse = top + jnp.log(jnp.sum(jnp.exp(sim - top[:, None]), axis=1))
        new_max = jnp.maximum(col_max, jnp.max(sim, axis=0))
        col_sum = col_sum * jnp.exp(col_max - new_max) + jnp.sum(jnp.exp(sim - new_max[None, :]), axis=0)
        col_max = new_max
        held.append((proj, factor, row_lse, sim))
    col_lse = col_max + jnp.log(col_sum)
    d_proj = []
    losses = []
    for start, (proj, factor, row_lse, sim) in zip(range(0, total, TILE), held):
        grad, loss = head_tile(
            proj, factor, image_emb, scale, row_lse, col_lse, every_pair[start : start + TILE], sim
        )
        d_proj.append(grad)
        losses.append(loss)
    d_proj = jnp.concatenate(d_proj)
    pair_loss = lax.dynamic_slice_in_dim(jnp.concatenate(losses), device * captions, captions)
    grad_proj = dot_tn(lax.dynamic_slice_in_dim(pool_all, device * own, own, axis=1), d_proj)
    d_each = dot_nt(d_proj, w_proj) / every_count[:, None]
    grad_down = dot_tn(hidden_sum, d_each.astype(BF16))
    d_mine = lax.dynamic_slice_in_dim(d_each, device * captions, captions)

    return pair_loss, d_mine, grad_proj, grad_down


def unpack_vectors(block, sizes, width):
    block = block.astype(F32)
    parts = [block[:, i, :size].reshape(-1) for i, size in enumerate(sizes)]
    pairs = parts[6].astype(jnp.int32) * 64 + parts[7].astype(jnp.int32)
    shapes = ((2, width), (2, width), (1, -1), (2, width), (2, width), (1, -1))
    vectors = [part.reshape(dims) for part, dims in zip(parts, shapes)]
    return [*vectors, pairs[:, None], parts[8][:, None]]


def on_device(grid, *args):
    (
        text_tokens,
        segment_ids,
        pair_index,
        image_tokens,
        logit_scale,
        img_gains,
        img_shifts,
        img_qkv,
        img_out,
        img_in,
        img_down,
        img_biases,
        img_proj,
        txt_gains,
        txt_shifts,
        txt_qkv,
        txt_out,
        txt_in,
        txt_down,
        txt_biases,
        txt_proj,
    ) = args
    devices = grid.devices
    width = text_tokens.shape[1]
    units = img_in.shape[1]
    scale = logit_scale[0]
    rows, length = segment_ids.shape
    tokens = rows * length
    captions = pair_index.shape[0]
    images = image_tokens.shape[0] // PATCHES
    device = lax.axis_index("blk")
    own = width // devices
    table = grid.table()

    caption_of = (jnp.arange(rows, dtype=jnp.int32)[:, None] * CAPS + segment_ids).reshape(tokens)
    caption_col, caption_row = caption_of[:, None], caption_of[None, :]
    member = (jnp.arange(captions, dtype=jnp.int32)[:, None] == caption_row).astype(F32)

    vec = (img_gains.shape[0], img_shifts.shape[0], img_biases.shape[0])
    vectors = [img_gains, img_shifts, img_biases, txt_gains, txt_shifts, txt_biases]
    (block,) = run(
        vector_pack_kernel,
        [shape((16, 128), BF16)],
        [],
        table,
        [caption_row, pair_index[None], *[v[None] for v in vectors]],
        [],
        us=1,
    )
    block = to_all(block, devices)
    pairs = images // 2
    padded = pairs * GROUP_PAD
    x_image = jnp.pad(
        image_tokens.reshape(pairs, 2 * PATCHES, width), ((0, 0), (0, GROUP_PAD - 2 * PATCHES), (0, 0))
    ).reshape(padded, width)
    regular = grid.regular and own % 8 == 0
    text_parts = [txt_qkv, txt_out, txt_in, txt_proj]
    if regular:
        line0 = grid.line(beside(img_down))
        pair1, pair2 = pair_up(grid, table, [[img_qkv, img_out], [img_in, img_proj]])
        *line0, pair1, pair2 = tie(*line0, pair1, pair2)

        chunk0 = Chunk(grid, jnp.stack(line0), width, False)
        side0 = grid.square(chunk0.line)
        line1 = grid.line(pair1)
        *side0, line1[1], line1[2], line1[3], block = tie(*side0, *line1[1:], block)
        text_all = lax.all_gather(
            after(jnp.concatenate(text_parts, axis=1), line1[1]), "blk", axis=0, tiled=True
        )
        text_w = columns_of(text_all, [w.shape[1] for w in text_parts])

        line1, *to = side_operands((chunk0, *side0), line1)
        chunk1 = Chunk(grid, line1, width, False)
        side1 = grid.shift(to[0], 2, 1), grid.shift(to[1], 1, 1)
        line2 = grid.line(pair2)
        vectors = unpack_vectors(block, vec + vec + (captions,) * 3, width)
        *side1, line2[1], line2[2], line2[3], x_image = tie(*side1, *line2[1:], x_image)

        line2, *to = side_operands((chunk1, *side1), line2)
        chunk2 = Chunk(grid, line2, 1024, False)
        side2 = grid.shift(to[0], 2, 1), grid.shift(to[1], 1, 1)
        other1 = grid.across(chunk1.line, *side1)
        line3 = grid.line(beside(txt_down))
        tied = tie(*side2, *line3[1:], *other1, *vectors)
        side2, line3, other1, vectors = tied[:2], [line3[0], *tied[2:5]], tied[5:8], tied[8:]

        to = side_operands((chunk2, *side2), None)
        side3 = grid.shift(to[0], 2, 1), grid.shift(to[1], 1, 1)
        other2 = grid.across(*after_all(side2, *to), chunk2.line)
        chunk3 = Chunk(grid, jnp.stack(line3), width, False)
        chunk1.hold(chunk1.line, other1[0], 0, 0, 0, 0, chunk1.cols)
        settle(chunk1, chunk0, side1, other1[1:])
        settle(chunk2, chunk1, side2, other2[:2])
        chunk2.hold(chunk2.line, other2[2], 0, 0, 0, 0, chunk2.cols)
        image_w = [chunk1.halves(width, 3 * width, 0), chunk1.halves(width, width, 3 * width // 2)]
        where = after(table, *to)
    else:
        image_w = [gathered(w) for w in (img_qkv, img_out, img_in, img_proj, img_down)]
        text_w = [gathered(w) for w in (*text_parts, txt_down)]
        vectors = unpack_vectors(block, vec + vec + (captions,) * 3, width)
        where = table
    img_g, img_s, img_b, gains, shifts, biases, every_pair, every_count = vectors
    image_second = run(
        image_attention,
        [shape((padded, width), F32)],
        [((padded, width), BF16), ((padded, 3 * width), BF16), ((padded, width), BF16)],
        where,
        [x_image, img_g, img_s],
        image_w[:2],
        us=19,
    )[0]
    where = table
    if regular:
        *side3, image_second = tie(*side3, image_second)
        side4 = grid.square(after(chunk3.line, image_second))
        settle(None, chunk2, side3, grid.across(*after_all(side3, chunk3.line)))
        other0 = grid.across(*after_all((chunk0.line, *side0), image_second))
        chunk0.hold(chunk0.line, other0[0], 0, 0, 0, 0, chunk0.cols)
        settle(chunk0, None, side0, other0[1:])
        image_w += [
            chunk2.halves(width, units, 0),
            chunk2.halves(width, width, units // 2),
            chunk0.deep(units, width),
        ]
        where = after(table, chunk3.line)
    (image_emb,) = run(
        image_rest,
        [shape((images, width), BF16)],
        [((padded, width), BF16), ((images, units), F32), ((images, width), F32)],
        where,
        [image_second, img_g, img_s, img_b],
        [image_w[2], image_w[4], image_w[3]],
        us=18,
    )
    if regular:
        *side4, image_emb = tie(*side4, image_emb)
        to = side_operands((chunk3, *side4), None)
        side5 = grid.shift(to[0], 2, 1), grid.shift(to[1], 1, 1)
        other4 = grid.across(*after_all(side4, *to), chunk3.line)
        settle(chunk3, None, side4, other4[:2])
        chunk3.hold(chunk3.line, other4[2], 0, 0, 0, 0, chunk3.cols)
    image_all = to_all(image_emb, devices)
    where = after(table, *to) if regular else after(table, image_emb)

    heads = tokens // (2 * HEAD) * (width // (2 * HEAD))
    qkv, probs, mixed, second, hidden, slope, hidden_sum = run(
        text_front,
        [
            shape((tokens, 3 * width), BF16),
            shape((heads, 4 * HEAD, 2 * HEAD), F32),
            shape((tokens, width), BF16),
            shape((tokens, width), F32),
            shape((tokens, units), BF16),
            shape((tokens, units), F32),
            shape((captions, units), BF16),
        ],
        [((tokens, width), BF16)],
        where,
        [text_tokens, caption_col, caption_row, gains, shifts, biases],
        text_w[:3],
        us=17,
    )
    if regular:
        *side5, second = tie(*side5, second)
        settle(None, chunk3, side5, grid.across(*side5))
        text_w.append(chunk3.deep(units, width))
    text_out, pool_low = run(
        text_outer,
        [shape((tokens, width), BF16), shape((captions, width), BF16)],
        [],
        table,
        [second, hidden, caption_row, biases],
        text_w[4:5],
        us=5,
    )
    half = width // 2
    pool_low, image_emb = tie(pool_low, image_all)
    image_emb = image_emb.reshape(-1, width)
    wide_part = units // devices
    sent = jnp.concatenate(
        [
            jnp.broadcast_to(pool_low[None], (devices, captions, width)),
            hidden_sum.reshape(captions, devices, wide_part).transpose(1, 0, 2),
        ],
        axis=2,
    )
    sent = lax.all_to_all(sent, "blk", 0, 0).reshape(-1, width + wide_part)
    pool_all, hidden_sum = sent[:, :width], sent[:, width:]
    total = pool_all.shape[0]
    if total <= TILE:
        pool_cols = lax.dynamic_slice_in_dim(pool_all, device * own, own, axis=1)
        losses, d_mine, grad_proj, grad_down, mine_in, theirs_in, d_inner, sums_in = run(
            functools.partial(head_back, devices),
            [
                shape((total, 1), F32),
                shape((captions, width), F32),
                shape((own, width), F32),
                shape((units // devices, width), F32),
                shape((half, units), BF16),
                shape((half, units), BF16),
                shape((tokens, units), BF16),
                shape((1, units), F32),
            ],
            [((half, tokens), BF16), ((half, tokens), BF16), ((3 * captions, units), BF16)],
            table,
            [
                pool_all, image_emb, every_pair, every_count, hidden_sum, pool_cols,
                caption_col, second, slope, gains, shifts,
            ],
            [text_w[3], text_w[4]],
            us=25,
            passes_table=True,
            scalars=[logit_scale],
        )
        pair_loss = lax.dynamic_slice_in_dim(losses[:, 0], device * captions, captions)
    else:
        w_proj = run(copy_weight, [shape((width, width), BF16)], [], table, [], text_w[3:4])[0]
        pair_loss, d_mine, grad_proj, grad_down = head_tiled(
            total, captions, own, scale, pool_all, image_emb, every_pair[:, 0], every_count[:, 0], hidden_sum, w_proj
        )
        mine_in, theirs_in, d_inner, sums_in = run(
            functools.partial(back_inner, devices),
            [
                shape((half, units), BF16),
                shape((half, units), BF16),
                shape((tokens, units), BF16),
                shape((1, units), F32),
            ],
            [((half, tokens), BF16), ((half, tokens), BF16), ((3 * captions, units), BF16)],
            table,
            [d_mine, caption_col, second, slope, gains, shifts],
            text_w[4:5],
            us=15,
            passes_table=True,
        )

    d_second, d_mixed, sums_out = run(
        back_second,
        [shape((tokens, width), F32), shape((tokens, width), BF16), shape((8, width), F32)],
        [((tokens, width), F32)],
        table,
        [d_mine, d_inner, caption_col, second, gains],
        [text_w[2], text_w[1]],
    )
    if regular:
        got_in, d_mixed = tie(grid.shift(theirs_in, 3, 1), d_mixed)
        held_in, got_in, sent = grid.reduce_start(table, mine_in, got_in)
    (d_qkv,) = run(back_attention, [shape((tokens, 3 * width), BF16)], [], table, [d_mixed, qkv, probs], [])
    where = table
    mine_qkv, theirs_qkv = run(
        functools.partial(back_weights, devices),
        [shape((half, 4 * width), BF16), shape((half, 4 * width), BF16)],
        [((half, tokens), BF16)] * 4,
        where,
        [text_tokens, d_second, d_qkv, mixed, gains, shifts],
        [],
        us=5,
        passes_table=True,
    )
    where = after(table, mine_qkv)
    if regular:
        *got_in, mine_qkv, theirs_qkv = tie(*got_in, mine_qkv, theirs_qkv)
        got_qkv = grid.shift(theirs_qkv, 3, 1)
        held_in, got_in, sent = grid.reduce_next(table, held_in, got_in)
    if regular:
        held_qkv, got_qkv, sent = grid.reduce_start(table, mine_qkv, got_qkv)
        where = after(table, *sent)
    text_grad, sums_qkv = run(
        back_outer,
        [shape((tokens, width), F32), shape((8, width), F32)],
        [((tokens, width), F32)],
        where,
        [text_tokens, d_second, d_qkv, gains],
        text_w[:1],
        us=5,
    )
    (sums,) = run(
        pack_sums, [shape((devices, 384), F32)], [], table, [sums_qkv, sums_out, sums_in], [], us=2
    )
    if not regular:
        sums = lax.all_to_all(sums, "blk", 0, 0, tiled=True)
    if regular:
        text_grad, sums, *got_in = tie(text_grad, sums, *got_in)
        kept_in, got_in = grid.reduce_line(table, held_in, got_in)
        kept_in, *got_qkv = tie(kept_in, *got_qkv)
        held_qkv, got_qkv, sent = grid.reduce_next(table, held_qkv, got_qkv)
        sums = lax.all_to_all(sums, "blk", 0, 0, tiled=True)
        kept_qkv, got_qkv = grid.reduce_line(table, held_qkv, got_qkv)
        sums, *got_in = tie(sums, *got_in)
        (grad_in,) = grid.reduce_end(table, kept_in, got_in, [units])
        grad_qkv, grad_out = grid.reduce_end(table, kept_qkv, got_qkv, [3 * width, width])
    else:
        grad_in = reduce_grads(grid, mine_in, theirs_in, width)
        grad_qkv = reduce_grads(grid, mine_qkv, theirs_qkv, width)
        grad_qkv, grad_out = grad_qkv[:, : 3 * width], grad_qkv[:, 3 * width :]
    sums = jnp.sum(sums, axis=0)
    return (
        pair_loss,
        text_out,
        text_grad,
        sums[: vec[0]],
        sums[128 : 128 + vec[1]],
        grad_qkv,
        grad_out,
        grad_in,
        grad_down,
        sums[256 : 256 + vec[2]],
        grad_proj,
    )


def copy_weight(weight, out):
    out[...] = weight()[...]


def axis_sizes(mesh):
    devices = list(mesh.devices.flat)
    places = [(*d.coords, d.core_on_chip) for d in devices]
    sizes = []
    stride = len(devices)
    left = [0, 1, 2, 3]
    while stride > 1 and left:
        for axis in left:
            size = 1 + max(p[axis] for p in places) - min(p[axis] for p in places)
            step = stride // size
            if size > 1 and all(
                p[axis] - places[0][axis] == (i // step) % size for i, p in enumerate(places)
            ):
                sizes.append(size)
                left.remove(axis)
                stride = step
                break
        else:
            return [len(devices)]
    return sizes


def solution(mesh):
    grid = Grid(mesh.shape["blk"], axis_sizes(mesh))
    row = P("blk", None)
    flat = P("blk")
    tower = (flat, flat, row, row, row, row, flat, row)

    def body(*args):
        return on_device(grid, *args)

    return jax.shard_map(
        body,
        mesh=mesh,
        in_specs=(row, row, flat, row, P()) + tower + tower,
        out_specs=(flat, row, row, flat, flat, row, row, row, row, flat, row),
        check_vma=False,
    )
```
